32 devices in a mesh: band: 1, chan: 16 (over z, y, core), stn: 2 (over x).
Axes of the slice: x: 2, y: 2, z: 4, core: 2. Of those that a mesh axis runs over, the one named last changes fastest.
Arguments:
- observed: bfloat16 [8, 16, 2, 8, 256, 256], P('stn', ('band', 'chan')), may hold values from -18 to 18
- pair_table: int32 [8], P('stn'), may hold values from 0 to 3, as said below
- flag_rows: int32 [8], P('stn'), may hold values from 0 to 64
- gains: float32 [8, 8, 16, 512], P(None, None, ('band', 'chan'), 'stn'), may hold values from -3 to 3
- duals: float32 [8, 8, 16, 512], P(None, None, ('band', 'chan'), 'stn'), may hold values from -1.2 to 1.2
- prior_coeffs: float32 [8, 8, 4, 512], P('band', None, None, 'stn'), may hold values from -3 to 3
- delays: float32 [2, 8, 512], P(None, None, 'stn'), may hold values from -8 to 8
- brightness: float32 [8, 8], P('band'), may hold values from -2 to 2
Outputs:
- gains_out: float32 [8, 8, 16, 512], P(None, None, ('band', 'chan'), 'stn')
- coeffs_out: float32 [8, 8, 4, 512], P('band', None, None, 'stn')
- duals_out: float32 [8, 8, 16, 512], P(None, None, ('band', 'chan'), 'stn')
The draws below stay inside these ranges and needn't reach their ends.
Inputs may be any that keep to these rules, and one draw needn't show every extreme that they name: `pair_table`: each pair id 0 .. 2 stands in exactly one slot; every other slot holds 3.
All inputs are finite; a program needn't handle non-finite values.
Results may differ from the reference program's by a relative error of at most 0.0003.
Values sent between devices are 32-bit elements; how exact they have to be, the bound alone decides.
No kernel may reach another device: no remote copies, remote signals or barrier semaphores. Data moves between devices by JAX's collectives and lax.ppermute only.
A program may use at most 128 MiB of HBM per device.

```python
import math
import jax
import jax.numpy as jnp
import numpy as np
from jax import lax

STATIONS = 512
DIRS = 8
DUMPS = 2
ITERS = 3
BLOCK = 256
NPAIRS = 3
SLOTS_ALL = 8
CHANNELS = 16
N_STN = 2


def draw_observed(key, part):
    key = jax.random.fold_in(key, 5)
    first_key = jax.random.fold_in(key, 0)
    shape_all = (SLOTS_ALL, CHANNELS, DUMPS, 8, BLOCK, BLOCK)
    ramp = jnp.sqrt(1.0 + 2.0 * jnp.arange(CHANNELS, dtype=jnp.float32) / max(CHANNELS - 1, 1)).reshape(1, CHANNELS, 1, 1, 1, 1)
    base = jnp.clip(jax.random.normal(first_key, shape_all, jnp.float32), -5.0, 5.0)
    return (2.0 * base * ramp).astype(jnp.bfloat16)


def draw_pair_table(key, part):
    key = jax.random.fold_in(key, 11)
    order_perm = jax.random.permutation(key, SLOTS_ALL)
    values = jnp.minimum(jnp.arange(SLOTS_ALL, dtype=jnp.int32), NPAIRS)
    return jnp.zeros((SLOTS_ALL,), jnp.int32).at[order_perm].set(values)


def draw_flag_rows(key, part):
    key = jax.random.fold_in(key, 23)
    first_key, second_key = jax.random.split(key)
    counts = jax.random.randint(first_key, (SLOTS_ALL,), 0, BLOCK // 4 + 1)
    where_top = jax.random.randint(second_key, (), 0, SLOTS_ALL)
    counts = counts.at[where_top].set(BLOCK // 4)
    return counts.at[(where_top + 1) % SLOTS_ALL].set(0).astype(jnp.int32)


def block_scale(key, extent, cuts, least, largest):
    factor_of, own = 1.0, jax.random.fold_in(key, 6)
    for dim, shards_of in cuts:
        heights = jnp.exp(jax.random.uniform(jax.random.fold_in(own, dim), (shards_of,), jnp.float32, least / len(cuts), largest / len(cuts)))
        factor_of = factor_of * jnp.repeat(heights, extent[dim] // shards_of).reshape([-1 if axis == dim else 1 for axis in range(len(extent))])
    return factor_of


def centred(key, extent, scale, most, pieces=(), held_as=jnp.bfloat16):
    values = scale * jax.random.normal(key, extent, jnp.float32)
    if pieces:
        values = values * block_scale(key, extent, pieces, -0.22, 0.18)
    return jnp.clip(values, -most, most).astype(held_as)


def setup_inputs(seed: int = 0, part: int = 0) -> dict:
    splits = jax.random.split(jax.random.key(seed), 9)
    part_keys = jax.random.split(jax.random.fold_in(splits[8], part), 9)
    return {
        "observed": draw_observed(jax.random.fold_in(jax.random.fold_in(splits[8], part), 71), part),
        "pair_table": draw_pair_table(jax.random.fold_in(splits[8], 71), part),
        "flag_rows": draw_flag_rows(jax.random.fold_in(splits[8], 71), part),
        "gains": centred(part_keys[3], (8, DIRS, CHANNELS, STATIONS), 0.5, 3.0, ((2, 16), (3, 2)), jnp.float32),
        "duals": centred(part_keys[4], (8, DIRS, CHANNELS, STATIONS), 0.2, 1.2, ((2, 16), (3, 2)), jnp.float32),
        "prior_coeffs": centred(part_keys[5], (8, DIRS, 4, STATIONS), 0.5, 3.0, ((3, 2),), jnp.float32),
        "delays": jnp.clip(jax.random.uniform(splits[6], (DUMPS, DIRS, STATIONS), jnp.float32, -8.0, 8.0) * block_scale(splits[6], (DUMPS, DIRS, STATIONS), ((2, 2),), -0.4, 0.0), -8.0, 8.0),
        "brightness": centred(part_keys[7], (8, DIRS), 0.35, 2.0, (), jnp.float32),
    }


PRECISE = lax.Precision.HIGHEST
EPSILON = 1e-06
SPECTRAL_INDEX = 0.7

def pair_lists(station_blocks):
    first_blocks = []
    second_blocks = []
    for first_id in range(station_blocks):
        for second_id in range(first_id, station_blocks):
            first_blocks.append(first_id)
            second_blocks.append(second_id)
    first_blocks.append(0)
    second_blocks.append(0)
    return (np.array(first_blocks, np.int32), np.array(second_blocks, np.int32))

def bernstein(channel_ids, total_channels):
    position = (channel_ids.astype(jnp.float32) + 0.5) / total_channels
    others = 1.0 - position
    return jnp.stack([others ** 3, 3.0 * position * others ** 2, 3.0 * position ** 2 * others, position ** 3], axis=1)

def coherency(brightness, frequency):
    spectral = frequency ** (-SPECTRAL_INDEX)
    bright_re = spectral[:, None, None, None] * brightness[:4].reshape(2, 2, -1)[None]
    bright_im = spectral[:, None, None, None] * brightness[4:].reshape(2, 2, -1)[None]
    return (bright_re, bright_im)

def rotate(gain_block, delay_block, frequency):
    phases = 2.0 * math.pi * frequency[:, None, None, None] * delay_block[None]
    cosine = jnp.cos(phases)[:, :, None]
    sine_part = jnp.sin(phases)[:, :, None]
    gain_re = jnp.transpose(gain_block[:4], (2, 0, 1, 3))[:, None]
    gain_im = jnp.transpose(gain_block[4:], (2, 0, 1, 3))[:, None]
    rot_re = cosine * gain_re - sine_part * gain_im
    rot_im = cosine * gain_im + sine_part * gain_re
    split_shape = rot_re.shape[:2] + (2, 2) + rot_re.shape[3:]
    return (rot_re.reshape(split_shape), rot_im.reshape(split_shape))

def combine_part(rotated, bright):
    return jnp.einsum('ctikda,ckld->ctilda', rotated, bright, precision=PRECISE)

def left_side(rot_re, rot_im, bright_re, bright_im):
    mixed_re = combine_part(rot_re, bright_re) - combine_part(rot_im, bright_im)
    mixed_im = combine_part(rot_re, bright_im) + combine_part(rot_im, bright_re)
    return jnp.stack([mixed_re, mixed_im], axis=3)

def right_side(rot_re, rot_im):
    real_rows = jnp.stack([rot_re, rot_im], axis=3)
    imag_rows = jnp.stack([-rot_im, rot_re], axis=3)
    return jnp.stack([real_rows, imag_rows], axis=2)

def predict(left_rows, right_rows):
    visible = jnp.einsum('ctirlda,ctqjrldb->ctqijab', left_rows, right_rows, precision=PRECISE)
    return visible.reshape(visible.shape[:2] + (8,) + visible.shape[5:])

def visibilities(first_gain, second_gain, first_delay, second_delay, frequency, bright_re, bright_im):
    first_re, first_im = rotate(first_gain, first_delay, frequency)
    second_re, second_im = rotate(second_gain, second_delay, frequency)
    return predict(left_side(first_re, first_im, bright_re, bright_im), right_side(second_re, second_im))

def slot_geometry(pair_id, flagged, first_table, second_table, block_size, pair_count):
    pair_ids = jnp.arange(pair_count + 1, dtype=jnp.int32)
    onehot = (pair_id == pair_ids).astype(jnp.int32)
    first_id = jnp.sum(onehot * first_table).astype(jnp.int32)
    second_id = jnp.sum(onehot * second_table).astype(jnp.int32)
    row_ids = jnp.arange(block_size, dtype=jnp.int32)
    is_live = pair_id < pair_count
    keep_mask = (row_ids[:, None] >= flagged) & ((first_id < second_id) | (row_ids[:, None] < row_ids[None, :])) & is_live
    return (first_id, second_id, is_live, keep_mask.astype(jnp.float32))

def cho_apply(factor_lower, moments):
    order_size = factor_lower.shape[0]
    forward = []
    for row_index in range(order_size):
        running = moments[row_index]
        for col_index in range(row_index):
            running = running - factor_lower[row_index, col_index] * forward[col_index]
        forward.append(running / factor_lower[row_index, row_index])
    backward = [None] * order_size
    for row_index in range(order_size - 1, -1, -1):
        running = forward[row_index]
        for col_index in range(row_index + 1, order_size):
            running = running - factor_lower[col_index, row_index] * backward[col_index]
        backward[row_index] = running / factor_lower[row_index, row_index]
    return jnp.stack(backward, axis=0)

def reference(observed, pair_table, flag_rows, gains, duals, prior_coeffs, delays, brightness):
    first_table, second_table = pair_lists(N_STN)
    pair_count = N_STN * (N_STN + 1) // 2
    block_size = STATIONS // N_STN
    penalty = STATIONS * DUMPS / 16.0
    channel_ids = jnp.arange(CHANNELS, dtype=jnp.int32)
    frequency = 1.0 + channel_ids.astype(jnp.float32) / CHANNELS
    basis = bernstein(channel_ids, CHANNELS)
    prior_fit = jnp.einsum('ck,edks->edcs', basis, prior_coeffs, precision=PRECISE)
    target = prior_fit - duals
    bright_re, bright_im = coherency(brightness, frequency)

    def channel_inputs(channel):
        freq_one = lax.dynamic_slice_in_dim(frequency, channel, 1, 0)
        re_one = lax.dynamic_slice_in_dim(bright_re, channel, 1, 0)
        im_one = lax.dynamic_slice_in_dim(bright_im, channel, 1, 0)
        return (freq_one, re_one, im_one)

    def blocks(field, first_id, second_id, axis_pos):
        return (lax.dynamic_slice_in_dim(field, first_id * block_size, block_size, axis_pos), lax.dynamic_slice_in_dim(field, second_id * block_size, block_size, axis_pos))

    def data_loss(gains_one, channel):
        data = lax.dynamic_slice_in_dim(observed, channel, 1, 1)
        freq_one, re_one, im_one = channel_inputs(channel)

        def visit(running, item):
            observed_slot, pair_id, flagged = item
            first_id, second_id, is_live, keep_mask = slot_geometry(pair_id, flagged, first_table, second_table, block_size, pair_count)
            first_gain, second_gain = blocks(gains_one, first_id, second_id, 3)
            first_delay, second_delay = blocks(delays, first_id, second_id, 2)
            misfit = observed_slot.astype(jnp.float32) - visibilities(first_gain, second_gain, first_delay, second_delay, freq_one, re_one, im_one)
            return (running + 0.5 * jnp.sum(keep_mask * misfit * misfit), None)
        running, unused = lax.scan(visit, jnp.zeros((), jnp.float32), (data, pair_table, flag_rows))
        return running
    gains_now = gains
    for iteration in range(ITERS):

        def channel_gradient(channel):
            gains_one = lax.dynamic_slice_in_dim(gains_now, channel, 1, 2)
            loss_value, pullback = jax.vjp(lambda field: data_loss(field, channel), gains_one)
            return pullback(jnp.ones_like(loss_value))[0][:, :, 0]
        data_grad = jnp.transpose(lax.map(channel_gradient, channel_ids), (1, 2, 0, 3))
        direction = data_grad + penalty * (gains_now - target)

        def channel_curvature(channel):
            freq_one, re_one, im_one = channel_inputs(channel)
            gains_one = lax.dynamic_slice_in_dim(gains_now, channel, 1, 2)
            step_one = lax.dynamic_slice_in_dim(direction, channel, 1, 2)

            def visit(running, item):
                pair_id, flagged = item
                first_id, second_id, is_live, keep_mask = slot_geometry(pair_id, flagged, first_table, second_table, block_size, pair_count)
                first_gain, second_gain = blocks(gains_one, first_id, second_id, 3)
                first_step, second_step = blocks(step_one, first_id, second_id, 3)
                first_delay, second_delay = blocks(delays, first_id, second_id, 2)
                tangent = jax.jvp(lambda left_gain, right_gain: visibilities(left_gain, right_gain, first_delay, second_delay, freq_one, re_one, im_one), (first_gain, second_gain), (first_step, second_step))[1]
                return (running + jnp.sum(keep_mask * tangent * tangent), None)
            running, unused = lax.scan(visit, jnp.zeros((), jnp.float32), (pair_table, flag_rows))
            return running
        curvature = jnp.sum(lax.map(channel_curvature, channel_ids))
        grad_sq = jnp.sum(direction * direction)
        step_length = grad_sq / (curvature + penalty * grad_sq + EPSILON)
        gains_now = gains_now - step_length * direction
    gram_matrix = jnp.dot(basis.T.astype(jnp.float32), basis.astype(jnp.float32), precision=PRECISE, preferred_element_type=jnp.float32)
    factor_lower = jnp.linalg.cholesky(gram_matrix)
    moments = jnp.einsum('ck,edcs->keds', basis, gains_now + duals, precision=PRECISE)
    solved = cho_apply(factor_lower, moments)
    coeffs = jnp.transpose(solved, (1, 2, 0, 3))
    fitted = jnp.einsum('ck,edks->edcs', basis, coeffs, precision=PRECISE)
    return (gains_now, coeffs, duals + gains_now - fitted)
```

```python
import functools
import math

import jax
import jax.numpy as jnp
import numpy as np
from jax import lax
from jax.experimental import pallas as pl
from jax.experimental.pallas import tpu as pltpu
from jax.sharding import PartitionSpec as P

ITERS = 3
EPSILON = 1e-06
SPECTRAL_INDEX = 0.7
DIRS = 8
CHUNK = 128
VMEM_BYTES = 48 * 1024 * 1024
F32 = jnp.float32
BF16 = jnp.bfloat16

NT = (((1,), (1,)), ((), ()))
NN = (((1,), (0,)), ((), ()))
TN = (((0,), (0,)), ((), ()))


def dot(lhs, rhs, dims):
    return lax.dot_general(lhs, rhs, dims, preferred_element_type=F32)


def pair_lists(station_blocks):
    return [(p, q) for p in range(station_blocks) for q in range(p, station_blocks)]


def bernstein_np(total_channels):
    position = (np.arange(total_channels, dtype=np.float64) + 0.5) / total_channels
    others = 1.0 - position
    return np.stack(
        [others**3, 3.0 * position * others**2, 3.0 * position**2 * others, position**3], axis=1
    )


def split(x):
    high = x.astype(BF16)
    return high, (x - high.astype(F32)).astype(BF16)


def pack(x):
    high, low = split(x)
    return jnp.concatenate([high, low], axis=0)


def trig(delay, freq):
    turns = delay * freq
    turns = turns - jnp.floor(turns + 0.5)
    x = turns * math.pi
    x2 = x * x
    sin_half = x * (
        1.0
        + x2
        * (
            -1.0 / 6
            + x2
            * (
                1.0 / 120
                + x2
                * (
                    -1.0 / 5040
                    + x2 * (1.0 / 362880 + x2 * (-1.0 / 39916800 + x2 * (1.0 / 6227020800)))
                )
            )
        )
    )
    cos_half = 1.0 + x2 * (
        -0.5
        + x2
        * (
            1.0 / 24
            + x2
            * (
                -1.0 / 720
                + x2
                * (
                    1.0 / 40320
                    + x2 * (-1.0 / 3628800 + x2 * (1.0 / 479001600 + x2 * (-1.0 / 87178291200)))
                )
            )
        )
    )
    return 1.0 - 2.0 * sin_half * sin_half, 2.0 * sin_half * cos_half


def rotate(field, cosine, sine):
    re = [field[8 * m : 8 * m + 8] for m in range(4)]
    im = [field[32 + 8 * m : 40 + 8 * m] for m in range(4)]
    return (
        [cosine * re[m] - sine * im[m] for m in range(4)],
        [cosine * im[m] + sine * re[m] for m in range(4)],
    )


def coherency_rows(coh, width):
    reps = width // coh.shape[1]
    rows = [jnp.concatenate([coh[8 * e : 8 * e + 8]] * reps, axis=1) for e in range(8)]
    return rows[:4], rows[4:]


def left_rows(rot, bright):
    (a_re, a_im), (c_re, c_im) = rot, bright
    out = []
    for i in range(2):
        re_rows, im_rows = [], []
        for l in range(2):
            re = im = None
            for k in range(2):
                ar, ai, cr, ci = a_re[2 * i + k], a_im[2 * i + k], c_re[2 * k + l], c_im[2 * k + l]
                tr, ti = ar * cr - ai * ci, ar * ci + ai * cr
                re, im = (tr, ti) if re is None else (re + tr, im + ti)
            re_rows.append(re)
            im_rows.append(im)
        out.append(jnp.concatenate(re_rows + im_rows, axis=0))
    return out


def right_rows(rot):
    a_re, a_im = rot
    real = [
        jnp.concatenate([a_re[2 * j], a_re[2 * j + 1], a_im[2 * j], a_im[2 * j + 1]], axis=0)
        for j in range(2)
    ]
    imag = [
        jnp.concatenate([-a_im[2 * j], -a_im[2 * j + 1], a_re[2 * j], a_re[2 * j + 1]], axis=0)
        for j in range(2)
    ]
    return real + imag


def field_gradient(h_left, h_right, bright, cosine, sine):
    c_re, c_im = bright
    g_re, g_im = [], []
    for i in range(2):
        for k in range(2):
            j = i
            re = h_right[j][8 * k : 8 * k + 8] + h_right[2 + j][16 + 8 * k : 24 + 8 * k]
            im = h_right[j][16 + 8 * k : 24 + 8 * k] - h_right[2 + j][8 * k : 8 * k + 8]
            for l in range(2):
                lr = h_left[i][8 * l : 8 * l + 8]
                li = h_left[i][16 + 8 * l : 24 + 8 * l]
                cr, ci = c_re[2 * k + l], c_im[2 * k + l]
                re = re + lr * cr + li * ci
                im = im + li * cr - lr * ci
            g_re.append(cosine * re + sine * im)
            g_im.append(cosine * im - sine * re)
    return jnp.concatenate(g_re + g_im, axis=0)


def data_kernel(
    block,
    pairs,
    dumps,
    slots,
    penalty,
    with_target,
    table,
    flags,
    own,
    freq,
    field_ref,
    delay_ref,
    coh_ref,
    *refs,
):
    if with_target:
        target_ref, refs = refs[0], refs[1:]
    observed, out_ref, held, sems, xp, yp, hl, ha = refs
    stations = field_ref.shape[1]
    pair_count = len(pairs)

    def copy_of(slot, t):
        return pltpu.make_async_copy(observed.at[slot, t], held.at[slot, t], sems.at[slot, t])

    for slot in range(slots):

        @pl.when(table[slot] < pair_count)
        def _():
            for t in range(dumps):
                copy_of(slot, t).start()

    freq_value = freq[0]
    bright = coherency_rows(coh_ref[...], stations)
    for t in range(dumps):
        cosine, sine = trig(delay_ref[8 * t : 8 * t + 8, :], freq_value)
        rot = rotate(field_ref[...], cosine, sine)
        for i, rows in enumerate(left_rows(rot, bright)):
            xp[t, i] = pack(rows)
        for rj, rows in enumerate(right_rows(rot)):
            yp[t, rj] = pack(rows)
    hl[...] = jnp.zeros_like(hl)
    ha[...] = jnp.zeros_like(ha)

    def visit(slot, unused):
        pair = table[slot]

        @pl.when(pair < pair_count)
        def _():
            first, second = jnp.int32(0), jnp.int32(0)
            for k, (p, q) in enumerate(pairs):
                first = first + jnp.where(pair == k, p, 0)
                second = second + jnp.where(pair == k, q, 0)
            row = lax.broadcasted_iota(jnp.int32, (block, block), 0)
            col = lax.broadcasted_iota(jnp.int32, (block, block), 1)
            keep = (row < col) | (first < second)
            lane = lax.broadcasted_iota(jnp.int32, (1, block), 1)
            live = (lane >= flags[slot]).astype(F32)
            live16 = live.astype(BF16)
            at_p = pl.ds(pl.multiple_of(first * block, CHUNK), block)
            at_q = pl.ds(pl.multiple_of(second * block, CHUNK), block)
            for t in range(dumps):
                copy_of(slot, t).wait()
                acc_left = [None, None]
                acc_right = [None] * 4
                xs = [xp[t, i, :, at_p] * live16 for i in range(2)]
                ys = [yp[t, rj, :, at_q] for rj in range(4)]
                for r in range(2):
                    for i in range(2):
                        for j in range(2):
                            tile = held[slot, t, 4 * r + 2 * i + j]
                            tile = jnp.where(keep, tile, jnp.zeros_like(tile))
                            rj = 2 * r + j
                            left = dot(ys[rj], tile, NT)
                            right = dot(xs[i], tile, NN)
                            acc_left[i] = left if acc_left[i] is None else acc_left[i] + left
                            acc_right[rj] = right if acc_right[rj] is None else acc_right[rj] + right
                for i in range(2):
                    hl[t, i, :, at_p] += (acc_left[i][:32] + acc_left[i][32:]) * live
                for rj in range(4):
                    ha[t, rj, :, at_q] += acc_right[rj][:32] + acc_right[rj][32:]

        return unused

    lax.fori_loop(0, slots, visit, jnp.int32(0))

    total = None
    for t in range(dumps):
        cosine, sine = trig(delay_ref[8 * t : 8 * t + 8, :], freq_value)
        piece = field_gradient(
            [hl[t, i] for i in range(2)], [ha[t, rj] for rj in range(4)], bright, cosine, sine
        )
        total = piece if total is None else total + piece
    out_ref[...] = -total
    at_own = pl.ds(pl.multiple_of(own[0] * block, CHUNK), block)
    prior = field_ref[:, at_own]
    if with_target:
        prior = prior - target_ref[...]
    out_ref[:, at_own] += penalty * prior


def data_part(geometry, table, flags, own, freq, field, delays, coh, target, observed):
    block, pairs, penalty = geometry
    slots, dumps = observed.shape[:2]
    stations = field.shape[1]
    smem = pl.BlockSpec(memory_space=pltpu.SMEM)
    vmem = pl.BlockSpec(memory_space=pltpu.VMEM)
    hbm = pl.BlockSpec(memory_space=pl.ANY)
    with_target = target is not None
    body = functools.partial(data_kernel, block, pairs, dumps, slots, penalty, with_target)
    extra = (target,) if with_target else ()
    return pl.pallas_call(
        body,
        name="data_part",
        out_shape=jax.ShapeDtypeStruct(field.shape, F32),
        in_specs=[smem] * 4 + [vmem] * (3 + len(extra)) + [hbm],
        out_specs=vmem,
        scratch_shapes=[
            pltpu.VMEM(observed.shape, BF16),
            pltpu.SemaphoreType.DMA((slots, dumps)),
            pltpu.VMEM((dumps, 2, 64, stations), BF16),
            pltpu.VMEM((dumps, 4, 64, stations), BF16),
            pltpu.VMEM((dumps, 2, 32, stations), F32),
            pltpu.VMEM((dumps, 4, 32, stations), F32),
        ],
        compiler_params=pltpu.CompilerParams(vmem_limit_bytes=VMEM_BYTES),
        cost_estimate=pl.CostEstimate(
            flops=6000000000, bytes_accessed=8000000, transcendentals=0
        ),
    )(table, flags, own, freq, field, delays, coh, *extra, observed)


def fold_gram(high_low, other, rows):
    wide = dot(high_low, other[:rows], NT)
    return wide[:rows] + wide[rows:] + dot(high_low[:rows], other[rows:], NT)


def apply_gram(gram, packed, rows):
    size = gram.shape[0]
    both = pack(gram)
    wide = dot(both, packed[:rows], NN)
    return wide[:size] + wide[size:] + dot(both[:size], packed[rows:], NN)


def lanes(parts, start, size):
    return jnp.concatenate([part[:, start : start + size] for part in parts], axis=1)


def model_kernel(block, pairs, dumps, penalty, update, freq, *refs):
    if update:
        scal_ref, current_ref, previous_ref, linear_ref, mine_ref, theirs_ref, *refs = refs
    else:
        current_ref, mine_ref, theirs_ref, *refs = refs
    delay_ref, coh_ref, table_ref, current_out, linear_out, direction_out, sums_out, hl, ha = refs
    stations = current_ref.shape[1]
    chunk = min(CHUNK, block)
    per_block = block // chunk
    chunks = stations // chunk
    blocks = stations // block

    step_linear = mine_ref[...] + theirs_ref[...]
    if update:
        grad_sq = scal_ref[0:1, :]
        curvature = scal_ref[1:2, :]
        alpha = grad_sq / (curvature + penalty * grad_sq + EPSILON)
        alpha = jnp.concatenate([alpha] * (stations // 128), axis=1)
        current = current_ref[...] - alpha * previous_ref[...]
        linear = linear_ref[...] - alpha * step_linear
    else:
        current = current_ref[...]
        linear = step_linear
    current_out[...] = current
    linear_out[...] = linear

    ids, counts = table_ref[0:1, :], table_ref[1:2, :]
    lane = lax.broadcasted_iota(jnp.int32, (1, block), 1).astype(F32)
    masks = {}
    for k, pair in enumerate(pairs):
        flagged = jnp.sum(jnp.where(ids == float(k), counts, 0.0), axis=1, keepdims=True)
        masks[pair] = (lane >= flagged).astype(F32)

    def mask_of(pair, chunk_id):
        start = (chunk_id % per_block) * chunk
        return masks[pair][:, start : start + chunk]

    def twice(mask):
        return jnp.concatenate([mask, mask], axis=1)

    row = lax.broadcasted_iota(jnp.int32, (2 * chunk, 4 * chunk), 0) % chunk
    col = lax.broadcasted_iota(jnp.int32, (2 * chunk, 4 * chunk), 1) % chunk
    upper = row < col

    freq_value = freq[0]
    bright = coherency_rows(coh_ref[...], stations)

    def rect_terms(chunk_id):
        own = chunk_id // per_block
        terms = []
        inside = [c for c in range(chunk_id + 1, (own + 1) * per_block)]
        if inside:
            terms.append(((own, own), inside))
        for q in range(own + 1, blocks):
            terms.append(((own, q), list(range(q * per_block, (q + 1) * per_block))))
        return terms

    gradient = linear
    trigs = []
    for t in range(dumps):
        cosine, sine = trig(delay_ref[8 * t : 8 * t + 8, :], freq_value)
        trigs.append((cosine, sine))
        rot = rotate(current, cosine, sine)
        xs = [pack(v) for v in left_rows(rot, bright)]
        ys = [pack(v) for v in right_rows(rot)]
        gram_y = [
            fold_gram(lanes(ys, c * chunk, chunk), lanes(ys, c * chunk, chunk), 32)
            for c in range(chunks)
        ]
        sums_x = [None] * chunks
        for c in range(chunks):
            xc = lanes(xs, c * chunk, chunk)
            yc = lanes(ys, c * chunk, chunk)
            own = c // per_block
            xw = xc * twice(mask_of((own, own), c)).astype(BF16)
            yn = jnp.concatenate([yc[:32], yc[:32], yc[32:], yc[32:]], axis=0)
            model = dot(jnp.concatenate([xw, xw], axis=0), yn, TN)
            model = jnp.where(upper, model, 0.0)
            high, low = split(model)
            left = dot(yc, high, NT) + dot(yc, low, NT)
            right = dot(xw, high, NN) + dot(xw, low, NN)
            left = left[:32] + left[32:]
            right = right[:32] + right[32:]
            for pair, others in rect_terms(c):
                gram = gram_y[others[0]]
                for o in others[1:]:
                    gram = gram + gram_y[o]
                mask = twice(mask_of(pair, c))
                left = left + apply_gram(gram, xc, 32) * mask
                gram_x = fold_gram(xc * mask.astype(BF16), xc, 32)
                for o in others:
                    sums_x[o] = gram_x if sums_x[o] is None else sums_x[o] + gram_x
            if sums_x[c] is not None:
                right = right + apply_gram(sums_x[c], yc, 32)
            for i in range(2):
                hl[i, :, c * chunk : (c + 1) * chunk] = left[:, i * chunk : (i + 1) * chunk]
            for rj in range(4):
                ha[rj, :, c * chunk : (c + 1) * chunk] = right[:, rj * chunk : (rj + 1) * chunk]
        gradient = gradient + field_gradient(
            [hl[i] for i in range(2)], [ha[rj] for rj in range(4)], bright, cosine, sine
        )
    direction_out[...] = gradient
    direction = gradient

    squares = jnp.zeros((8, 4 * chunk), F32)
    grams = jnp.zeros((64, 64), F32)
    for t in range(dumps):
        cosine, sine = trigs[t]
        rot = rotate(current, cosine, sine)
        step = rotate(direction, cosine, sine)
        xs = [pack(v) for v in left_rows(rot, bright)]
        ys = [pack(v) for v in right_rows(rot)]
        dxs = [pack(v) for v in left_rows(step, bright)]
        dys = [pack(v) for v in right_rows(step)]

        def stacked(first, second, c):
            one = lanes(first, c * chunk, chunk)
            two = lanes(second, c * chunk, chunk)
            return jnp.concatenate([one[:32], two[:32], one[32:], two[32:]], axis=0)

        gram_y = [None] * chunks
        for c in range(chunks):
            xc = stacked(dxs, xs, c)
            yc = stacked(ys, dys, c)
            own = c // per_block
            xw = xc * twice(mask_of((own, own), c)).astype(BF16)
            tangent = dot(
                jnp.concatenate([xw, xw], axis=0),
                jnp.concatenate([yc[:64], yc[:64], yc[64:], yc[64:]], axis=0),
                TN,
            )
            tangent = jnp.where(upper, tangent, 0.0)
            square = tangent * tangent
            squares = squares + jnp.sum(square.reshape(2 * chunk // 8, 8, 4 * chunk), axis=0)
            if c > 0:
                gram_y[c] = fold_gram(yc, yc, 64)
        for c in range(chunks):
            for pair, others in rect_terms(c):
                gram = gram_y[others[0]]
                for o in others[1:]:
                    gram = gram + gram_y[o]
                xc = stacked(dxs, xs, c)
                gram_x = fold_gram(xc * twice(mask_of(pair, c)).astype(BF16), xc, 64)
                grams = grams + gram * gram_x
    curvature = jnp.sum(squares, keepdims=True) + jnp.sum(grams, keepdims=True)
    grad_sq = jnp.sum(direction * direction, keepdims=True)
    row8 = lax.broadcasted_iota(jnp.int32, (8, 128), 0)
    sums_out[...] = jnp.where(row8 == 0, grad_sq, jnp.where(row8 == 1, curvature, 0.0))


def model_part(geometry, dumps, freq, state, delays, coh, table):
    block, pairs, penalty = geometry
    smem = pl.BlockSpec(memory_space=pltpu.SMEM)
    vmem = pl.BlockSpec(memory_space=pltpu.VMEM)
    update = len(state) == 6
    field = state[1] if update else state[0]
    stations = field.shape[1]
    like = jax.ShapeDtypeStruct(field.shape, F32)
    return pl.pallas_call(
        functools.partial(model_kernel, block, pairs, dumps, penalty, update),
        name="model_part",
        out_shape=(like, like, like, jax.ShapeDtypeStruct((8, 128), F32)),
        in_specs=[smem] + [vmem] * (len(state) + 3),
        out_specs=(vmem,) * 4,
        scratch_shapes=[pltpu.VMEM((2, 32, stations), F32), pltpu.VMEM((4, 32, stations), F32)],
        compiler_params=pltpu.CompilerParams(vmem_limit_bytes=VMEM_BYTES),
        cost_estimate=pl.CostEstimate(
            flops=6000000000, bytes_accessed=2000000, transcendentals=0
        ),
    )(freq, *state, delays, coh, table)


def chan_sum(value, count):
    bit = 1
    while bit < count:
        offsets = [bit, 2 * bit, 3 * bit] if 4 * bit <= count else [bit]
        got = [lax.ppermute(value, "chan", [(i, i ^ o) for i in range(count)]) for o in offsets]
        if len(got) == 3:
            value = (value + got[0]) + (got[1] + got[2])
            bit *= 4
        else:
            value = value + got[0]
            bit *= 2
    return value


def other_stations(value, count):
    if count == 2:
        return lax.ppermute(value, "stn", [(0, 1), (1, 0)])
    return lax.psum(value, "stn") - value


def shards(observed, pair_table, flag_rows, gains, duals, prior_coeffs, delays, brightness):
    stn_count = lax.axis_size("stn")
    chan_count = lax.axis_size("chan")
    stn_index = lax.axis_index("stn")
    chan_index = lax.axis_index("chan")
    entries, dirs, chan_local, block = gains.shape
    slots, dumps = observed.shape[0], observed.shape[2]
    stations = block * stn_count
    pairs = pair_lists(stn_count)
    penalty = stations * dumps / 16.0
    geometry = (block, pairs, penalty)
    basis = bernstein_np(chan_count)
    solve = basis @ np.linalg.inv(basis.T @ basis)
    basis_row = lax.dynamic_slice_in_dim(jnp.asarray(basis, F32), chan_index, 1, 0)[0]
    solve_row = lax.dynamic_slice_in_dim(jnp.asarray(solve, F32), chan_index, 1, 0)[0]

    frequency = 1.0 + chan_index.astype(F32) / chan_count
    coh = brightness * frequency ** (-SPECTRAL_INDEX)
    coh = jnp.broadcast_to(coh.reshape(entries * dirs, 1), (entries * dirs, 128))
    freq = frequency.reshape(1)
    own = stn_index.reshape(1).astype(jnp.int32)

    gains_own = gains.reshape(entries * dirs, block)
    duals_own = duals.reshape(entries * dirs, block)
    ids = jnp.pad(pair_table.astype(F32), (0, block - slots), constant_values=-1.0)
    counts = jnp.pad(flag_rows.astype(F32), (0, block - slots))
    rows = jnp.concatenate(
        [gains_own, delays.reshape(dumps * dirs, block), ids[None], counts[None], jnp.zeros((6, block), F32)]
    )
    rows = lax.all_gather(rows, "stn", axis=1, tiled=True)
    field = rows[: entries * dirs]
    delay_all = rows[entries * dirs : entries * dirs + dumps * dirs]
    table = rows[entries * dirs + dumps * dirs :]

    prior = prior_coeffs.reshape(entries * dirs, 4, block)
    prior_fit = sum(basis_row[k] * prior[:, k] for k in range(4))
    target = prior_fit - duals_own

    observed = observed.reshape((slots,) + observed.shape[2:])
    data = functools.partial(data_part, geometry, pair_table, flag_rows, own, freq)
    mine = data(field, delay_all, coh, target, observed)
    theirs = other_stations(mine, stn_count)
    state = (field, mine, theirs)
    for iteration in range(ITERS):
        current, linear, direction, sums = model_part(
            geometry, dumps, freq, state, delay_all, coh, table
        )
        if iteration + 1 < ITERS:
            mine = data(direction, delay_all, coh, None, observed)
            theirs = other_stations(mine, stn_count)
        sums = chan_sum(sums, chan_count)
        state = (sums, current, direction, linear, mine, theirs)

    alpha = sums[0, 0] / (sums[1, 0] + penalty * sums[0, 0] + EPSILON)
    at_own = stn_index * block
    gains_new = lax.dynamic_slice_in_dim(
        current, at_own, block, 1
    ) - alpha * lax.dynamic_slice_in_dim(direction, at_own, block, 1)
    shifted = gains_new + duals_own
    parts = jnp.stack([solve_row[k] * shifted for k in range(4)])
    parts = parts.reshape(chan_count, -1, 128)
    parts = jnp.sum(lax.all_to_all(parts, "chan", 0, 0, tiled=True), axis=0)
    parts = jnp.broadcast_to(parts[None], (chan_count,) + parts.shape)
    coeffs = lax.all_to_all(parts, "chan", 0, 0, tiled=True).reshape(4, entries * dirs, block)
    fitted = sum(basis_row[k] * coeffs[k] for k in range(4))
    coeffs_out = jnp.transpose(coeffs.reshape(4, entries, dirs, block), (1, 2, 0, 3))
    return (
        gains_new.reshape(gains.shape),
        coeffs_out,
        (shifted - fitted).reshape(gains.shape),
    )


def solution(mesh):
    return jax.shard_map(
        shards,
        mesh=mesh,
        in_specs=(
            P("stn", ("band", "chan"), None, None, None, None),
            P("stn"),
            P("stn"),
            P(None, None, ("band", "chan"), "stn"),
            P(None, None, ("band", "chan"), "stn"),
            P("band", None, None, "stn"),
            P(None, None, "stn"),
            P("band", None),
        ),
        out_specs=(
            P(None, None, ("band", "chan"), "stn"),
            P("band", None, None, "stn"),
            P(None, None, ("band", "chan"), "stn"),
        ),
        check_vma=False,
    )
```

```python
import functools
import math

import jax
import jax.numpy as jnp
import numpy as np
from jax import lax
from jax.experimental import pallas as pl
from jax.experimental.pallas import tpu as pltpu
from jax.sharding import PartitionSpec as P

ITERS = 3
EPSILON = 1e-06
SPECTRAL_INDEX = 0.7
DIRS = 8
CHUNK = 128
VMEM_BYTES = 48 * 1024 * 1024
F32 = jnp.float32
BF16 = jnp.bfloat16

NT = (((1,), (1,)), ((), ()))
NN = (((1,), (0,)), ((), ()))
TN = (((0,), (0,)), ((), ()))


def dot(lhs, rhs, dims):
    return lax.dot_general(lhs, rhs, dims, preferred_element_type=F32)


def pair_lists(station_blocks):
    return [(p, q) for p in range(station_blocks) for q in range(p, station_blocks)]


def bernstein_np(total_channels):
    position = (np.arange(total_channels, dtype=np.float64) + 0.5) / total_channels
    others = 1.0 - position
    return np.stack(
        [others**3, 3.0 * position * others**2, 3.0 * position**2 * others, position**3], axis=1
    )


def split(x):
    high = x.astype(BF16)
    return high, (x - high.astype(F32)).astype(BF16)


def pack(x):
    high, low = split(x)
    return jnp.concatenate([high, low], axis=0)


def trig(delay, freq):
    turns = delay * freq
    turns = turns - jnp.floor(turns + 0.5)
    x = turns * math.pi
    x2 = x * x
    sin_half = x * (
        1.0
        + x2
        * (
            -1.0 / 6
            + x2
            * (
                1.0 / 120
                + x2
                * (
                    -1.0 / 5040
                    + x2 * (1.0 / 362880 + x2 * (-1.0 / 39916800 + x2 * (1.0 / 6227020800)))
                )
            )
        )
    )
    cos_half = 1.0 + x2 * (
        -0.5
        + x2
        * (
            1.0 / 24
            + x2
            * (
                -1.0 / 720
                + x2
                * (
                    1.0 / 40320
                    + x2 * (-1.0 / 3628800 + x2 * (1.0 / 479001600 + x2 * (-1.0 / 87178291200)))
                )
            )
        )
    )
    return 1.0 - 2.0 * sin_half * sin_half, 2.0 * sin_half * cos_half


def rotate(field, cosine, sine):
    re = [field[8 * m : 8 * m + 8] for m in range(4)]
    im = [field[32 + 8 * m : 40 + 8 * m] for m in range(4)]
    return (
        [cosine * re[m] - sine * im[m] for m in range(4)],
        [cosine * im[m] + sine * re[m] for m in range(4)],
    )


def coherency_rows(coh, width):
    reps = width // coh.shape[1]
    rows = [jnp.concatenate([coh[8 * e : 8 * e + 8]] * reps, axis=1) for e in range(8)]
    return rows[:4], rows[4:]


def left_rows(rot, bright):
    (a_re, a_im), (c_re, c_im) = rot, bright
    out = []
    for i in range(2):
        re_rows, im_rows = [], []
        for l in range(2):
            re = im = None
            for k in range(2):
                ar, ai, cr, ci = a_re[2 * i + k], a_im[2 * i + k], c_re[2 * k + l], c_im[2 * k + l]
                tr, ti = ar * cr - ai * ci, ar * ci + ai * cr
                re, im = (tr, ti) if re is None else (re + tr, im + ti)
            re_rows.append(re)
            im_rows.append(im)
        out.append(jnp.concatenate(re_rows + im_rows, axis=0))
    return out


def right_rows(rot):
    a_re, a_im = rot
    real = [
        jnp.concatenate([a_re[2 * j], a_re[2 * j + 1], a_im[2 * j], a_im[2 * j + 1]], axis=0)
        for j in range(2)
    ]
    imag = [
        jnp.concatenate([-a_im[2 * j], -a_im[2 * j + 1], a_re[2 * j], a_re[2 * j + 1]], axis=0)
        for j in range(2)
    ]
    return real + imag


def field_gradient(h_left, h_right, bright, cosine, sine):
    c_re, c_im = bright
    g_re, g_im = [], []
    for i in range(2):
        for k in range(2):
            j = i
            re = h_right[j][8 * k : 8 * k + 8] + h_right[2 + j][16 + 8 * k : 24 + 8 * k]
            im = h_right[j][16 + 8 * k : 24 + 8 * k] - h_right[2 + j][8 * k : 8 * k + 8]
            for l in range(2):
                lr = h_left[i][8 * l : 8 * l + 8]
                li = h_left[i][16 + 8 * l : 24 + 8 * l]
                cr, ci = c_re[2 * k + l], c_im[2 * k + l]
                re = re + lr * cr + li * ci
                im = im + li * cr - lr * ci
            g_re.append(cosine * re + sine * im)
            g_im.append(cosine * im - sine * re)
    return jnp.concatenate(g_re + g_im, axis=0)


def coherency_tile(brightness, freq):
    spectral = jnp.exp(-SPECTRAL_INDEX * jnp.log(jnp.full((8, 128), freq, F32)))
    tiles = []
    for e in range(8):
        column = jnp.transpose(jnp.broadcast_to(brightness[e : e + 1, :], (8, 8)))[:, :1]
        tiles.append(column * spectral)
    return jnp.concatenate(tiles, axis=0)


def position_of(chan_count):
    return lax.axis_index("chan").astype(F32) * (1.0 / chan_count)


def frequency_of(chan_count):
    return 1.0 + position_of(chan_count)


def basis_of(chan_count):
    x = position_of(chan_count) + 0.5 / chan_count
    y = 1.0 - x
    return [y * y * y, 3.0 * x * y * y, 3.0 * x * x * y, x * x * x]


def solve_of(chan_count):
    basis = bernstein_np(chan_count)
    inverse = np.linalg.inv(basis.T @ basis)
    row = basis_of(chan_count)
    return [sum(row[m] * float(inverse[m, k]) for m in range(4)) for k in range(4)]


def data_kernel(block, pairs, dumps, slots, penalty, chan_count, first_call, joined, *refs):
    if first_call:
        if joined:
            table, flags, gains_all, delays_all, *refs = refs
        else:
            table, flags, gains_mine, gains_other, delays_mine, delays_other, *refs = refs
        duals, prior, brightness, observed, field_ref, delay_ref, coh_ref, out_ref, *refs = refs
    else:
        table, flags, field_ref, delay_ref, coh_ref, observed, out_ref, *refs = refs
    held, sems, xp, yp, hl, ha = refs
    stations = field_ref.shape[1]
    pair_count = len(pairs)
    own = lax.axis_index("stn")
    at_own = pl.ds(pl.multiple_of(own * block, CHUNK), block)

    def copy_of(slot, t):
        return pltpu.make_async_copy(observed.at[slot, t], held.at[slot, t], sems.at[slot, t])

    for slot in range(slots):

        @pl.when(table[slot] < pair_count)
        def _():
            for t in range(dumps):
                copy_of(slot, t).start()

    freq_value = frequency_of(chan_count)
    if first_call:
        if joined:
            field_ref[...] = gains_all[:, 0, :]
            delay_ref[...] = delays_all[...]
        else:
            at_other = pl.ds(pl.multiple_of((1 - own) * block, CHUNK), block)
            field_ref[:, at_own] = gains_mine[:, 0, :]
            field_ref[:, at_other] = gains_other[:, 0, :]
            delay_ref[:, at_own] = delays_mine[...]
            delay_ref[:, at_other] = delays_other[...]
        coh_ref[...] = coherency_tile(brightness[...], freq_value)
    bright = coherency_rows(coh_ref[...], stations)
    for t in range(dumps):
        cosine, sine = trig(delay_ref[8 * t : 8 * t + 8, :], freq_value)
        rot = rotate(field_ref[...], cosine, sine)
        for i, rows in enumerate(left_rows(rot, bright)):
            xp[t, i] = pack(rows)
        for rj, rows in enumerate(right_rows(rot)):
            yp[t, rj] = pack(rows)
    hl[...] = jnp.zeros_like(hl)
    ha[...] = jnp.zeros_like(ha)

    def visit(slot, unused):
        pair = table[slot]

        @pl.when(pair < pair_count)
        def _():
            first, second = jnp.int32(0), jnp.int32(0)
            for k, (p, q) in enumerate(pairs):
                first = first + jnp.where(pair == k, p, 0)
                second = second + jnp.where(pair == k, q, 0)
            row = lax.broadcasted_iota(jnp.int32, (block, block), 0)
            col = lax.broadcasted_iota(jnp.int32, (block, block), 1)
            keep = (row < col) | (first < second)
            lane = lax.broadcasted_iota(jnp.int32, (1, block), 1)
            live = (lane >= flags[slot]).astype(F32)
            live16 = live.astype(BF16)
            at_p = pl.ds(pl.multiple_of(first * block, CHUNK), block)
            at_q = pl.ds(pl.multiple_of(second * block, CHUNK), block)
            for t in range(dumps):
                copy_of(slot, t).wait()
                acc_left = [None, None]
                acc_right = [None] * 4
                xs = [xp[t, i, :, at_p] * live16 for i in range(2)]
                ys = [yp[t, rj, :, at_q] for rj in range(4)]
                for r in range(2):
                    for i in range(2):
                        for j in range(2):
                            tile = held[slot, t, 4 * r + 2 * i + j]
                            tile = jnp.where(keep, tile, jnp.zeros_like(tile))
                            rj = 2 * r + j
                            left = dot(ys[rj], tile, NT)
                            right = dot(xs[i], tile, NN)
                            acc_left[i] = left if acc_left[i] is None else acc_left[i] + left
                            acc_right[rj] = right if acc_right[rj] is None else acc_right[rj] + right
                for i in range(2):
                    hl[t, i, :, at_p] += (acc_left[i][:32] + acc_left[i][32:]) * live
                for rj in range(4):
                    ha[t, rj, :, at_q] += acc_right[rj][:32] + acc_right[rj][32:]

        return unused

    lax.fori_loop(0, slots, visit, jnp.int32(0))

    total = None
    for t in range(dumps):
        cosine, sine = trig(delay_ref[8 * t : 8 * t + 8, :], freq_value)
        piece = field_gradient(
            [hl[t, i] for i in range(2)], [ha[t, rj] for rj in range(4)], bright, cosine, sine
        )
        total = piece if total is None else total + piece
    out_ref[:64, :] = -total
    out_ref[:64, at_own] += penalty * field_ref[:, at_own]
    if first_call:
        target = -duals[:, 0, :]
        basis = basis_of(chan_count)
        for k in range(4):
            target = target + basis[k] * prior[:, k, :]
        out_ref[:64, at_own] += -penalty * target
        lane = lax.broadcasted_iota(jnp.int32, (8, stations), 1)
        counts = jnp.zeros((8, stations), F32)
        for slot in range(slots):
            held_here = (lane == table[slot]) & (lane < pair_count)
            counts = counts + jnp.where(held_here, flags[slot].astype(F32), 0.0)
        out_ref[64:, :] = counts


def data_part(geometry, table, flags, fields, observed):
    block, pairs, penalty, chan_count, stations = geometry
    slots, dumps = observed.shape[:2]
    smem = pl.BlockSpec(memory_space=pltpu.SMEM)
    vmem = pl.BlockSpec(memory_space=pltpu.VMEM)
    hbm = pl.BlockSpec(memory_space=pl.ANY)
    first_call = len(fields) > 3
    joined = len(fields) == 5
    body = functools.partial(
        data_kernel, block, pairs, dumps, slots, penalty, chan_count, first_call, joined
    )
    shapes = [(64, stations), (8 * dumps, stations), (64, 128), (72, stations)]
    if not first_call:
        shapes = [(64, stations)]
    return pl.pallas_call(
        body,
        name="data_part",
        out_shape=tuple(jax.ShapeDtypeStruct(s, F32) for s in shapes),
        in_specs=[smem] * 2 + [vmem] * len(fields) + [hbm],
        out_specs=(vmem,) * len(shapes),
        scratch_shapes=[
            pltpu.VMEM(observed.shape, BF16),
            pltpu.SemaphoreType.DMA((slots, dumps)),
            pltpu.VMEM((dumps, 2, 64, stations), BF16),
            pltpu.VMEM((dumps, 4, 64, stations), BF16),
            pltpu.VMEM((dumps, 2, 32, stations), F32),
            pltpu.VMEM((dumps, 4, 32, stations), F32),
        ],
        compiler_params=pltpu.CompilerParams(vmem_limit_bytes=VMEM_BYTES),
        cost_estimate=pl.CostEstimate(
            flops=6000000000, bytes_accessed=8000000, transcendentals=0
        ),
    )(table, flags, *fields, observed)


def fold_gram(high_low, other, rows):
    wide = dot(high_low, other[:rows], NT)
    return wide[:rows] + wide[rows:] + dot(high_low[:rows], other[rows:], NT)


def apply_gram(gram, packed, rows):
    size = gram.shape[0]
    both = pack(gram)
    wide = dot(both, packed[:rows], NN)
    return wide[:size] + wide[size:] + dot(both[:size], packed[rows:], NN)


def lanes(parts, start, size):
    return jnp.concatenate([part[:, start : start + size] for part in parts], axis=1)


def model_kernel(block, pairs, dumps, penalty, chan_count, update, *refs):
    if update:
        scal_ref, current_ref, previous_ref, linear_ref, counts_ref, mine_ref, theirs_ref, *refs = refs
        delay_ref, coh_ref, current_out, *refs = refs
    else:
        current_ref, mine_ref, theirs_ref, delay_ref, coh_ref, counts_out, *refs = refs
    linear_out, direction_out, sums_out, hl, ha = refs
    stations = current_ref.shape[1]
    chunk = min(CHUNK, block)
    per_block = block // chunk
    chunks = stations // chunk
    blocks = stations // block

    step_linear = mine_ref[:64, :] + theirs_ref[:64, :]
    if update:
        counts = counts_ref[0:1, :]
        grad_sq = scal_ref[0:1, :]
        curvature = scal_ref[1:2, :]
        alpha = grad_sq / (curvature + penalty * grad_sq + EPSILON)
        alpha = jnp.concatenate([alpha] * (stations // 128), axis=1)
        current = current_ref[...] - alpha * previous_ref[...]
        linear = linear_ref[...] - alpha * step_linear
        current_out[...] = current
    else:
        counts_out[...] = mine_ref[64:, :128] + theirs_ref[64:, :128]
        counts = mine_ref[64:65, :128] + theirs_ref[64:65, :128]
        current = current_ref[...]
        linear = step_linear
    linear_out[...] = linear

    lane = lax.broadcasted_iota(jnp.int32, (1, block), 1).astype(F32)
    masks = {}
    for k, pair in enumerate(pairs):
        masks[pair] = (lane >= counts[:, k : k + 1]).astype(F32)

    def mask_of(pair, chunk_id):
        start = (chunk_id % per_block) * chunk
        return masks[pair][:, start : start + chunk]

    def twice(mask):
        return jnp.concatenate([mask, mask], axis=1)

    row = lax.broadcasted_iota(jnp.int32, (2 * chunk, 4 * chunk), 0) % chunk
    col = lax.broadcasted_iota(jnp.int32, (2 * chunk, 4 * chunk), 1) % chunk
    upper = row < col

    freq_value = frequency_of(chan_count)
    bright = coherency_rows(coh_ref[...], stations)

    def rect_terms(chunk_id):
        own = chunk_id // per_block
        terms = []
        inside = [c for c in range(chunk_id + 1, (own + 1) * per_block)]
        if inside:
            terms.append(((own, own), inside))
        for q in range(own + 1, blocks):
            terms.append(((own, q), list(range(q * per_block, (q + 1) * per_block))))
        return terms

    gradient = linear
    trigs = []
    for t in range(dumps):
        cosine, sine = trig(delay_ref[8 * t : 8 * t + 8, :], freq_value)
        trigs.append((cosine, sine))
        rot = rotate(current, cosine, sine)
        xs = [pack(v) for v in left_rows(rot, bright)]
        ys = [pack(v) for v in right_rows(rot)]
        gram_y = [
            fold_gram(lanes(ys, c * chunk, chunk), lanes(ys, c * chunk, chunk), 32)
            for c in range(chunks)
        ]
        sums_x = [None] * chunks
        for c in range(chunks):
            xc = lanes(xs, c * chunk, chunk)
            yc = lanes(ys, c * chunk, chunk)
            own = c // per_block
            xw = xc * twice(mask_of((own, own), c)).astype(BF16)
            yn = jnp.concatenate([yc[:32], yc[:32], yc[32:], yc[32:]], axis=0)
            model = dot(jnp.concatenate([xw, xw], axis=0), yn, TN)
            model = jnp.where(upper, model, 0.0)
            high, low = split(model)
            left = dot(yc, high, NT) + dot(yc, low, NT)
            right = dot(xw, high, NN) + dot(xw, low, NN)
            left = left[:32] + left[32:]
            right = right[:32] + right[32:]
            for pair, others in rect_terms(c):
                gram = gram_y[others[0]]
                for o in others[1:]:
                    gram = gram + gram_y[o]
                mask = twice(mask_of(pair, c))
                left = left + apply_gram(gram, xc, 32) * mask
                gram_x = fold_gram(xc * mask.astype(BF16), xc, 32)
                for o in others:
                    sums_x[o] = gram_x if sums_x[o] is None else sums_x[o] + gram_x
            if sums_x[c] is not None:
                right = right + apply_gram(sums_x[c], yc, 32)
            for i in range(2):
                hl[i, :, c * chunk : (c + 1) * chunk] = left[:, i * chunk : (i + 1) * chunk]
            for rj in range(4):
                ha[rj, :, c * chunk : (c + 1) * chunk] = right[:, rj * chunk : (rj + 1) * chunk]
        gradient = gradient + field_gradient(
            [hl[i] for i in range(2)], [ha[rj] for rj in range(4)], bright, cosine, sine
        )
    direction_out[...] = gradient
    direction = gradient

    squares = jnp.zeros((8, 4 * chunk), F32)
    grams = jnp.zeros((64, 64), F32)
    for t in range(dumps):
        cosine, sine = trigs[t]
        rot = rotate(current, cosine, sine)
        step = rotate(direction, cosine, sine)
        xs = [pack(v) for v in left_rows(rot, bright)]
        ys = [pack(v) for v in right_rows(rot)]
        dxs = [pack(v) for v in left_rows(step, bright)]
        dys = [pack(v) for v in right_rows(step)]

        def stacked(first, second, c):
            one = lanes(first, c * chunk, chunk)
            two = lanes(second, c * chunk, chunk)
            return jnp.concatenate([one[:32], two[:32], one[32:], two[32:]], axis=0)

        gram_y = [None] * chunks
        for c in range(chunks):
            xc = stacked(dxs, xs, c)
            yc = stacked(ys, dys, c)
            own = c // per_block
            xw = xc * twice(mask_of((own, own), c)).astype(BF16)
            tangent = dot(
                jnp.concatenate([xw, xw], axis=0),
                jnp.concatenate([yc[:64], yc[:64], yc[64:], yc[64:]], axis=0),
                TN,
            )
            tangent = jnp.where(upper, tangent, 0.0)
            square = tangent * tangent
            squares = squares + jnp.sum(square.reshape(2 * chunk // 8, 8, 4 * chunk), axis=0)
            if c > 0:
                gram_y[c] = fold_gram(yc, yc, 64)
        for c in range(chunks):
            for pair, others in rect_terms(c):
                gram = gram_y[others[0]]
                for o in others[1:]:
                    gram = gram + gram_y[o]
                xc = stacked(dxs, xs, c)
                gram_x = fold_gram(xc * twice(mask_of(pair, c)).astype(BF16), xc, 64)
                grams = grams + gram * gram_x
    curvature = jnp.sum(squares, keepdims=True) + jnp.sum(grams, keepdims=True)
    grad_sq = jnp.sum(direction * direction, keepdims=True)
    row8 = lax.broadcasted_iota(jnp.int32, (8, 128), 0)
    sums_out[...] = jnp.where(row8 == 0, grad_sq, jnp.where(row8 == 1, curvature, 0.0))


def model_part(geometry, dumps, state, delays, coh):
    block, pairs, penalty, chan_count, stations = geometry
    vmem = pl.BlockSpec(memory_space=pltpu.VMEM)
    update = len(state) > 3
    like = jax.ShapeDtypeStruct((64, stations), F32)
    tile = jax.ShapeDtypeStruct((8, 128), F32)
    return pl.pallas_call(
        functools.partial(model_kernel, block, pairs, dumps, penalty, chan_count, update),
        name="model_part",
        out_shape=(like if update else tile, like, like, tile),
        in_specs=[vmem] * (len(state) + 2),
        out_specs=(vmem,) * 4,
        scratch_shapes=[pltpu.VMEM((2, 32, stations), F32), pltpu.VMEM((4, 32, stations), F32)],
        compiler_params=pltpu.CompilerParams(vmem_limit_bytes=VMEM_BYTES),
        cost_estimate=pl.CostEstimate(
            flops=6000000000, bytes_accessed=2000000, transcendentals=0
        ),
    )(*state, delays, coh)


def last_step_kernel(
    block, penalty, chan_count, sums, current, direction, duals, gains_out, shifted_out, keep_out, send_out
):
    at_own = pl.ds(pl.multiple_of(lax.axis_index("stn") * block, CHUNK), block)
    grad_sq = sums[0:1, :]
    alpha = grad_sq / (sums[1:2, :] + penalty * grad_sq + EPSILON)
    alpha = jnp.concatenate([alpha] * (block // 128), axis=1)
    gains_new = current[:, at_own] - alpha * direction[:, at_own]
    gains_out[:, 0, :] = gains_new
    shifted = gains_new + duals[:, 0, :]
    shifted_out[...] = shifted
    half = block // 2
    odd = lax.axis_index("chan") % 2 == 1
    low, high = shifted[:, :half], shifted[:, half:]
    keep, send = jnp.where(odd, high, low), jnp.where(odd, low, high)
    for k, scale in enumerate(solve_of(chan_count)):
        keep_out[64 * k : 64 * k + 64, :] = scale * keep
        send_out[64 * k : 64 * k + 64, :] = scale * send


def last_step(geometry, sums, current, direction, duals):
    block, pairs, penalty, chan_count, stations = geometry
    vmem = pl.BlockSpec(memory_space=pltpu.VMEM)
    shapes = [(64, 1, block), (64, block), (256, block // 2), (256, block // 2)]
    return pl.pallas_call(
        functools.partial(last_step_kernel, block, penalty, chan_count),
        name="last_step",
        out_shape=tuple(jax.ShapeDtypeStruct(s, F32) for s in shapes),
        in_specs=[vmem] * 4,
        out_specs=(vmem,) * 4,
    )(sums, current, direction, duals)


def consensus_kernel(block, chan_count, mine, theirs, shifted, coeffs_out, duals_out):
    odd = lax.axis_index("chan") % 2 == 1
    fitted = None
    for k, scale in enumerate(basis_of(chan_count)):
        one, two = mine[64 * k : 64 * k + 64, :], theirs[64 * k : 64 * k + 64, :]
        coeffs = jnp.concatenate([jnp.where(odd, two, one), jnp.where(odd, one, two)], axis=1)
        coeffs_out[:, k, :] = coeffs
        fitted = scale * coeffs if fitted is None else fitted + scale * coeffs
    duals_out[:, 0, :] = shifted[...] - fitted


def consensus(geometry, mine, theirs, shifted):
    block, pairs, penalty, chan_count, stations = geometry
    vmem = pl.BlockSpec(memory_space=pltpu.VMEM)
    shapes = [(64, 4, block), (64, 1, block)]
    return pl.pallas_call(
        functools.partial(consensus_kernel, block, chan_count),
        name="consensus",
        out_shape=tuple(jax.ShapeDtypeStruct(s, F32) for s in shapes),
        in_specs=[vmem] * 3,
        out_specs=(vmem,) * 2,
    )(mine, theirs, shifted)


def swap(value, count, offset):
    return lax.ppermute(value, "chan", [(i, i ^ offset) for i in range(count)])


def sum_stage(value, count, bit):
    if 4 * bit <= count:
        got = [swap(value, count, o * bit) for o in (1, 2, 3)]
        return 4 * bit, (value + got[0]) + (got[1] + got[2])
    return 2 * bit, value + swap(value, count, bit)


def other_stations(value):
    return lax.ppermute(value, "stn", [(0, 1), (1, 0)])


def both_stations(value, count):
    if count == 2:
        return value, other_stations(value)
    return jnp.zeros_like(value), lax.psum(value, "stn")


def shards(observed, pair_table, flag_rows, gains, duals, prior_coeffs, delays, brightness):
    stn_count = lax.axis_size("stn")
    chan_count = lax.axis_size("chan")
    entries, dirs, chan_local, block = gains.shape
    slots, dumps = observed.shape[0], observed.shape[2]
    stations = block * stn_count
    pairs = pair_lists(stn_count)
    penalty = stations * dumps / 16.0
    geometry = (block, pairs, penalty, chan_count, stations)

    observed = observed.reshape((slots,) + observed.shape[2:])
    gains_own = gains.reshape(entries * dirs, 1, block)
    duals_own = duals.reshape(entries * dirs, 1, block)
    prior = prior_coeffs.reshape(entries * dirs, 4, block)
    delays = delays.reshape(dumps * dirs, block)
    if stn_count == 2:
        parts = (gains_own, other_stations(gains_own), delays, other_stations(delays))
    else:
        parts = (
            lax.all_gather(gains_own, "stn", axis=2, tiled=True),
            lax.all_gather(delays, "stn", axis=1, tiled=True),
        )

    data = functools.partial(data_part, geometry, pair_table, flag_rows)
    current, delay_all, coh, mine = data(parts + (duals_own, prior, brightness), observed)
    mine, theirs = both_stations(mine, stn_count)
    counts, linear, direction, sums = model_part(
        geometry, dumps, (current, mine, theirs), delay_all, coh
    )
    for iteration in range(ITERS):
        last = iteration + 1 == ITERS
        bit, sums = sum_stage(sums, chan_count, 1)
        if not last:
            (mine,) = data((direction, delay_all, coh), observed)
            sums, mine = lax.optimization_barrier((sums, mine))
            mine, theirs = both_stations(mine, stn_count)
        while bit < chan_count:
            bit, sums = sum_stage(sums, chan_count, bit)
        if not last:
            current, linear, direction, sums = model_part(
                geometry,
                dumps,
                (sums, current, direction, linear, counts, mine, theirs),
                delay_all,
                coh,
            )

    gains_new, shifted, keep, send = last_step(geometry, sums, current, direction, duals_own)
    total = keep + swap(send, chan_count, 1)
    bit = 2
    while bit < chan_count:
        total = total + swap(total, chan_count, bit)
        bit *= 2
    coeffs, duals_new = consensus(geometry, total, swap(total, chan_count, 1), shifted)
    return (
        gains_new.reshape(gains.shape),
        coeffs.reshape(entries, dirs, 4, block),
        duals_new.reshape(gains.shape),
    )


def solution(mesh):
    return jax.shard_map(
        shards,
        mesh=mesh,
        in_specs=(
            P("stn", ("band", "chan"), None, None, None, None),
            P("stn"),
            P("stn"),
            P(None, None, ("band", "chan"), "stn"),
            P(None, None, ("band", "chan"), "stn"),
            P("band", None, None, "stn"),
            P(None, None, "stn"),
            P("band", None),
        ),
        out_specs=(
            P(None, None, ("band", "chan"), "stn"),
            P("band", None, None, "stn"),
            P(None, None, ("band", "chan"), "stn"),
        ),
        check_vma=False,
    )
```

```python
import functools
import math

import jax
import jax.numpy as jnp
import numpy as np
from jax import lax
from jax.experimental import pallas as pl
from jax.experimental.pallas import tpu as pltpu
from jax.sharding import PartitionSpec as P

ITERS = 3
EPSILON = 1e-06
SPECTRAL_INDEX = 0.7
DIRS = 8
CHUNK = 128
VMEM_BYTES = 48 * 1024 * 1024
AHEAD = 2
F32 = jnp.float32
BF16 = jnp.bfloat16

NT = (((1,), (1,)), ((), ()))
NN = (((1,), (0,)), ((), ()))
TN = (((0,), (0,)), ((), ()))


def dot(lhs, rhs, dims):
    return lax.dot_general(lhs, rhs, dims, preferred_element_type=F32)


def pair_lists(station_blocks):
    return [(p, q) for p in range(station_blocks) for q in range(p, station_blocks)]


def bernstein_np(total_channels):
    position = (np.arange(total_channels, dtype=np.float64) + 0.5) / total_channels
    others = 1.0 - position
    return np.stack(
        [others**3, 3.0 * position * others**2, 3.0 * position**2 * others, position**3], axis=1
    )


def split(x):
    high = x.astype(BF16)
    return high, (x - high.astype(F32)).astype(BF16)


def pack(x):
    high, low = split(x)
    return jnp.concatenate([high, low], axis=0)


def trig(delay, freq):
    turns = delay * freq
    turns = turns - jnp.floor(turns + 0.5)
    x = turns * math.pi
    x2 = x * x
    sin_half = x * (
        1.0
        + x2
        * (
            -1.0 / 6
            + x2
            * (
                1.0 / 120
                + x2
                * (
                    -1.0 / 5040
                    + x2 * (1.0 / 362880 + x2 * (-1.0 / 39916800 + x2 * (1.0 / 6227020800)))
                )
            )
        )
    )
    cos_half = 1.0 + x2 * (
        -0.5
        + x2
        * (
            1.0 / 24
            + x2
            * (
                -1.0 / 720
                + x2
                * (
                    1.0 / 40320
                    + x2 * (-1.0 / 3628800 + x2 * (1.0 / 479001600 + x2 * (-1.0 / 87178291200)))
                )
            )
        )
    )
    return 1.0 - 2.0 * sin_half * sin_half, 2.0 * sin_half * cos_half


def rotate(field, cosine, sine):
    re = [field[8 * m : 8 * m + 8] for m in range(4)]
    im = [field[32 + 8 * m : 40 + 8 * m] for m in range(4)]
    return (
        [cosine * re[m] - sine * im[m] for m in range(4)],
        [cosine * im[m] + sine * re[m] for m in range(4)],
    )


def coherency_rows(coh, width):
    reps = width // coh.shape[1]
    rows = [jnp.concatenate([coh[8 * e : 8 * e + 8]] * reps, axis=1) for e in range(8)]
    return rows[:4], rows[4:]


def left_rows(rot, bright):
    (a_re, a_im), (c_re, c_im) = rot, bright
    out = []
    for i in range(2):
        re_rows, im_rows = [], []
        for l in range(2):
            re = im = None
            for k in range(2):
                ar, ai, cr, ci = a_re[2 * i + k], a_im[2 * i + k], c_re[2 * k + l], c_im[2 * k + l]
                tr, ti = ar * cr - ai * ci, ar * ci + ai * cr
                re, im = (tr, ti) if re is None else (re + tr, im + ti)
            re_rows.append(re)
            im_rows.append(im)
        out.append(jnp.concatenate(re_rows + im_rows, axis=0))
    return out


def right_rows(rot):
    a_re, a_im = rot
    real = [
        jnp.concatenate([a_re[2 * j], a_re[2 * j + 1], a_im[2 * j], a_im[2 * j + 1]], axis=0)
        for j in range(2)
    ]
    imag = [
        jnp.concatenate([-a_im[2 * j], -a_im[2 * j + 1], a_re[2 * j], a_re[2 * j + 1]], axis=0)
        for j in range(2)
    ]
    return real + imag


def field_gradient(h_left, h_right, bright, cosine, sine):
    c_re, c_im = bright
    g_re, g_im = [], []
    for i in range(2):
        for k in range(2):
            j = i
            re = h_right[j][8 * k : 8 * k + 8] + h_right[2 + j][16 + 8 * k : 24 + 8 * k]
            im = h_right[j][16 + 8 * k : 24 + 8 * k] - h_right[2 + j][8 * k : 8 * k + 8]
            for l in range(2):
                lr = h_left[i][8 * l : 8 * l + 8]
                li = h_left[i][16 + 8 * l : 24 + 8 * l]
                cr, ci = c_re[2 * k + l], c_im[2 * k + l]
                re = re + lr * cr + li * ci
                im = im + li * cr - lr * ci
            g_re.append(cosine * re + sine * im)
            g_im.append(cosine * im - sine * re)
    return jnp.concatenate(g_re + g_im, axis=0)


def coherency_tile(brightness, freq):
    spectral = jnp.exp(-SPECTRAL_INDEX * jnp.log(jnp.full((8, 128), freq, F32)))
    tiles = []
    for e in range(8):
        column = jnp.transpose(jnp.broadcast_to(brightness[e : e + 1, :], (8, 8)))[:, :1]
        tiles.append(column * spectral)
    return jnp.concatenate(tiles, axis=0)


def position_of(chan_count):
    return lax.axis_index("chan").astype(F32) * (1.0 / chan_count)


def frequency_of(chan_count):
    return 1.0 + position_of(chan_count)


def basis_of(chan_count):
    x = position_of(chan_count) + 0.5 / chan_count
    y = 1.0 - x
    return [y * y * y, 3.0 * x * y * y, 3.0 * x * x * y, x * x * x]


def solve_of(chan_count):
    basis = bernstein_np(chan_count)
    inverse = np.linalg.inv(basis.T @ basis)
    row = basis_of(chan_count)
    return [sum(row[m] * float(inverse[m, k]) for m in range(4)) for k in range(4)]


def vmem_specs(count):
    return [pl.BlockSpec(memory_space=pltpu.VMEM)] * count


def smem_specs(count):
    return [pl.BlockSpec(memory_space=pltpu.SMEM)] * count


def params():
    return pltpu.CompilerParams(vmem_limit_bytes=VMEM_BYTES)


def shape(*dims, dtype=F32):
    return jax.ShapeDtypeStruct(dims, dtype)


def own_lanes(block):
    return pl.ds(pl.multiple_of(lax.axis_index("stn") * block, CHUNK), block)


def pair_blocks(pairs, pair):
    first, second = jnp.int32(0), jnp.int32(0)
    for k, (p, q) in enumerate(pairs):
        first = first + jnp.where(pair == k, p, 0)
        second = second + jnp.where(pair == k, q, 0)
    return first, second


def prepare_kernel(block, pairs, slots, penalty, chan_count, *refs):
    table, flags, gains, duals, prior, bright, *refs = refs
    gains_out, duals_out, start_out, coh_out, counts_out = refs
    lane = lax.broadcasted_iota(jnp.int32, (8, 128), 1)
    counts = jnp.zeros((8, 128), F32)
    for slot in range(slots):
        held_here = (lane == table[slot]) & (lane < len(pairs))
        counts = counts + jnp.where(held_here, flags[slot].astype(F32), 0.0)
    counts_out[...] = counts
    coh_out[...] = coherency_tile(bright[...], frequency_of(chan_count))
    gains_out[...] = gains[:, 0, :]
    duals_own = duals[:, 0, :]
    duals_out[...] = duals_own
    target = -duals_own
    for k, scale in enumerate(basis_of(chan_count)):
        target = target + scale * prior[:, k, :]
    start_out[...] = -penalty * target


def prepare(geometry, table, flags, gains, duals, prior, brightness):
    block, pairs, dumps, penalty, chan_count, stations = geometry
    return pl.pallas_call(
        functools.partial(
            prepare_kernel, block, pairs, table.shape[0], penalty, chan_count
        ),
        name="prepare",
        out_shape=(
            shape(64, block),
            shape(64, block),
            shape(64, block),
            shape(64, 128),
            shape(8, 128),
        ),
        in_specs=smem_specs(2) + vmem_specs(4),
        out_specs=tuple(vmem_specs(5)),
        compiler_params=params(),
        cost_estimate=pl.CostEstimate(flops=1000000, bytes_accessed=2000000, transcendentals=0),
    )(table, flags, gains, duals, prior, brightness)


def data_kernel(block, pairs, dumps, slots, penalty, chan_count, first_call, joined, *refs):
    table, flags, observed, coh_ref, *refs = refs
    if first_call:
        if joined:
            gains_all, delays_all, *refs = refs
        else:
            gains_mine, gains_other, delays_mine, delays_other, *refs = refs
        start, counts_mine, ids_other, flags_other, out_ref, field_ref, delay_ref, counts_ref, *refs = refs
    else:
        field_ref, delay_ref, out_ref, *refs = refs
    held, sems, order, xp, yp, hl, ha = refs
    stations = field_ref.shape[1]
    pair_count = len(pairs)
    at_own = own_lanes(block)

    live_count = jnp.int32(0)
    for slot in range(slots):
        order[live_count] = jnp.int32(slot)
        live_count = live_count + jnp.where(table[slot] < pair_count, 1, 0)
    items = live_count * dumps

    def copy_of(item):
        slot, t = order[item // dumps], item % dumps
        return pltpu.make_async_copy(observed.at[slot, t], held.at[item], sems.at[item])

    for item in range(min(AHEAD, slots * dumps)):

        @pl.when(item < items)
        def _():
            copy_of(jnp.int32(item)).start()

    freq_value = frequency_of(chan_count)
    if first_call:
        if joined:
            field_ref[...] = gains_all[:, 0, :]
            delay_ref[...] = delays_all[...]
        else:
            at_other = pl.ds(pl.multiple_of((1 - lax.axis_index("stn")) * block, CHUNK), block)
            field_ref[:, at_own] = gains_mine[...]
            field_ref[:, at_other] = gains_other[:, 0, :]
            delay_ref[:, at_own] = delays_mine[...]
            delay_ref[:, at_other] = delays_other[...]
    bright = coherency_rows(coh_ref[...], stations)
    for t in range(dumps):
        cosine, sine = trig(delay_ref[8 * t : 8 * t + 8, :], freq_value)
        rot = rotate(field_ref[...], cosine, sine)
        for i, rows in enumerate(left_rows(rot, bright)):
            xp[t, i] = pack(rows)
        for rj, rows in enumerate(right_rows(rot)):
            yp[t, rj] = pack(rows)
    hl[...] = jnp.zeros_like(hl)
    ha[...] = jnp.zeros_like(ha)

    row = lax.broadcasted_iota(jnp.int32, (block, block), 0)
    col = lax.broadcasted_iota(jnp.int32, (block, block), 1)
    upper = row < col
    lane = lax.broadcasted_iota(jnp.int32, (1, block), 1)

    def visit(item, unused):
        slot, t = order[item // dumps], item % dumps
        first, second = pair_blocks(pairs, table[slot])
        keep = upper | (first < second)
        live = (lane >= flags[slot]).astype(F32)
        live16 = live.astype(BF16)
        at_p = pl.ds(pl.multiple_of(first * block, CHUNK), block)
        at_q = pl.ds(pl.multiple_of(second * block, CHUNK), block)
        copy_of(item).wait()

        @pl.when(item + AHEAD < items)
        def _():
            copy_of(item + AHEAD).start()

        acc_left = [None, None]
        acc_right = [None] * 4
        xs = [xp[t, i, :, at_p] * live16 for i in range(2)]
        ys = [yp[t, rj, :, at_q] for rj in range(4)]
        for r in range(2):
            for i in range(2):
                for j in range(2):
                    tile = held[item, 4 * r + 2 * i + j]
                    tile = jnp.where(keep, tile, jnp.zeros_like(tile))
                    rj = 2 * r + j
                    left = dot(ys[rj], tile, NT)
                    right = dot(xs[i], tile, NN)
                    acc_left[i] = left if acc_left[i] is None else acc_left[i] + left
                    acc_right[rj] = right if acc_right[rj] is None else acc_right[rj] + right
        for i in range(2):
            hl[t, i, :, at_p] += (acc_left[i][:32] + acc_left[i][32:]) * live
        for rj in range(4):
            ha[t, rj, :, at_q] += acc_right[rj][:32] + acc_right[rj][32:]
        return unused

    lax.fori_loop(0, items, visit, jnp.int32(0))

    total = None
    for t in range(dumps):
        cosine, sine = trig(delay_ref[8 * t : 8 * t + 8, :], freq_value)
        piece = field_gradient(
            [hl[t, i] for i in range(2)], [ha[t, rj] for rj in range(4)], bright, cosine, sine
        )
        total = piece if total is None else total + piece
    out_ref[...] = -total
    prior = penalty * field_ref[:, at_own]
    if first_call:
        prior = prior + start[...]
        counts = counts_mine[...]
        pair_lane = lax.broadcasted_iota(jnp.int32, (8, 128), 1)
        for k in range(pair_count):
            theirs = jnp.where(ids_other[...] == k, flags_other[...], 0).astype(F32)
            total_flags = jnp.sum(theirs, axis=1, keepdims=True)
            counts = counts + jnp.where(pair_lane == k, total_flags, 0.0)
        counts_ref[...] = counts
    out_ref[:, at_own] += prior


def data_part(geometry, table, flags, observed, coh, fields):
    block, pairs, dumps, penalty, chan_count, stations = geometry
    slots = observed.shape[0]
    first_call = len(fields) > 2
    joined = len(fields) == 6
    body = functools.partial(
        data_kernel, block, pairs, dumps, slots, penalty, chan_count, first_call, joined
    )
    shapes = [shape(64, stations)]
    if first_call:
        shapes += [shape(64, stations), shape(8 * dumps, stations), shape(8, 128)]
    return pl.pallas_call(
        body,
        name="data_part",
        out_shape=tuple(shapes),
        in_specs=smem_specs(2) + [pl.BlockSpec(memory_space=pl.ANY)] + vmem_specs(1 + len(fields)),
        out_specs=tuple(vmem_specs(len(shapes))),
        scratch_shapes=[
            pltpu.VMEM((slots * dumps,) + observed.shape[2:], BF16),
            pltpu.SemaphoreType.DMA((slots * dumps,)),
            pltpu.SMEM((slots,), jnp.int32),
            pltpu.VMEM((dumps, 2, 64, stations), BF16),
            pltpu.VMEM((dumps, 4, 64, stations), BF16),
            pltpu.VMEM((dumps, 2, 32, stations), F32),
            pltpu.VMEM((dumps, 4, 32, stations), F32),
        ],
        compiler_params=params(),
        cost_estimate=pl.CostEstimate(
            flops=6000000000, bytes_accessed=8000000, transcendentals=0
        ),
    )(table, flags, observed, coh, *fields)


def fold_gram(high_low, other, rows):
    wide = dot(high_low, other[:rows], NT)
    return wide[:rows] + wide[rows:] + dot(high_low[:rows], other[rows:], NT)


def apply_gram(gram, packed, rows):
    size = gram.shape[0]
    both = pack(gram)
    wide = dot(both, packed[:rows], NN)
    return wide[:size] + wide[size:] + dot(both[:size], packed[rows:], NN)


def lanes(parts, start, size):
    return jnp.concatenate([part[:, start : start + size] for part in parts], axis=1)


def twice(mask):
    return jnp.concatenate([mask, mask], axis=1)


class Chunks:
    def __init__(self, block, stations, pairs, counts):
        self.block = block
        self.size = min(CHUNK, block)
        self.per_block = block // self.size
        self.count = stations // self.size
        self.blocks = stations // block
        lane = lax.broadcasted_iota(jnp.int32, (1, block), 1).astype(F32)
        self.masks = {
            pair: (lane >= counts[:, k : k + 1]).astype(F32) for k, pair in enumerate(pairs)
        }
        row = lax.broadcasted_iota(jnp.int32, (2 * self.size, 4 * self.size), 0) % self.size
        col = lax.broadcasted_iota(jnp.int32, (2 * self.size, 4 * self.size), 1) % self.size
        self.upper = row < col

    def mask(self, pair, chunk):
        start = (chunk % self.per_block) * self.size
        return twice(self.masks[pair][:, start : start + self.size])

    def own_pair(self, chunk):
        return (chunk // self.per_block, chunk // self.per_block)

    def rect_terms(self, chunk):
        own = chunk // self.per_block
        terms = []
        inside = list(range(chunk + 1, (own + 1) * self.per_block))
        if inside:
            terms.append(((own, own), inside))
        for q in range(own + 1, self.blocks):
            terms.append(((own, q), list(range(q * self.per_block, (q + 1) * self.per_block))))
        return terms


def sum_of(parts):
    total = parts[0]
    for part in parts[1:]:
        total = total + part
    return total


def halves(rows, axis, bit):
    size = rows.shape[axis] // 2
    low = lax.slice_in_dim(rows, 0, size, axis=axis)
    high = lax.slice_in_dim(rows, size, 2 * size, axis=axis)
    odd = (lax.axis_index("chan") // bit) % 2 == 1
    return jnp.where(odd, high, low), jnp.where(odd, low, high)


def store_moments(fields, sums, chan_count, keep_out, send_out):
    for field_id, field in enumerate(fields):
        for out, part in zip((keep_out, send_out), halves(field, 1, 1)):
            for start, rows in zip((0, 264), halves(part, 0, 2)):
                for k, scale in enumerate(solve_of(chan_count)):
                    at = start + 128 * field_id + 32 * k
                    out[at : at + 32, :] = scale * rows
    for out in (keep_out, send_out):
        out[256:264, :] = sums
        out[520:528, :] = sums


def step_length(grad_sq, curvature, penalty):
    return grad_sq / (curvature + penalty * grad_sq + EPSILON)


def gradient_kernel(block, pairs, dumps, penalty, chan_count, update, *refs):
    counts_ref, delay_ref, coh_ref, current_ref, *refs = refs
    if update:
        sums_ref, direction_ref, *refs = refs
    gradient_out, *refs = refs
    if update:
        current_out, alpha_out, *refs = refs
    hl, ha = refs
    stations = current_ref.shape[1]
    chunks = Chunks(block, stations, pairs, counts_ref[0:1, :])
    size = chunks.size

    current = current_ref[...]
    if update:
        sums = jnp.sum(sums_ref[...], axis=0, keepdims=True)
        alpha = step_length(sums[:, 0:1], sums[:, 1:2], penalty)
        alpha_out[...] = jnp.broadcast_to(alpha, (8, 128))
        current = current - alpha * direction_ref[...]
        current_out[...] = current
    freq_value = frequency_of(chan_count)
    bright = coherency_rows(coh_ref[...], stations)
    gradient = None
    for t in range(dumps):
        cosine, sine = trig(delay_ref[8 * t : 8 * t + 8, :], freq_value)
        rot = rotate(current, cosine, sine)
        xs = [pack(v) for v in left_rows(rot, bright)]
        ys = [pack(v) for v in right_rows(rot)]
        gram_y = [
            fold_gram(lanes(ys, c * size, size), lanes(ys, c * size, size), 32)
            for c in range(chunks.count)
        ]
        sums_x = [None] * chunks.count
        for c in range(chunks.count):
            xc = lanes(xs, c * size, size)
            yc = lanes(ys, c * size, size)
            xw = xc * chunks.mask(chunks.own_pair(c), c).astype(BF16)
            yn = jnp.concatenate([yc[:32], yc[:32], yc[32:], yc[32:]], axis=0)
            model = dot(jnp.concatenate([xw, xw], axis=0), yn, TN)
            model = jnp.where(chunks.upper, model, 0.0)
            high, low = split(model)
            left = dot(yc, high, NT) + dot(yc, low, NT)
            right = dot(xw, high, NN) + dot(xw, low, NN)
            left = left[:32] + left[32:]
            right = right[:32] + right[32:]
            for pair, others in chunks.rect_terms(c):
                mask = chunks.mask(pair, c)
                left = left + apply_gram(sum_of([gram_y[o] for o in others]), xc, 32) * mask
                gram_x = fold_gram(xc * mask.astype(BF16), xc, 32)
                for o in others:
                    sums_x[o] = gram_x if sums_x[o] is None else sums_x[o] + gram_x
            if sums_x[c] is not None:
                right = right + apply_gram(sums_x[c], yc, 32)
            for i in range(2):
                hl[i, :, c * size : (c + 1) * size] = left[:, i * size : (i + 1) * size]
            for rj in range(4):
                ha[rj, :, c * size : (c + 1) * size] = right[:, rj * size : (rj + 1) * size]
        piece = field_gradient(
            [hl[i] for i in range(2)], [ha[rj] for rj in range(4)], bright, cosine, sine
        )
        gradient = piece if gradient is None else gradient + piece
    gradient_out[...] = gradient


def gradient_part(geometry, counts, delays, coh, current, step):
    block, pairs, dumps, penalty, chan_count, stations = geometry
    update = step is not None
    field = shape(64, stations)
    outs = [field]
    inputs = [counts, delays, coh, current]
    if update:
        inputs += step
        outs += [field, shape(8, 128)]
    return pl.pallas_call(
        functools.partial(gradient_kernel, block, pairs, dumps, penalty, chan_count, update),
        name="gradient_part",
        out_shape=tuple(outs),
        in_specs=vmem_specs(len(inputs)),
        out_specs=tuple(vmem_specs(len(outs))),
        scratch_shapes=[pltpu.VMEM((2, 32, stations), F32), pltpu.VMEM((4, 32, stations), F32)],
        compiler_params=params(),
        cost_estimate=pl.CostEstimate(
            flops=4000000000, bytes_accessed=2000000, transcendentals=0
        ),
    )(*inputs)


def curvature_kernel(block, pairs, dumps, penalty, chan_count, update, last, *refs):
    counts_ref, delay_ref, coh_ref, current_ref, gradient_ref, mine_ref, theirs_ref, *refs = refs
    if update:
        alpha_ref, linear_ref, *refs = refs
    if last:
        duals_ref, *refs = refs
    direction_out, *refs = refs
    if last:
        keep_out, send_out = refs
    else:
        linear_out, sums_out = refs
    stations = current_ref.shape[1]
    chunks = Chunks(block, stations, pairs, counts_ref[0:1, :])
    size = chunks.size

    current = current_ref[...]
    linear = mine_ref[...] + theirs_ref[...]
    if update:
        linear = linear_ref[...] - alpha_ref[0:1, 0:1] * linear
    direction = linear + gradient_ref[...]
    direction_out[...] = direction
    if not last:
        linear_out[...] = linear

    freq_value = frequency_of(chan_count)
    bright = coherency_rows(coh_ref[...], stations)
    squares = jnp.zeros((8, 4 * size), F32)
    grams = jnp.zeros((64, 64), F32)
    for t in range(dumps):
        cosine, sine = trig(delay_ref[8 * t : 8 * t + 8, :], freq_value)
        rot = rotate(current, cosine, sine)
        step = rotate(direction, cosine, sine)
        xs = [pack(v) for v in left_rows(rot, bright)]
        ys = [pack(v) for v in right_rows(rot)]
        dxs = [pack(v) for v in left_rows(step, bright)]
        dys = [pack(v) for v in right_rows(step)]

        def stacked(first, second, c):
            one = lanes(first, c * size, size)
            two = lanes(second, c * size, size)
            return jnp.concatenate([one[:32], two[:32], one[32:], two[32:]], axis=0)

        gram_y = [None] * chunks.count
        for c in range(chunks.count):
            xc = stacked(dxs, xs, c)
            yc = stacked(ys, dys, c)
            xw = xc * chunks.mask(chunks.own_pair(c), c).astype(BF16)
            tangent = dot(
                jnp.concatenate([xw, xw], axis=0),
                jnp.concatenate([yc[:64], yc[:64], yc[64:], yc[64:]], axis=0),
                TN,
            )
            tangent = jnp.where(chunks.upper, tangent, 0.0)
            square = tangent * tangent
            squares = squares + jnp.sum(square.reshape(2 * size // 8, 8, 4 * size), axis=0)
            if c > 0:
                gram_y[c] = fold_gram(yc, yc, 64)
        for c in range(chunks.count):
            for pair, others in chunks.rect_terms(c):
                xc = stacked(dxs, xs, c)
                gram_x = fold_gram(xc * chunks.mask(pair, c).astype(BF16), xc, 64)
                grams = grams + sum_of([gram_y[o] for o in others]) * gram_x
    curvature = jnp.sum(squares, keepdims=True) + jnp.sum(grams, keepdims=True)
    grad_sq = jnp.sum(direction * direction, keepdims=True)
    rows = 8 if last else chan_count
    lane = lax.broadcasted_iota(jnp.int32, (rows, block // 2 if last else 128), 1)
    sums = jnp.where(lane == 0, grad_sq, jnp.where(lane == 1, curvature, 0.0))
    if last:
        base = current_ref[:, own_lanes(block)] + duals_ref[...]
        store_moments(
            (base, direction_out[:, own_lanes(block)]), sums, chan_count, keep_out, send_out
        )
    else:
        sums_out[...] = sums


def curvature_part(geometry, counts, delays, coh, current, gradient, shares, before, duals):
    block, pairs, dumps, penalty, chan_count, stations = geometry
    update, last = before is not None, duals is not None
    field = shape(64, stations)
    if last:
        outs = [field] + [shape(528, block // 2)] * 2
    else:
        outs = [field, field, shape(chan_count, 128)]
    inputs = [counts, delays, coh, current, gradient, *shares]
    if update:
        inputs += before
    if last:
        inputs.append(duals)
    return pl.pallas_call(
        functools.partial(
            curvature_kernel, block, pairs, dumps, penalty, chan_count, update, last
        ),
        name="curvature_part",
        out_shape=tuple(outs),
        in_specs=vmem_specs(len(inputs)),
        out_specs=tuple(vmem_specs(len(outs))),
        compiler_params=params(),
        cost_estimate=pl.CostEstimate(
            flops=2000000000, bytes_accessed=2000000, transcendentals=0
        ),
    )(*inputs)


def combine_kernel(penalty, one, two, coeffs_out, alpha_out):
    total = one[...] + two[...]
    alpha = step_length(total[256:257, 0:1], total[256:257, 1:2], penalty)
    coeffs_out[...] = total[:128] - alpha * total[128:256]
    alpha_out[...] = jnp.broadcast_to(alpha, (8, 128))


def combine(geometry, one, two):
    penalty = geometry[3]
    return pl.pallas_call(
        functools.partial(combine_kernel, penalty),
        name="combine",
        out_shape=(shape(128, one.shape[1]), shape(8, 128)),
        in_specs=vmem_specs(2),
        out_specs=tuple(vmem_specs(2)),
        compiler_params=params(),
    )(one, two)


def last_step_kernel(block, alpha, current, direction, duals, gains_out, shifted_out):
    at_own = own_lanes(block)
    gains_new = current[:, at_own] - alpha[0:1, 0:1] * direction[:, at_own]
    gains_out[:, 0, :] = gains_new
    shifted_out[...] = gains_new + duals[...]


def last_step(geometry, *inputs):
    block = geometry[0]
    return pl.pallas_call(
        functools.partial(last_step_kernel, block),
        name="last_step",
        out_shape=(shape(64, 1, block), shape(64, block)),
        in_specs=vmem_specs(len(inputs)),
        out_specs=tuple(vmem_specs(2)),
        compiler_params=params(),
    )(*inputs)


def consensus_kernel(chan_count, own, core, row, both, shifted, coeffs_out, duals_out):
    place = lax.axis_index("chan")
    odd_core, odd_row = place % 2 == 1, (place // 2) % 2 == 1

    def joined(one, two, odd, axis):
        return jnp.concatenate([jnp.where(odd, two, one), jnp.where(odd, one, two)], axis=axis)

    fitted = None
    for k, scale in enumerate(basis_of(chan_count)):
        at = slice(32 * k, 32 * k + 32)
        coeffs = joined(
            joined(own[at, :], core[at, :], odd_core, 1),
            joined(row[at, :], both[at, :], odd_core, 1),
            odd_row,
            0,
        )
        coeffs_out[:, k, :] = coeffs
        fitted = scale * coeffs if fitted is None else fitted + scale * coeffs
    duals_out[:, 0, :] = shifted[...] - fitted


def consensus(geometry, *inputs):
    block, pairs, dumps, penalty, chan_count, stations = geometry
    return pl.pallas_call(
        functools.partial(consensus_kernel, chan_count),
        name="consensus",
        out_shape=(shape(64, 4, block), shape(64, 1, block)),
        in_specs=vmem_specs(len(inputs)),
        out_specs=tuple(vmem_specs(2)),
        compiler_params=params(),
    )(*inputs)


def swap(value, count, offset):
    return lax.ppermute(value, "chan", [(i, i ^ offset) for i in range(count)])


def other_stations(value):
    return lax.ppermute(value, "stn", [(0, 1), (1, 0)])


def both_stations(value, count):
    if count == 2:
        return value, other_stations(value)
    return jnp.zeros_like(value), lax.psum(value, "stn")


def shards(observed, pair_table, flag_rows, gains, duals, prior_coeffs, delays, brightness):
    stn_count = lax.axis_size("stn")
    chan_count = lax.axis_size("chan")
    entries, dirs, chan_local, block = gains.shape
    slots, dumps = observed.shape[0], observed.shape[2]
    stations = block * stn_count
    pairs = pair_lists(stn_count)
    penalty = stations * dumps / 16.0
    geometry = (block, pairs, dumps, penalty, chan_count, stations)

    observed = observed.reshape((slots,) + observed.shape[2:])
    gains_raw = gains.reshape(entries * dirs, 1, block)
    delays_raw = delays.reshape(dumps * dirs, block)
    duals_raw = duals.reshape(entries * dirs, 1, block)
    prior = prior_coeffs.reshape(entries * dirs, 4, block)
    ids_raw, flags_raw = pair_table.reshape(1, slots), flag_rows.reshape(1, slots)
    if stn_count == 2:
        gains_other, delays_other = other_stations(gains_raw), other_stations(delays_raw)
        ids_other, flags_other = other_stations(ids_raw), other_stations(flags_raw)
    else:
        gains_all = lax.all_gather(gains_raw, "stn", axis=2, tiled=True)
        delays_all = lax.all_gather(delays_raw, "stn", axis=1, tiled=True)
        ids_other = lax.all_gather(ids_raw, "stn", axis=1, tiled=True)
        flags_other = lax.all_gather(flags_raw, "stn", axis=1, tiled=True)
    gains_own, duals_own, start, coh, counts = prepare(
        geometry, pair_table, flag_rows, gains_raw, duals_raw, prior, brightness
    )
    if stn_count == 2:
        fields = (gains_own, gains_other, delays_raw, delays_other)
    else:
        fields = (gains_all, delays_all)
        counts = jnp.zeros_like(counts)
    data = functools.partial(data_part, geometry, pair_table, flag_rows, observed, coh)
    share, current, delay_all, counts = data(fields + (start, counts, ids_other, flags_other))
    shares = both_stations(share, stn_count)

    step = before = None
    for iteration in range(ITERS):
        last = iteration + 1 == ITERS
        gradient, *rest = gradient_part(geometry, counts, delay_all, coh, current, step)
        if step is not None:
            current, alpha = rest
            before = (alpha, linear)
        direction, *rest = curvature_part(
            geometry,
            counts,
            delay_all,
            coh,
            current,
            gradient,
            shares,
            before,
            duals_own if last else None,
        )
        if not last:
            linear, sums = rest
            sums = lax.all_to_all(sums, "chan", 0, 0, tiled=True)
            (share,) = data((direction, delay_all))
            shares = both_stations(share, stn_count)
            step = (sums, direction)

    keep, send = rest
    total = keep + swap(send, chan_count, 1)
    value, other = total[:264], swap(total[264:], chan_count, 2)
    bit = 4
    while bit < chan_count:
        value = value + other
        other = swap(value, chan_count, bit)
        bit *= 2
    quarter, alpha = combine(geometry, value, other)
    gains_new, shifted = last_step(geometry, alpha, current, direction, duals_own)
    quarters = [quarter] + [swap(quarter, chan_count, o) for o in (1, 2, 3)]
    coeffs, duals_new = consensus(geometry, *quarters, shifted)
    return (
        gains_new.reshape(gains.shape),
        coeffs.reshape(entries, dirs, 4, block),
        duals_new.reshape(gains.shape),
    )


def solution(mesh):
    return jax.shard_map(
        shards,
        mesh=mesh,
        in_specs=(
            P("stn", ("band", "chan"), None, None, None, None),
            P("stn"),
            P("stn"),
            P(None, None, ("band", "chan"), "stn"),
            P(None, None, ("band", "chan"), "stn"),
            P("band", None, None, "stn"),
            P(None, None, "stn"),
            P("band", None),
        ),
        out_specs=(
            P(None, None, ("band", "chan"), "stn"),
            P("band", None, None, "stn"),
            P(None, None, ("band", "chan"), "stn"),
        ),
        check_vma=False,
    )
```

```python
import functools
import math

import jax
import jax.numpy as jnp
import numpy as np
from jax import lax
from jax.experimental import pallas as pl
from jax.experimental.pallas import tpu as pltpu
from jax.sharding import PartitionSpec as P

ITERS = 3
EPSILON = 1e-06
SPECTRAL_INDEX = 0.7
DIRS = 8
CHUNK = 128
VMEM_BYTES = 48 * 1024 * 1024
AHEAD = 2
F32 = jnp.float32
BF16 = jnp.bfloat16

NT = (((1,), (1,)), ((), ()))
NN = (((1,), (0,)), ((), ()))
TN = (((0,), (0,)), ((), ()))


def dot(lhs, rhs, dims):
    return lax.dot_general(lhs, rhs, dims, preferred_element_type=F32)


def pair_lists(station_blocks):
    return [(p, q) for p in range(station_blocks) for q in range(p, station_blocks)]


def bernstein_np(total_channels):
    position = (np.arange(total_channels, dtype=np.float64) + 0.5) / total_channels
    others = 1.0 - position
    return np.stack(
        [others**3, 3.0 * position * others**2, 3.0 * position**2 * others, position**3], axis=1
    )


def split(x):
    high = x.astype(BF16)
    return high, (x - high.astype(F32)).astype(BF16)


def pack(x):
    high, low = split(x)
    return jnp.concatenate([high, low], axis=0)


def trig(delay, freq):
    turns = delay * freq
    turns = turns - jnp.floor(turns + 0.5)
    x = turns * math.pi
    x2 = x * x
    sin_half = x * (
        1.0
        + x2
        * (
            -1.0 / 6
            + x2
            * (
                1.0 / 120
                + x2
                * (
                    -1.0 / 5040
                    + x2 * (1.0 / 362880 + x2 * (-1.0 / 39916800 + x2 * (1.0 / 6227020800)))
                )
            )
        )
    )
    cos_half = 1.0 + x2 * (
        -0.5
        + x2
        * (
            1.0 / 24
            + x2
            * (
                -1.0 / 720
                + x2
                * (
                    1.0 / 40320
                    + x2 * (-1.0 / 3628800 + x2 * (1.0 / 479001600 + x2 * (-1.0 / 87178291200)))
                )
            )
        )
    )
    return 1.0 - 2.0 * sin_half * sin_half, 2.0 * sin_half * cos_half


def rotate(field, cosine, sine):
    re = [field[8 * m : 8 * m + 8] for m in range(4)]
    im = [field[32 + 8 * m : 40 + 8 * m] for m in range(4)]
    return (
        [cosine * re[m] - sine * im[m] for m in range(4)],
        [cosine * im[m] + sine * re[m] for m in range(4)],
    )


def coherency_rows(coh, width):
    reps = width // coh.shape[1]
    rows = [jnp.concatenate([coh[8 * e : 8 * e + 8]] * reps, axis=1) for e in range(8)]
    return rows[:4], rows[4:]


def left_rows(rot, bright):
    (a_re, a_im), (c_re, c_im) = rot, bright
    out = []
    for i in range(2):
        re_rows, im_rows = [], []
        for l in range(2):
            re = im = None
            for k in range(2):
                ar, ai, cr, ci = a_re[2 * i + k], a_im[2 * i + k], c_re[2 * k + l], c_im[2 * k + l]
                tr, ti = ar * cr - ai * ci, ar * ci + ai * cr
                re, im = (tr, ti) if re is None else (re + tr, im + ti)
            re_rows.append(re)
            im_rows.append(im)
        out.append(jnp.concatenate(re_rows + im_rows, axis=0))
    return out


def right_rows(rot):
    a_re, a_im = rot
    real = [
        jnp.concatenate([a_re[2 * j], a_re[2 * j + 1], a_im[2 * j], a_im[2 * j + 1]], axis=0)
        for j in range(2)
    ]
    imag = [
        jnp.concatenate([-a_im[2 * j], -a_im[2 * j + 1], a_re[2 * j], a_re[2 * j + 1]], axis=0)
        for j in range(2)
    ]
    return real + imag


def field_gradient(h_left, h_right, bright, cosine, sine):
    c_re, c_im = bright
    g_re, g_im = [], []
    for i in range(2):
        for k in range(2):
            j = i
            re = h_right[j][8 * k : 8 * k + 8] + h_right[2 + j][16 + 8 * k : 24 + 8 * k]
            im = h_right[j][16 + 8 * k : 24 + 8 * k] - h_right[2 + j][8 * k : 8 * k + 8]
            for l in range(2):
                lr = h_left[i][8 * l : 8 * l + 8]
                li = h_left[i][16 + 8 * l : 24 + 8 * l]
                cr, ci = c_re[2 * k + l], c_im[2 * k + l]
                re = re + lr * cr + li * ci
                im = im + li * cr - lr * ci
            g_re.append(cosine * re + sine * im)
            g_im.append(cosine * im - sine * re)
    return jnp.concatenate(g_re + g_im, axis=0)


def coherency_tile(brightness, freq):
    spectral = jnp.exp(-SPECTRAL_INDEX * jnp.log(jnp.full((8, 128), freq, F32)))
    tiles = []
    for e in range(8):
        column = jnp.transpose(jnp.broadcast_to(brightness[e : e + 1, :], (8, 8)))[:, :1]
        tiles.append(column * spectral)
    return jnp.concatenate(tiles, axis=0)


def position_of(chan_count, offset=0):
    place = lax.axis_index("chan")
    if offset:
        place = place ^ offset
    return place.astype(F32) * (1.0 / chan_count)


def frequency_of(chan_count):
    return 1.0 + position_of(chan_count)


def basis_of(chan_count, offset=0):
    x = position_of(chan_count, offset) + 0.5 / chan_count
    y = 1.0 - x
    return [y * y * y, 3.0 * x * y * y, 3.0 * x * x * y, x * x * x]


def solve_of(chan_count, offset):
    basis = bernstein_np(chan_count)
    inverse = np.linalg.inv(basis.T @ basis)
    row = basis_of(chan_count, offset)
    return [sum(row[m] * float(inverse[m, k]) for m in range(4)) for k in range(4)]


def vmem_specs(count):
    return [pl.BlockSpec(memory_space=pltpu.VMEM)] * count


def smem_specs(count):
    return [pl.BlockSpec(memory_space=pltpu.SMEM)] * count


def params():
    return pltpu.CompilerParams(vmem_limit_bytes=VMEM_BYTES)


def shape(*dims, dtype=F32):
    return jax.ShapeDtypeStruct(dims, dtype)


def own_lanes(block):
    return pl.ds(pl.multiple_of(lax.axis_index("stn") * block, CHUNK), block)


def pair_blocks(pairs, pair):
    first, second = jnp.int32(0), jnp.int32(0)
    for k, (p, q) in enumerate(pairs):
        first = first + jnp.where(pair == k, p, 0)
        second = second + jnp.where(pair == k, q, 0)
    return first, second


def prepare_kernel(block, pairs, slots, penalty, chan_count, *refs):
    table, flags, duals, prior, bright, *refs = refs
    duals_out, start_out, coh_out, counts_out = refs
    lane = lax.broadcasted_iota(jnp.int32, (8, 128), 1)
    counts = jnp.zeros((8, 128), F32)
    for slot in range(slots):
        held_here = (lane == table[slot]) & (lane < len(pairs))
        counts = counts + jnp.where(held_here, flags[slot].astype(F32), 0.0)
    counts_out[...] = counts
    coh_out[...] = coherency_tile(bright[...], frequency_of(chan_count))
    duals_own = duals[:, 0, :]
    duals_out[...] = duals_own
    target = -duals_own
    for k, scale in enumerate(basis_of(chan_count)):
        target = target + scale * prior[:, k, :]
    start_out[...] = -penalty * target


def prepare(geometry, table, flags, duals, prior, brightness):
    block, pairs, dumps, penalty, chan_count, stations = geometry
    return pl.pallas_call(
        functools.partial(
            prepare_kernel, block, pairs, table.shape[0], penalty, chan_count
        ),
        name="prepare",
        out_shape=(
            shape(64, block),
            shape(64, block),
            shape(64, 128),
            shape(8, 128),
        ),
        in_specs=smem_specs(2) + vmem_specs(3),
        out_specs=tuple(vmem_specs(4)),
        compiler_params=params(),
        cost_estimate=pl.CostEstimate(flops=1000000, bytes_accessed=2000000, transcendentals=0),
    )(table, flags, duals, prior, brightness)


def data_kernel(block, pairs, dumps, slots, penalty, chan_count, first_call, joined, *refs):
    table, flags, observed, coh_ref, *refs = refs
    if first_call:
        if joined:
            rows_all, *refs = refs
        else:
            rows_mine, rows_other, *refs = refs
        start, counts_mine, ints_other, out_ref, field_ref, delay_ref, counts_ref, *refs = refs
    else:
        field_ref, delay_ref, out_ref, *refs = refs
    held, sems, order, keep, xp, yp, hl, ha = refs
    stations = field_ref.shape[1]
    pair_count = len(pairs)
    at_own = own_lanes(block)

    live_count = jnp.int32(0)
    for slot in range(slots):
        order[live_count] = jnp.int32(slot)
        live_count = live_count + jnp.where(table[slot] < pair_count, 1, 0)
    items = live_count * dumps

    def copy_of(item):
        slot, t = order[item // dumps], item % dumps
        return pltpu.make_async_copy(observed.at[slot, t], held.at[item], sems.at[item])

    for item in range(min(AHEAD, slots * dumps)):

        @pl.when(item < items)
        def _():
            copy_of(jnp.int32(item)).start()

    freq_value = frequency_of(chan_count)
    if first_call:
        if joined:
            field_ref[...] = rows_all[:64, 0, :]
            delay_ref[...] = rows_all[64:, 0, :]
        else:
            at_other = pl.ds(pl.multiple_of((1 - lax.axis_index("stn")) * block, CHUNK), block)
            for at, rows in ((at_own, rows_mine), (at_other, rows_other)):
                field_ref[:, at] = rows[:64, 0, :]
                delay_ref[:, at] = rows[64:, 0, :]
    bright = coherency_rows(coh_ref[...], stations)
    for t in range(dumps):
        cosine, sine = trig(delay_ref[8 * t : 8 * t + 8, :], freq_value)
        rot = rotate(field_ref[...], cosine, sine)
        for i, rows in enumerate(left_rows(rot, bright)):
            xp[t, i] = pack(rows)
        for rj, rows in enumerate(right_rows(rot)):
            yp[t, rj] = pack(rows)
    hl[...] = jnp.zeros_like(hl)
    ha[...] = jnp.zeros_like(ha)

    row = lax.broadcasted_iota(jnp.int32, (block, block), 0)
    col = lax.broadcasted_iota(jnp.int32, (block, block), 1)
    keep[0] = (row < col).astype(F32).astype(BF16)
    keep[1] = jnp.ones((block, block), BF16)
    lane = lax.broadcasted_iota(jnp.int32, (1, block), 1)

    def visit(item, unused):
        slot, t = order[item // dumps], item % dumps
        first, second = pair_blocks(pairs, table[slot])
        kept = keep[jnp.where(first < second, 1, 0)]
        live = (lane >= flags[slot]).astype(F32)
        live16 = live.astype(BF16)
        at_p = pl.ds(pl.multiple_of(first * block, CHUNK), block)
        at_q = pl.ds(pl.multiple_of(second * block, CHUNK), block)
        copy_of(item).wait()

        @pl.when(item + AHEAD < items)
        def _():
            copy_of(item + AHEAD).start()

        acc_left = [None, None]
        acc_right = [None] * 4
        xs = [xp[t, i, :, at_p] * live16 for i in range(2)]
        ys = [yp[t, rj, :, at_q] for rj in range(4)]
        for r in range(2):
            for i in range(2):
                for j in range(2):
                    tile = held[item, 4 * r + 2 * i + j]
                    tile = tile * kept
                    rj = 2 * r + j
                    left = dot(ys[rj], tile, NT)
                    right = dot(xs[i], tile, NN)
                    acc_left[i] = left if acc_left[i] is None else acc_left[i] + left
                    acc_right[rj] = right if acc_right[rj] is None else acc_right[rj] + right
        for i in range(2):
            hl[t, i, :, at_p] += (acc_left[i][:32] + acc_left[i][32:]) * live
        for rj in range(4):
            ha[t, rj, :, at_q] += acc_right[rj][:32] + acc_right[rj][32:]
        return unused

    lax.fori_loop(0, items, visit, jnp.int32(0))

    total = None
    for t in range(dumps):
        cosine, sine = trig(delay_ref[8 * t : 8 * t + 8, :], freq_value)
        piece = field_gradient(
            [hl[t, i] for i in range(2)], [ha[t, rj] for rj in range(4)], bright, cosine, sine
        )
        total = piece if total is None else total + piece
    out_ref[...] = -total
    prior = penalty * field_ref[:, at_own]
    if first_call:
        prior = prior + start[...]
        counts = counts_mine[...]
        pair_lane = lax.broadcasted_iota(jnp.int32, (8, 128), 1)
        for k in range(pair_count):
            theirs = jnp.where(ints_other[0:1, :] == k, ints_other[1:2, :], 0).astype(F32)
            total_flags = jnp.sum(theirs, axis=1, keepdims=True)
            counts = counts + jnp.where(pair_lane == k, total_flags, 0.0)
        counts_ref[...] = counts
    out_ref[:, at_own] += prior


def data_part(geometry, table, flags, observed, coh, fields):
    block, pairs, dumps, penalty, chan_count, stations = geometry
    slots = observed.shape[0]
    first_call = len(fields) > 2
    joined = len(fields) == 4
    body = functools.partial(
        data_kernel, block, pairs, dumps, slots, penalty, chan_count, first_call, joined
    )
    shapes = [shape(64, stations)]
    if first_call:
        shapes += [shape(64, stations), shape(8 * dumps, stations), shape(8, 128)]
    return pl.pallas_call(
        body,
        name="data_part",
        out_shape=tuple(shapes),
        in_specs=smem_specs(2) + [pl.BlockSpec(memory_space=pl.ANY)] + vmem_specs(1 + len(fields)),
        out_specs=tuple(vmem_specs(len(shapes))),
        scratch_shapes=[
            pltpu.VMEM((slots * dumps,) + observed.shape[2:], BF16),
            pltpu.SemaphoreType.DMA((slots * dumps,)),
            pltpu.SMEM((slots,), jnp.int32),
            pltpu.VMEM((2, block, block), BF16),
            pltpu.VMEM((dumps, 2, 64, stations), BF16),
            pltpu.VMEM((dumps, 4, 64, stations), BF16),
            pltpu.VMEM((dumps, 2, 32, stations), F32),
            pltpu.VMEM((dumps, 4, 32, stations), F32),
        ],
        compiler_params=params(),
        cost_estimate=pl.CostEstimate(
            flops=6000000000, bytes_accessed=8000000, transcendentals=0
        ),
    )(table, flags, observed, coh, *fields)


def fold_gram(high_low, other, rows):
    wide = dot(high_low, other[:rows], NT)
    return wide[:rows] + wide[rows:] + dot(high_low[:rows], other[rows:], NT)


def apply_gram(gram, packed, rows):
    size = gram.shape[0]
    both = pack(gram)
    wide = dot(both, packed[:rows], NN)
    return wide[:size] + wide[size:] + dot(both[:size], packed[rows:], NN)


def lanes(parts, start, size):
    return jnp.concatenate([part[:, start : start + size] for part in parts], axis=1)


def twice(mask):
    return jnp.concatenate([mask, mask], axis=1)


class Chunks:
    def __init__(self, block, stations, pairs, counts):
        self.block = block
        self.size = min(CHUNK, block)
        self.per_block = block // self.size
        self.count = stations // self.size
        self.blocks = stations // block
        lane = lax.broadcasted_iota(jnp.int32, (1, block), 1).astype(F32)
        self.masks = {
            pair: (lane >= counts[:, k : k + 1]).astype(F32) for k, pair in enumerate(pairs)
        }
        row = lax.broadcasted_iota(jnp.int32, (2 * self.size, 4 * self.size), 0) % self.size
        col = lax.broadcasted_iota(jnp.int32, (2 * self.size, 4 * self.size), 1) % self.size
        self.upper = row < col

    def mask(self, pair, chunk):
        start = (chunk % self.per_block) * self.size
        return twice(self.masks[pair][:, start : start + self.size])

    def own_pair(self, chunk):
        return (chunk // self.per_block, chunk // self.per_block)

    def rect_terms(self, chunk):
        own = chunk // self.per_block
        terms = []
        inside = list(range(chunk + 1, (own + 1) * self.per_block))
        if inside:
            terms.append(((own, own), inside))
        for q in range(own + 1, self.blocks):
            terms.append(((own, q), list(range(q * self.per_block, (q + 1) * self.per_block))))
        return terms


def sum_of(parts):
    total = parts[0]
    for part in parts[1:]:
        total = total + part
    return total


def halves(rows, axis, odd):
    size = rows.shape[axis] // 2
    low = lax.slice_in_dim(rows, 0, size, axis=axis)
    high = lax.slice_in_dim(rows, size, 2 * size, axis=axis)
    return jnp.where(odd, high, low), jnp.where(odd, low, high)


def store_quarters(fields, sums, outs):
    place = lax.axis_index("chan")
    odd_lanes, odd_rows = place % 2 == 1, (place // 2) % 2 == 1
    for n, field in enumerate(fields):
        for o, part in enumerate(halves(field, 1, odd_lanes)):
            for p, quarter in enumerate(halves(part, 0, odd_rows)):
                outs[o + 2 * p][32 * n : 32 * n + 32, :] = quarter
    for out in outs:
        out[32 * len(fields) :, :] = sums


def step_length(grad_sq, curvature, penalty):
    return grad_sq / (curvature + penalty * grad_sq + EPSILON)


def gradient_kernel(block, pairs, dumps, penalty, chan_count, update, *refs):
    counts_ref, delay_ref, coh_ref, current_ref, *refs = refs
    if update:
        sums_ref, direction_ref, *refs = refs
    gradient_out, *refs = refs
    if update:
        current_out, alpha_out, *refs = refs
    xp, yp, hl, ha = refs
    stations = current_ref.shape[1]
    chunks = Chunks(block, stations, pairs, counts_ref[0:1, :])
    size = chunks.size

    current = current_ref[...]
    if update:
        sums = jnp.sum(sums_ref[...], axis=0, keepdims=True)
        alpha = step_length(sums[:, 0:1], sums[:, 1:2], penalty)
        alpha_out[...] = jnp.broadcast_to(alpha, (8, 128))
        current = current - alpha * direction_ref[...]
        current_out[...] = current
    freq_value = frequency_of(chan_count)
    bright = coherency_rows(coh_ref[...], stations)
    gradient = None
    for t in range(dumps):
        cosine, sine = trig(delay_ref[8 * t : 8 * t + 8, :], freq_value)
        rot = rotate(current, cosine, sine)
        xs = [pack(v) for v in left_rows(rot, bright)]
        ys = [pack(v) for v in right_rows(rot)]
        for i in range(2):
            xp[t, i] = xs[i]
        for rj in range(4):
            yp[t, rj] = ys[rj]
        gram_y = [
            fold_gram(lanes(ys, c * size, size), lanes(ys, c * size, size), 32)
            for c in range(chunks.count)
        ]
        sums_x = [None] * chunks.count
        for c in range(chunks.count):
            xc = lanes(xs, c * size, size)
            yc = lanes(ys, c * size, size)
            xw = xc * chunks.mask(chunks.own_pair(c), c).astype(BF16)
            yn = jnp.concatenate([yc[:32], yc[:32], yc[32:], yc[32:]], axis=0)
            model = dot(jnp.concatenate([xw, xw], axis=0), yn, TN)
            model = jnp.where(chunks.upper, model, 0.0)
            high, low = split(model)
            left = dot(yc, high, NT) + dot(yc, low, NT)
            right = dot(xw, high, NN) + dot(xw, low, NN)
            left = left[:32] + left[32:]
            right = right[:32] + right[32:]
            for pair, others in chunks.rect_terms(c):
                mask = chunks.mask(pair, c)
                left = left + apply_gram(sum_of([gram_y[o] for o in others]), xc, 32) * mask
                gram_x = fold_gram(xc * mask.astype(BF16), xc, 32)
                for o in others:
                    sums_x[o] = gram_x if sums_x[o] is None else sums_x[o] + gram_x
            if sums_x[c] is not None:
                right = right + apply_gram(sums_x[c], yc, 32)
            for i in range(2):
                hl[i, :, c * size : (c + 1) * size] = left[:, i * size : (i + 1) * size]
            for rj in range(4):
                ha[rj, :, c * size : (c + 1) * size] = right[:, rj * size : (rj + 1) * size]
        piece = field_gradient(
            [hl[i] for i in range(2)], [ha[rj] for rj in range(4)], bright, cosine, sine
        )
        gradient = piece if gradient is None else gradient + piece
    gradient_out[...] = gradient


def gradient_part(geometry, counts, delays, coh, current, step):
    block, pairs, dumps, penalty, chan_count, stations = geometry
    update = step is not None
    field = shape(64, stations)
    outs = [field]
    inputs = [counts, delays, coh, current]
    if update:
        inputs += step
        outs += [field, shape(8, 128)]
    outs += [shape(dumps, rows, 64, stations, dtype=BF16) for rows in (2, 4)]
    return pl.pallas_call(
        functools.partial(gradient_kernel, block, pairs, dumps, penalty, chan_count, update),
        name="gradient_part",
        out_shape=tuple(outs),
        in_specs=vmem_specs(len(inputs)),
        out_specs=tuple(vmem_specs(len(outs))),
        scratch_shapes=[pltpu.VMEM((2, 32, stations), F32), pltpu.VMEM((4, 32, stations), F32)],
        compiler_params=params(),
        cost_estimate=pl.CostEstimate(
            flops=4000000000, bytes_accessed=2000000, transcendentals=0
        ),
    )(*inputs)


def curvature_kernel(block, pairs, dumps, penalty, chan_count, update, last, *refs):
    counts_ref, delay_ref, coh_ref, xp, yp, gradient_ref, mine_ref, theirs_ref, *refs = refs
    if update:
        alpha_ref, linear_ref, *refs = refs
    if last:
        duals_ref, current_ref, *refs = refs
    direction_out, *refs = refs
    if not last:
        linear_out, sums_out = refs
    stations = mine_ref.shape[1]
    chunks = Chunks(block, stations, pairs, counts_ref[0:1, :])
    size = chunks.size

    linear = mine_ref[...] + theirs_ref[...]
    if update:
        linear = linear_ref[...] - alpha_ref[0:1, 0:1] * linear
    direction = linear + gradient_ref[...]
    direction_out[...] = direction
    if not last:
        linear_out[...] = linear

    freq_value = frequency_of(chan_count)
    bright = coherency_rows(coh_ref[...], stations)
    squares = jnp.zeros((8, 4 * size), F32)
    grams = jnp.zeros((64, 64), F32)
    if last:
        visited, repeats, copies = range(dumps), 1, 1
    else:
        stn_count = stations // block
        shared = stn_count % dumps == 0
        visited = [lax.axis_index("stn") % dumps] if shared else range(dumps)
        repeats, copies = (stn_count // dumps if shared else stn_count), stn_count
    for t in visited:
        delay = delay_ref[pl.ds(pl.multiple_of(8 * t, 8), 8), :]
        cosine, sine = trig(delay, freq_value)
        step = rotate(direction, cosine, sine)
        xs = [xp[t, i] for i in range(2)]
        ys = [yp[t, rj] for rj in range(4)]
        dxs = [pack(v) for v in left_rows(step, bright)]
        dys = [pack(v) for v in right_rows(step)]

        def stacked(first, second, c):
            one = lanes(first, c * size, size)
            two = lanes(second, c * size, size)
            return jnp.concatenate([one[:32], two[:32], one[32:], two[32:]], axis=0)

        gram_y = [None] * chunks.count
        for c in range(chunks.count):
            xc = stacked(dxs, xs, c)
            yc = stacked(ys, dys, c)
            xw = xc * chunks.mask(chunks.own_pair(c), c).astype(BF16)
            tangent = dot(
                jnp.concatenate([xw, xw], axis=0),
                jnp.concatenate([yc[:64], yc[:64], yc[64:], yc[64:]], axis=0),
                TN,
            )
            tangent = jnp.where(chunks.upper, tangent, 0.0)
            square = tangent * tangent
            squares = squares + jnp.sum(square.reshape(2 * size // 8, 8, 4 * size), axis=0)
            if c > 0:
                gram_y[c] = fold_gram(yc, yc, 64)
        for c in range(chunks.count):
            for pair, others in chunks.rect_terms(c):
                xc = stacked(dxs, xs, c)
                gram_x = fold_gram(xc * chunks.mask(pair, c).astype(BF16), xc, 64)
                grams = grams + sum_of([gram_y[o] for o in others]) * gram_x
    curvature = jnp.sum(squares, keepdims=True) + jnp.sum(grams, keepdims=True)
    grad_sq = jnp.sum(direction * direction, keepdims=True)
    grad_sq = grad_sq * (1.0 / copies)
    curvature = curvature * (1.0 / repeats)
    rows = 8 if last else chan_count * copies
    lane = lax.broadcasted_iota(jnp.int32, (rows, block // 2 if last else 128), 1)
    sums = jnp.where(lane == 0, grad_sq, jnp.where(lane == 1, curvature, 0.0))
    if last:
        base = current_ref[:, own_lanes(block)] + duals_ref[...]
        store_quarters((base, direction_out[:, own_lanes(block)]), sums, refs)
    else:
        sums_out[...] = sums


def curvature_part(geometry, counts, delays, coh, factors, gradient, shares, before, last):
    block, pairs, dumps, penalty, chan_count, stations = geometry
    update = before is not None
    field = shape(64, stations)
    if last is not None:
        outs = [field] + [shape(72, block // 2)] * 4
    else:
        outs = [field, field, shape(chan_count * (stations // block), 128)]
    inputs = [counts, delays, coh, *factors, gradient, *shares]
    if update:
        inputs += before
    if last is not None:
        inputs += last
    return pl.pallas_call(
        functools.partial(
            curvature_kernel, block, pairs, dumps, penalty, chan_count, update, last is not None
        ),
        name="curvature_part",
        out_shape=tuple(outs),
        in_specs=vmem_specs(len(inputs)),
        out_specs=tuple(vmem_specs(len(outs))),
        compiler_params=params(),
        cost_estimate=pl.CostEstimate(
            flops=2000000000, bytes_accessed=2000000, transcendentals=0
        ),
    )(*inputs)


def weigh_kernel(chan_count, *refs):
    *parts, out = refs
    scales = [solve_of(chan_count, offset) for offset in range(4)]
    for n in range(2):
        for k in range(4):
            at = 128 * n + 32 * k
            terms = [scales[o][k] * parts[o][32 * n : 32 * n + 32, :] for o in range(4)]
            out[at : at + 32, :] = sum_in_pairs(terms)
    out[256:, :] = sum_in_pairs([part[64:, :] for part in parts])


def sum_in_pairs(terms):
    return (terms[0] + terms[1]) + (terms[2] + terms[3])


def weigh(geometry, *parts):
    chan_count = geometry[4]
    return pl.pallas_call(
        functools.partial(weigh_kernel, chan_count),
        name="weigh",
        out_shape=shape(264, parts[0].shape[1]),
        in_specs=vmem_specs(4),
        out_specs=vmem_specs(1)[0],
        compiler_params=params(),
    )(*parts)


def combine_kernel(penalty, one, two, coeffs_out, alpha_out):
    total = one[...] + two[...]
    alpha = step_length(total[256:257, 0:1], total[256:257, 1:2], penalty)
    coeffs_out[...] = total[:128] - alpha * total[128:256]
    alpha_out[...] = jnp.broadcast_to(alpha, (8, 128))


def combine(geometry, one, two):
    penalty = geometry[3]
    return pl.pallas_call(
        functools.partial(combine_kernel, penalty),
        name="combine",
        out_shape=(shape(128, one.shape[1]), shape(8, 128)),
        in_specs=vmem_specs(2),
        out_specs=tuple(vmem_specs(2)),
        compiler_params=params(),
    )(one, two)


def last_step_kernel(block, alpha, current, direction, duals, gains_out, shifted_out):
    at_own = own_lanes(block)
    gains_new = current[:, at_own] - alpha[0:1, 0:1] * direction[:, at_own]
    gains_out[:, 0, :] = gains_new
    shifted_out[...] = gains_new + duals[...]


def last_step(geometry, *inputs):
    block = geometry[0]
    return pl.pallas_call(
        functools.partial(last_step_kernel, block),
        name="last_step",
        out_shape=(shape(64, 1, block), shape(64, block)),
        in_specs=vmem_specs(len(inputs)),
        out_specs=tuple(vmem_specs(2)),
        compiler_params=params(),
    )(*inputs)


def consensus_kernel(chan_count, own, core, row, both, shifted, coeffs_out, duals_out):
    place = lax.axis_index("chan")
    odd_core, odd_row = place % 2 == 1, (place // 2) % 2 == 1

    def joined(one, two, odd, axis):
        return jnp.concatenate([jnp.where(odd, two, one), jnp.where(odd, one, two)], axis=axis)

    fitted = None
    for k, scale in enumerate(basis_of(chan_count)):
        at = slice(32 * k, 32 * k + 32)
        coeffs = joined(
            joined(own[at, :], core[at, :], odd_core, 1),
            joined(row[at, :], both[at, :], odd_core, 1),
            odd_row,
            0,
        )
        coeffs_out[:, k, :] = coeffs
        fitted = scale * coeffs if fitted is None else fitted + scale * coeffs
    duals_out[:, 0, :] = shifted[...] - fitted


def consensus(geometry, *inputs):
    block, pairs, dumps, penalty, chan_count, stations = geometry
    return pl.pallas_call(
        functools.partial(consensus_kernel, chan_count),
        name="consensus",
        out_shape=(shape(64, 4, block), shape(64, 1, block)),
        in_specs=vmem_specs(len(inputs)),
        out_specs=tuple(vmem_specs(2)),
        compiler_params=params(),
    )(*inputs)


def swap(value, count, offset):
    return lax.ppermute(value, "chan", [(i, i ^ offset) for i in range(count)])


def other_stations(value):
    return lax.ppermute(value, "stn", [(0, 1), (1, 0)])


def both_stations(value, count):
    if count == 2:
        return value, other_stations(value)
    return jnp.zeros_like(value), lax.psum(value, "stn")


def shards(observed, pair_table, flag_rows, gains, duals, prior_coeffs, delays, brightness):
    stn_count = lax.axis_size("stn")
    chan_count = lax.axis_size("chan")
    entries, dirs, chan_local, block = gains.shape
    slots, dumps = observed.shape[0], observed.shape[2]
    stations = block * stn_count
    pairs = pair_lists(stn_count)
    penalty = stations * dumps / 16.0
    geometry = (block, pairs, dumps, penalty, chan_count, stations)

    observed = observed.reshape((slots,) + observed.shape[2:])
    duals_raw = duals.reshape(entries * dirs, 1, block)
    prior = prior_coeffs.reshape(entries * dirs, 4, block)
    rows = jnp.concatenate(
        [gains.reshape(entries * dirs, 1, block), delays.reshape(dumps * dirs, 1, block)]
    )
    ints = jnp.stack([pair_table, flag_rows])
    if stn_count == 2:
        fields = (rows, other_stations(rows))
        ints_other = other_stations(ints)
    else:
        fields = (lax.all_gather(rows, "stn", axis=2, tiled=True),)
        ints_other = lax.all_gather(ints, "stn", axis=1, tiled=True)
    duals_own, start, coh, counts = prepare(
        geometry, pair_table, flag_rows, duals_raw, prior, brightness
    )
    if stn_count != 2:
        counts = jnp.zeros_like(counts)
    data = functools.partial(data_part, geometry, pair_table, flag_rows, observed, coh)
    share, current, delay_all, counts = data(fields + (start, counts, ints_other))
    shares = both_stations(share, stn_count)

    step = before = None
    for iteration in range(ITERS):
        last = iteration + 1 == ITERS
        gradient, *rest = gradient_part(geometry, counts, delay_all, coh, current, step)
        if step is not None:
            current, alpha, *rest = rest
            before = (alpha, linear)
        direction, *rest = curvature_part(
            geometry,
            counts,
            delay_all,
            coh,
            rest,
            gradient,
            shares,
            before,
            (duals_own, current) if last else None,
        )
        if not last:
            linear, sums = rest
            sums = lax.all_to_all(sums, ("chan", "stn"), 0, 0, tiled=True)
            (share,) = data((direction, delay_all))
            shares = both_stations(share, stn_count)
            step = (sums, direction)

    quarters = rest[:1] + [swap(rest[o], chan_count, o) for o in (1, 2, 3)]
    value, bit = weigh(geometry, *quarters), 4
    other = swap(value, chan_count, bit)
    while 2 * bit < chan_count:
        value, bit = value + other, 2 * bit
        other = swap(value, chan_count, bit)
    quarter, alpha = combine(geometry, value, other)
    gains_new, shifted = last_step(geometry, alpha, current, direction, duals_own)
    quarters = [quarter] + [swap(quarter, chan_count, o) for o in (1, 2, 3)]
    coeffs, duals_new = consensus(geometry, *quarters, shifted)
    return (
        gains_new.reshape(gains.shape),
        coeffs.reshape(entries, dirs, 4, block),
        duals_new.reshape(gains.shape),
    )


def solution(mesh):
    return jax.shard_map(
        shards,
        mesh=mesh,
        in_specs=(
            P("stn", ("band", "chan"), None, None, None, None),
            P("stn"),
            P("stn"),
            P(None, None, ("band", "chan"), "stn"),
            P(None, None, ("band", "chan"), "stn"),
            P("band", None, None, "stn"),
            P(None, None, "stn"),
            P("band", None),
        ),
        out_specs=(
            P(None, None, ("band", "chan"), "stn"),
            P("band", None, None, "stn"),
            P(None, None, ("band", "chan"), "stn"),
        ),
        check_vma=False,
    )
```

```python
import functools
import math

import jax
import jax.numpy as jnp
import numpy as np
from jax import lax
from jax.experimental import pallas as pl
from jax.experimental.pallas import tpu as pltpu
from jax.sharding import PartitionSpec as P

ITERS = 3
EPSILON = 1e-06
SPECTRAL_INDEX = 0.7
DIRS = 8
CHUNK = 128
VMEM_BYTES = 24 * 1024 * 1024
COPY_BYTES = 48 * 1024 * 1024
AHEAD = 2
F32 = jnp.float32
BF16 = jnp.bfloat16

COSTLY = pl.CostEstimate(flops=20000000000, bytes_accessed=20000000, transcendentals=0)

NT = (((1,), (1,)), ((), ()))
NN = (((1,), (0,)), ((), ()))
TN = (((0,), (0,)), ((), ()))


def dot(lhs, rhs, dims):
    return lax.dot_general(lhs, rhs, dims, preferred_element_type=F32)


def pair_lists(station_blocks):
    return [(p, q) for p in range(station_blocks) for q in range(p, station_blocks)]


def bernstein_np(total_channels):
    position = (np.arange(total_channels, dtype=np.float64) + 0.5) / total_channels
    others = 1.0 - position
    return np.stack(
        [others**3, 3.0 * position * others**2, 3.0 * position**2 * others, position**3], axis=1
    )


def split(x):
    high = x.astype(BF16)
    return high, (x - high.astype(F32)).astype(BF16)


def pack(x):
    high, low = split(x)
    return jnp.concatenate([high, low], axis=0)


def trig(delay, freq):
    turns = delay * freq
    turns = turns - jnp.floor(turns + 0.5)
    x = turns * math.pi
    x2 = x * x
    sin_half = x * (
        1.0
        + x2
        * (
            -1.0 / 6
            + x2
            * (
                1.0 / 120
                + x2
                * (
                    -1.0 / 5040
                    + x2 * (1.0 / 362880 + x2 * (-1.0 / 39916800 + x2 * (1.0 / 6227020800)))
                )
            )
        )
    )
    cos_half = 1.0 + x2 * (
        -0.5
        + x2
        * (
            1.0 / 24
            + x2
            * (
                -1.0 / 720
                + x2
                * (
                    1.0 / 40320
                    + x2 * (-1.0 / 3628800 + x2 * (1.0 / 479001600 + x2 * (-1.0 / 87178291200)))
                )
            )
        )
    )
    return 1.0 - 2.0 * sin_half * sin_half, 2.0 * sin_half * cos_half


def rotate(field, cosine, sine):
    re = [field[8 * m : 8 * m + 8] for m in range(4)]
    im = [field[32 + 8 * m : 40 + 8 * m] for m in range(4)]
    return (
        [cosine * re[m] - sine * im[m] for m in range(4)],
        [cosine * im[m] + sine * re[m] for m in range(4)],
    )


def coherency_rows(coh, width):
    reps = width // coh.shape[1]
    rows = [jnp.concatenate([coh[8 * e : 8 * e + 8]] * reps, axis=1) for e in range(8)]
    return rows[:4], rows[4:]


def left_rows(rot, bright):
    (a_re, a_im), (c_re, c_im) = rot, bright
    out = []
    for i in range(2):
        re_rows, im_rows = [], []
        for l in range(2):
            re = im = None
            for k in range(2):
                ar, ai, cr, ci = a_re[2 * i + k], a_im[2 * i + k], c_re[2 * k + l], c_im[2 * k + l]
                tr, ti = ar * cr - ai * ci, ar * ci + ai * cr
                re, im = (tr, ti) if re is None else (re + tr, im + ti)
            re_rows.append(re)
            im_rows.append(im)
        out.append(jnp.concatenate(re_rows + im_rows, axis=0))
    return out


def right_rows(rot):
    a_re, a_im = rot
    real = [
        jnp.concatenate([a_re[2 * j], a_re[2 * j + 1], a_im[2 * j], a_im[2 * j + 1]], axis=0)
        for j in range(2)
    ]
    imag = [
        jnp.concatenate([-a_im[2 * j], -a_im[2 * j + 1], a_re[2 * j], a_re[2 * j + 1]], axis=0)
        for j in range(2)
    ]
    return real + imag


def field_gradient(h_left, h_right, bright, cosine, sine):
    c_re, c_im = bright
    g_re, g_im = [], []
    for i in range(2):
        for k in range(2):
            j = i
            re = h_right[j][8 * k : 8 * k + 8] + h_right[2 + j][16 + 8 * k : 24 + 8 * k]
            im = h_right[j][16 + 8 * k : 24 + 8 * k] - h_right[2 + j][8 * k : 8 * k + 8]
            for l in range(2):
                lr = h_left[i][8 * l : 8 * l + 8]
                li = h_left[i][16 + 8 * l : 24 + 8 * l]
                cr, ci = c_re[2 * k + l], c_im[2 * k + l]
                re = re + lr * cr + li * ci
                im = im + li * cr - lr * ci
            g_re.append(cosine * re + sine * im)
            g_im.append(cosine * im - sine * re)
    return jnp.concatenate(g_re + g_im, axis=0)


def coherency_tile(brightness, freq):
    spectral = jnp.exp(-SPECTRAL_INDEX * jnp.log(jnp.full((8, 128), freq, F32)))
    tiles = []
    for e in range(8):
        column = jnp.transpose(jnp.broadcast_to(brightness[e : e + 1, :], (8, 8)))[:, :1]
        tiles.append(column * spectral)
    return jnp.concatenate(tiles, axis=0)


def position_of(chan_count, offset=0):
    place = lax.axis_index("chan")
    if offset:
        place = place ^ offset
    return place.astype(F32) * (1.0 / chan_count)


def frequency_of(chan_count):
    return 1.0 + position_of(chan_count)


def basis_of(chan_count, offset=0):
    x = position_of(chan_count, offset) + 0.5 / chan_count
    y = 1.0 - x
    return [y * y * y, 3.0 * x * y * y, 3.0 * x * x * y, x * x * x]


def solve_of(chan_count, offset):
    basis = bernstein_np(chan_count)
    inverse = np.linalg.inv(basis.T @ basis)
    row = basis_of(chan_count, offset)
    return [sum(row[m] * float(inverse[m, k]) for m in range(4)) for k in range(4)]


def vmem_specs(count):
    return [pl.BlockSpec(memory_space=pltpu.VMEM)] * count


def smem_specs(count):
    return [pl.BlockSpec(memory_space=pltpu.SMEM)] * count


def params(limit=None):
    return pltpu.CompilerParams(vmem_limit_bytes=limit or VMEM_BYTES)


def shape(*dims, dtype=F32):
    return jax.ShapeDtypeStruct(dims, dtype)


def own_lanes(block):
    return pl.ds(pl.multiple_of(lax.axis_index("stn") * block, CHUNK), block)


def pair_blocks(pairs, pair):
    first, second = jnp.int32(0), jnp.int32(0)
    for k, (p, q) in enumerate(pairs):
        first = first + jnp.where(pair == k, p, 0)
        second = second + jnp.where(pair == k, q, 0)
    return first, second


def masks_kernel(masks):
    block = masks.shape[1]
    row = lax.broadcasted_iota(jnp.int32, (block, block), 0)
    col = lax.broadcasted_iota(jnp.int32, (block, block), 1)
    masks[0] = (row < col).astype(F32).astype(BF16)
    masks[1] = jnp.ones((block, block), BF16)


def baseline_masks(block):
    return pl.pallas_call(
        masks_kernel,
        name="baseline_masks",
        out_shape=shape(2, block, block, dtype=BF16),
        out_specs=vmem_specs(1)[0],
        compiler_params=params(),
        cost_estimate=COSTLY,
    )()


def rows_kernel(masks, gains, delays, ids, flags, rows):
    fields, stations = gains.shape[0] + delays.shape[0], gains.shape[2]
    rows[: gains.shape[0]] = gains[...]
    rows[gains.shape[0] : fields] = delays[...].reshape(delays.shape[0], 1, stations)
    rows[fields:] = jnp.full((2, 1, stations), -1.0, F32)
    slots = ids.shape[1]
    rows[fields, :, :slots] = ids[...].astype(F32)
    rows[fields + 1, :, :slots] = flags[...].astype(F32)


def field_rows(masks, gains, delays, ids, flags):
    return pl.pallas_call(
        rows_kernel,
        name="field_rows",
        out_shape=shape(gains.shape[0] + delays.shape[0] + 2, 1, gains.shape[2]),
        in_specs=vmem_specs(5),
        out_specs=vmem_specs(1)[0],
        compiler_params=params(),
        cost_estimate=COSTLY,
    )(masks, gains, delays, ids, flags)


def prepare_kernel(block, pairs, slots, penalty, chan_count, *refs):
    table, flags, duals, prior, bright, *refs = refs
    duals_out, start_out, coh_out, counts_out = refs
    lane = lax.broadcasted_iota(jnp.int32, (8, 128), 1)
    counts = jnp.zeros((8, 128), F32)
    for slot in range(slots):
        held_here = (lane == table[slot]) & (lane < len(pairs))
        counts = counts + jnp.where(held_here, flags[slot].astype(F32), 0.0)
    counts_out[...] = counts
    coh_out[...] = coherency_tile(bright[...], frequency_of(chan_count))
    duals_own = duals[:, 0, :]
    duals_out[...] = duals_own
    target = -duals_own
    for k, scale in enumerate(basis_of(chan_count)):
        target = target + scale * prior[:, k, :]
    start_out[...] = -penalty * target


def prepare(geometry, table, flags, duals, prior, brightness):
    block, pairs, dumps, penalty, chan_count, stations = geometry
    return pl.pallas_call(
        functools.partial(
            prepare_kernel, block, pairs, table.shape[0], penalty, chan_count
        ),
        name="prepare",
        out_shape=(
            shape(64, block),
            shape(64, block),
            shape(64, 128),
            shape(8, 128),
        ),
        in_specs=smem_specs(2) + vmem_specs(3),
        out_specs=tuple(vmem_specs(4)),
        compiler_params=params(),
        cost_estimate=pl.CostEstimate(flops=1000000, bytes_accessed=2000000, transcendentals=0),
    )(table, flags, duals, prior, brightness)


def data_kernel(block, pairs, dumps, slots, penalty, chan_count, first_call, joined, *refs):
    table, flags, observed, coh_ref, keep, *refs = refs
    if first_call:
        if joined:
            rows_all, *refs = refs
        else:
            rows_mine, rows_other, *refs = refs
        start, counts_mine, out_ref, field_ref, delay_ref, counts_ref, *refs = refs
    else:
        field_ref, delay_ref, out_ref, *refs = refs
    if first_call:
        order, xp, yp, hl, ha = refs
    else:
        held, sems, order, xp, yp, hl, ha = refs
    stations = field_ref.shape[1]
    pair_count = len(pairs)
    at_own = own_lanes(block)

    live_count = jnp.int32(0)
    for slot in range(slots):
        order[live_count] = jnp.int32(slot)
        live_count = live_count + jnp.where(table[slot] < pair_count, 1, 0)
    items = live_count * dumps

    def copy_of(item):
        slot, t = order[item // dumps], item % dumps
        return pltpu.make_async_copy(observed.at[slot, t], held.at[item], sems.at[item])

    if not first_call:
        for item in range(min(AHEAD, slots * dumps)):

            @pl.when(item < items)
            def _():
                copy_of(jnp.int32(item)).start()

    freq_value = frequency_of(chan_count)
    if first_call:
        if joined:
            rows_other = rows_all
            field_ref[...] = rows_all[:64, 0, :]
            delay_ref[...] = rows_all[64 : 64 + 8 * dumps, 0, :]
        else:
            at_other = pl.ds(pl.multiple_of((1 - lax.axis_index("stn")) * block, CHUNK), block)
            for at, rows in ((at_own, rows_mine), (at_other, rows_other)):
                field_ref[:, at] = rows[:64, 0, :]
                delay_ref[:, at] = rows[64 : 64 + 8 * dumps, 0, :]
    bright = coherency_rows(coh_ref[...], stations)
    for t in range(dumps):
        cosine, sine = trig(delay_ref[8 * t : 8 * t + 8, :], freq_value)
        rot = rotate(field_ref[...], cosine, sine)
        for i, rows in enumerate(left_rows(rot, bright)):
            xp[t, i] = pack(rows)
        for rj, rows in enumerate(right_rows(rot)):
            yp[t, rj] = pack(rows)
    hl[...] = jnp.zeros_like(hl)
    ha[...] = jnp.zeros_like(ha)

    lane = lax.broadcasted_iota(jnp.int32, (1, block), 1)

    def visit(item, unused):
        slot, t = order[item // dumps], item % dumps
        first, second = pair_blocks(pairs, table[slot])
        kept = keep[jnp.where(first < second, 1, 0)]
        live = (lane >= flags[slot]).astype(F32)
        live16 = live.astype(BF16)
        at_p = pl.ds(pl.multiple_of(first * block, CHUNK), block)
        at_q = pl.ds(pl.multiple_of(second * block, CHUNK), block)
        if not first_call:
            copy_of(item).wait()

            @pl.when(item + AHEAD < items)
            def _():
                copy_of(item + AHEAD).start()

        acc_left = [None, None]
        acc_right = [None] * 4
        xs = [xp[t, i, :, at_p] * live16 for i in range(2)]
        ys = [yp[t, rj, :, at_q] for rj in range(4)]
        for r in range(2):
            for i in range(2):
                for j in range(2):
                    m = 4 * r + 2 * i + j
                    tile = observed[slot, t, m] if first_call else held[item, m]
                    tile = tile * kept
                    rj = 2 * r + j
                    left = dot(ys[rj], tile, NT)
                    right = dot(xs[i], tile, NN)
                    acc_left[i] = left if acc_left[i] is None else acc_left[i] + left
                    acc_right[rj] = right if acc_right[rj] is None else acc_right[rj] + right
        for i in range(2):
            hl[t, i, :, at_p] += (acc_left[i][:32] + acc_left[i][32:]) * live
        for rj in range(4):
            ha[t, rj, :, at_q] += acc_right[rj][:32] + acc_right[rj][32:]
        return unused

    lax.fori_loop(0, items, visit, jnp.int32(0))

    total = None
    for t in range(dumps):
        cosine, sine = trig(delay_ref[8 * t : 8 * t + 8, :], freq_value)
        piece = field_gradient(
            [hl[t, i] for i in range(2)], [ha[t, rj] for rj in range(4)], bright, cosine, sine
        )
        total = piece if total is None else total + piece
    out_ref[...] = -total
    prior = penalty * field_ref[:, at_own]
    if first_call:
        prior = prior + start[...]
        counts = counts_mine[...]
        ids_other, flags_other = rows_other[64 + 8 * dumps], rows_other[65 + 8 * dumps]
        pair_lane = lax.broadcasted_iota(jnp.int32, (8, 128), 1)
        for k in range(pair_count):
            theirs = jnp.where(ids_other == float(k), flags_other, 0.0)
            total_flags = jnp.sum(theirs, axis=1, keepdims=True)
            counts = counts + jnp.where(pair_lane == k, total_flags, 0.0)
        counts_ref[...] = counts
    out_ref[:, at_own] += prior


def data_part(geometry, table, flags, observed, coh, masks, fields):
    block, pairs, dumps, penalty, chan_count, stations = geometry
    slots = observed.shape[0]
    first_call = len(fields) > 2
    joined = len(fields) == 3
    body = functools.partial(
        data_kernel, block, pairs, dumps, slots, penalty, chan_count, first_call, joined
    )
    shapes = [shape(64, stations)]
    if first_call:
        shapes += [shape(64, stations), shape(8 * dumps, stations), shape(8, 128)]
        place, copies = vmem_specs(1), []
    else:
        place = [pl.BlockSpec(memory_space=pl.ANY)]
        copies = [
            pltpu.VMEM((slots * dumps,) + observed.shape[2:], BF16),
            pltpu.SemaphoreType.DMA((slots * dumps,)),
        ]
    return pl.pallas_call(
        body,
        name="data_part",
        out_shape=tuple(shapes),
        in_specs=smem_specs(2) + place + vmem_specs(2 + len(fields)),
        out_specs=tuple(vmem_specs(len(shapes))),
        scratch_shapes=copies
        + [
            pltpu.SMEM((slots,), jnp.int32),
            pltpu.VMEM((dumps, 2, 64, stations), BF16),
            pltpu.VMEM((dumps, 4, 64, stations), BF16),
            pltpu.VMEM((dumps, 2, 32, stations), F32),
            pltpu.VMEM((dumps, 4, 32, stations), F32),
        ],
        compiler_params=params() if first_call else params(COPY_BYTES),
        cost_estimate=pl.CostEstimate(
            flops=6000000000, bytes_accessed=8000000, transcendentals=0
        ),
    )(table, flags, observed, coh, masks, *fields)


def fold_gram(high_low, other, rows):
    wide = dot(high_low, other[:rows], NT)
    return wide[:rows] + wide[rows:] + dot(high_low[:rows], other[rows:], NT)


def apply_gram(gram, packed, rows):
    size = gram.shape[0]
    both = pack(gram)
    wide = dot(both, packed[:rows], NN)
    return wide[:size] + wide[size:] + dot(both[:size], packed[rows:], NN)


def lanes(parts, start, size):
    return jnp.concatenate([part[:, start : start + size] for part in parts], axis=1)


def twice(mask):
    return jnp.concatenate([mask, mask], axis=1)


class Chunks:
    def __init__(self, block, stations, pairs, counts):
        self.block = block
        self.size = min(CHUNK, block)
        self.per_block = block // self.size
        self.count = stations // self.size
        self.blocks = stations // block
        lane = lax.broadcasted_iota(jnp.int32, (1, block), 1).astype(F32)
        self.masks = {
            pair: (lane >= counts[:, k : k + 1]).astype(F32) for k, pair in enumerate(pairs)
        }
        row = lax.broadcasted_iota(jnp.int32, (2 * self.size, 4 * self.size), 0) % self.size
        col = lax.broadcasted_iota(jnp.int32, (2 * self.size, 4 * self.size), 1) % self.size
        self.upper = row < col

    def mask(self, pair, chunk):
        start = (chunk % self.per_block) * self.size
        return twice(self.masks[pair][:, start : start + self.size])

    def own_pair(self, chunk):
        return (chunk // self.per_block, chunk // self.per_block)

    def rect_terms(self, chunk):
        own = chunk // self.per_block
        terms = []
        inside = list(range(chunk + 1, (own + 1) * self.per_block))
        if inside:
            terms.append(((own, own), inside))
        for q in range(own + 1, self.blocks):
            terms.append(((own, q), list(range(q * self.per_block, (q + 1) * self.per_block))))
        return terms


def sum_of(parts):
    total = parts[0]
    for part in parts[1:]:
        total = total + part
    return total


def halves(rows, axis, odd):
    size = rows.shape[axis] // 2
    low = lax.slice_in_dim(rows, 0, size, axis=axis)
    high = lax.slice_in_dim(rows, size, 2 * size, axis=axis)
    return jnp.where(odd, high, low), jnp.where(odd, low, high)


def store_quarters(fields, sums, outs):
    place = lax.axis_index("chan")
    odd_lanes, odd_rows = place % 2 == 1, (place // 2) % 2 == 1
    for n, field in enumerate(fields):
        for o, part in enumerate(halves(field, 1, odd_lanes)):
            for p, quarter in enumerate(halves(part, 0, odd_rows)):
                outs[o + 2 * p][32 * n : 32 * n + 32, :] = quarter
    for out in outs:
        out[32 * len(fields) :, :] = sums


def step_length(grad_sq, curvature, penalty):
    return grad_sq / (curvature + penalty * grad_sq + EPSILON)


def gradient_kernel(block, pairs, dumps, penalty, chan_count, update, *refs):
    counts_ref, delay_ref, coh_ref, current_ref, *refs = refs
    if update:
        sums_ref, direction_ref, *refs = refs
    gradient_out, *refs = refs
    if update:
        current_out, alpha_out, *refs = refs
    xp, yp, hl, ha = refs
    stations = current_ref.shape[1]
    chunks = Chunks(block, stations, pairs, counts_ref[0:1, :])
    size = chunks.size

    current = current_ref[...]
    if update:
        sums = jnp.sum(sums_ref[...], axis=0, keepdims=True)
        alpha = step_length(sums[:, 0:1], sums[:, 1:2], penalty)
        alpha_out[...] = jnp.broadcast_to(alpha, (8, 128))
        current = current - alpha * direction_ref[...]
        current_out[...] = current
    freq_value = frequency_of(chan_count)
    bright = coherency_rows(coh_ref[...], stations)
    gradient = None
    for t in range(dumps):
        cosine, sine = trig(delay_ref[8 * t : 8 * t + 8, :], freq_value)
        rot = rotate(current, cosine, sine)
        xs = [pack(v) for v in left_rows(rot, bright)]
        ys = [pack(v) for v in right_rows(rot)]
        for i in range(2):
            xp[t, i] = xs[i]
        for rj in range(4):
            yp[t, rj] = ys[rj]
        gram_y = [
            fold_gram(lanes(ys, c * size, size), lanes(ys, c * size, size), 32)
            for c in range(chunks.count)
        ]
        sums_x = [None] * chunks.count
        for c in range(chunks.count):
            xc = lanes(xs, c * size, size)
            yc = lanes(ys, c * size, size)
            xw = xc * chunks.mask(chunks.own_pair(c), c).astype(BF16)
            yn = jnp.concatenate([yc[:32], yc[:32], yc[32:], yc[32:]], axis=0)
            model = dot(jnp.concatenate([xw, xw], axis=0), yn, TN)
            model = jnp.where(chunks.upper, model, 0.0)
            high, low = split(model)
            left = dot(yc, high, NT) + dot(yc, low, NT)
            right = dot(xw, high, NN) + dot(xw, low, NN)
            left = left[:32] + left[32:]
            right = right[:32] + right[32:]
            for pair, others in chunks.rect_terms(c):
                mask = chunks.mask(pair, c)
                left = left + apply_gram(sum_of([gram_y[o] for o in others]), xc, 32) * mask
                gram_x = fold_gram(xc * mask.astype(BF16), xc, 32)
                for o in others:
                    sums_x[o] = gram_x if sums_x[o] is None else sums_x[o] + gram_x
            if sums_x[c] is not None:
                right = right + apply_gram(sums_x[c], yc, 32)
            for i in range(2):
                hl[i, :, c * size : (c + 1) * size] = left[:, i * size : (i + 1) * size]
            for rj in range(4):
                ha[rj, :, c * size : (c + 1) * size] = right[:, rj * size : (rj + 1) * size]
        piece = field_gradient(
            [hl[i] for i in range(2)], [ha[rj] for rj in range(4)], bright, cosine, sine
        )
        gradient = piece if gradient is None else gradient + piece
    gradient_out[...] = gradient


def gradient_part(geometry, counts, delays, coh, current, step):
    block, pairs, dumps, penalty, chan_count, stations = geometry
    update = step is not None
    field = shape(64, stations)
    outs = [field]
    inputs = [counts, delays, coh, current]
    if update:
        inputs += step
        outs += [field, shape(8, 128)]
    outs += [shape(dumps, rows, 64, stations, dtype=BF16) for rows in (2, 4)]
    return pl.pallas_call(
        functools.partial(gradient_kernel, block, pairs, dumps, penalty, chan_count, update),
        name="gradient_part",
        out_shape=tuple(outs),
        in_specs=vmem_specs(len(inputs)),
        out_specs=tuple(vmem_specs(len(outs))),
        scratch_shapes=[pltpu.VMEM((2, 32, stations), F32), pltpu.VMEM((4, 32, stations), F32)],
        compiler_params=params(),
        cost_estimate=pl.CostEstimate(
            flops=4000000000, bytes_accessed=2000000, transcendentals=0
        ),
    )(*inputs)


def curvature_kernel(block, pairs, dumps, penalty, chan_count, update, last, *refs):
    counts_ref, delay_ref, coh_ref, xp, yp, gradient_ref, mine_ref, theirs_ref, *refs = refs
    if update:
        alpha_ref, linear_ref, *refs = refs
    if last:
        duals_ref, current_ref, *refs = refs
    direction_out, *refs = refs
    if not last:
        linear_out, sums_out = refs
    stations = mine_ref.shape[1]
    chunks = Chunks(block, stations, pairs, counts_ref[0:1, :])
    size = chunks.size

    linear = mine_ref[...] + theirs_ref[...]
    if update:
        linear = linear_ref[...] - alpha_ref[0:1, 0:1] * linear
    direction = linear + gradient_ref[...]
    direction_out[...] = direction
    if not last:
        linear_out[...] = linear

    freq_value = frequency_of(chan_count)
    bright = coherency_rows(coh_ref[...], stations)
    squares = jnp.zeros((8, 4 * size), F32)
    grams = jnp.zeros((64, 64), F32)
    if last:
        visited, repeats, copies = range(dumps), 1, 1
    else:
        stn_count = stations // block
        shared = stn_count % dumps == 0
        visited = [lax.axis_index("stn") % dumps] if shared else range(dumps)
        repeats, copies = (stn_count // dumps if shared else stn_count), stn_count
    for t in visited:
        delay = delay_ref[pl.ds(pl.multiple_of(8 * t, 8), 8), :]
        cosine, sine = trig(delay, freq_value)
        step = rotate(direction, cosine, sine)
        xs = [xp[t, i] for i in range(2)]
        ys = [yp[t, rj] for rj in range(4)]
        dxs = [pack(v) for v in left_rows(step, bright)]
        dys = [pack(v) for v in right_rows(step)]

        def stacked(first, second, c):
            one = lanes(first, c * size, size)
            two = lanes(second, c * size, size)
            return jnp.concatenate([one[:32], two[:32], one[32:], two[32:]], axis=0)

        gram_y = [None] * chunks.count
        for c in range(chunks.count):
            xc = stacked(dxs, xs, c)
            yc = stacked(ys, dys, c)
            xw = xc * chunks.mask(chunks.own_pair(c), c).astype(BF16)
            tangent = dot(
                jnp.concatenate([xw, xw], axis=0),
                jnp.concatenate([yc[:64], yc[:64], yc[64:], yc[64:]], axis=0),
                TN,
            )
            tangent = jnp.where(chunks.upper, tangent, 0.0)
            square = tangent * tangent
            squares = squares + jnp.sum(square.reshape(2 * size // 8, 8, 4 * size), axis=0)
            if c > 0:
                gram_y[c] = fold_gram(yc, yc, 64)
        for c in range(chunks.count):
            for pair, others in chunks.rect_terms(c):
                xc = stacked(dxs, xs, c)
                gram_x = fold_gram(xc * chunks.mask(pair, c).astype(BF16), xc, 64)
                grams = grams + sum_of([gram_y[o] for o in others]) * gram_x
    curvature = jnp.sum(squares, keepdims=True) + jnp.sum(grams, keepdims=True)
    grad_sq = jnp.sum(direction * direction, keepdims=True)
    grad_sq = grad_sq * (1.0 / copies)
    curvature = curvature * (1.0 / repeats)
    rows = 8 if last else chan_count * copies
    lane = lax.broadcasted_iota(jnp.int32, (rows, block // 2 if last else 128), 1)
    sums = jnp.where(lane == 0, grad_sq, jnp.where(lane == 1, curvature, 0.0))
    if last:
        base = current_ref[:, own_lanes(block)] + duals_ref[...]
        store_quarters((base, direction_out[:, own_lanes(block)]), sums, refs)
    else:
        sums_out[...] = sums


def curvature_part(geometry, counts, delays, coh, factors, gradient, shares, before, last):
    block, pairs, dumps, penalty, chan_count, stations = geometry
    update = before is not None
    field = shape(64, stations)
    if last is not None:
        outs = [field] + [shape(72, block // 2)] * 4
    else:
        outs = [field, field, shape(chan_count * (stations // block), 128)]
    inputs = [counts, delays, coh, *factors, gradient, *shares]
    if update:
        inputs += before
    if last is not None:
        inputs += last
    return pl.pallas_call(
        functools.partial(
            curvature_kernel, block, pairs, dumps, penalty, chan_count, update, last is not None
        ),
        name="curvature_part",
        out_shape=tuple(outs),
        in_specs=vmem_specs(len(inputs)),
        out_specs=tuple(vmem_specs(len(outs))),
        compiler_params=params(),
        cost_estimate=pl.CostEstimate(
            flops=2000000000, bytes_accessed=2000000, transcendentals=0
        ),
    )(*inputs)


def weigh_kernel(chan_count, *refs):
    *parts, out = refs
    scales = [solve_of(chan_count, offset) for offset in range(4)]
    for n in range(2):
        for k in range(4):
            at = 128 * n + 32 * k
            terms = [scales[o][k] * parts[o][32 * n : 32 * n + 32, :] for o in range(4)]
            out[at : at + 32, :] = sum_in_pairs(terms)
    out[256:, :] = sum_in_pairs([part[64:, :] for part in parts])


def sum_in_pairs(terms):
    return (terms[0] + terms[1]) + (terms[2] + terms[3])


def weigh(geometry, *parts):
    chan_count = geometry[4]
    return pl.pallas_call(
        functools.partial(weigh_kernel, chan_count),
        name="weigh",
        out_shape=shape(264, parts[0].shape[1]),
        in_specs=vmem_specs(4),
        out_specs=vmem_specs(1)[0],
        compiler_params=params(),
    )(*parts)


def combine_kernel(penalty, one, two, coeffs_out, alpha_out):
    total = one[...] + two[...]
    alpha = step_length(total[256:257, 0:1], total[256:257, 1:2], penalty)
    coeffs_out[...] = total[:128] - alpha * total[128:256]
    alpha_out[...] = jnp.broadcast_to(alpha, (8, 128))


def combine(geometry, one, two):
    penalty = geometry[3]
    return pl.pallas_call(
        functools.partial(combine_kernel, penalty),
        name="combine",
        out_shape=(shape(128, one.shape[1]), shape(8, 128)),
        in_specs=vmem_specs(2),
        out_specs=tuple(vmem_specs(2)),
        compiler_params=params(),
    )(one, two)


def last_step_kernel(block, alpha, current, direction, duals, gains_out, shifted_out):
    at_own = own_lanes(block)
    gains_new = current[:, at_own] - alpha[0:1, 0:1] * direction[:, at_own]
    gains_out[:, 0, :] = gains_new
    shifted_out[...] = gains_new + duals[...]


def last_step(geometry, *inputs):
    block = geometry[0]
    return pl.pallas_call(
        functools.partial(last_step_kernel, block),
        name="last_step",
        out_shape=(shape(64, 1, block), shape(64, block)),
        in_specs=vmem_specs(len(inputs)),
        out_specs=tuple(vmem_specs(2)),
        compiler_params=params(),
    )(*inputs)


def consensus_kernel(chan_count, own, core, row, both, shifted, coeffs_out, duals_out):
    place = lax.axis_index("chan")
    odd_core, odd_row = place % 2 == 1, (place // 2) % 2 == 1

    def joined(one, two, odd, axis):
        return jnp.concatenate([jnp.where(odd, two, one), jnp.where(odd, one, two)], axis=axis)

    fitted = None
    for k, scale in enumerate(basis_of(chan_count)):
        at = slice(32 * k, 32 * k + 32)
        coeffs = joined(
            joined(own[at, :], core[at, :], odd_core, 1),
            joined(row[at, :], both[at, :], odd_core, 1),
            odd_row,
            0,
        )
        coeffs_out[:, k, :] = coeffs
        fitted = scale * coeffs if fitted is None else fitted + scale * coeffs
    duals_out[:, 0, :] = shifted[...] - fitted


def consensus(geometry, *inputs):
    block, pairs, dumps, penalty, chan_count, stations = geometry
    return pl.pallas_call(
        functools.partial(consensus_kernel, chan_count),
        name="consensus",
        out_shape=(shape(64, 4, block), shape(64, 1, block)),
        in_specs=vmem_specs(len(inputs)),
        out_specs=tuple(vmem_specs(2)),
        compiler_params=params(),
    )(*inputs)


def swap(value, count, offset):
    return lax.ppermute(value, "chan", [(i, i ^ offset) for i in range(count)])


def other_stations(value):
    return lax.ppermute(value, "stn", [(0, 1), (1, 0)])


def both_stations(value, count):
    if count == 2:
        return value, other_stations(value)
    return jnp.zeros_like(value), lax.psum(value, "stn")


def shards(observed, pair_table, flag_rows, gains, duals, prior_coeffs, delays, brightness):
    stn_count = lax.axis_size("stn")
    chan_count = lax.axis_size("chan")
    entries, dirs, chan_local, block = gains.shape
    slots, dumps = observed.shape[0], observed.shape[2]
    stations = block * stn_count
    pairs = pair_lists(stn_count)
    penalty = stations * dumps / 16.0
    geometry = (block, pairs, dumps, penalty, chan_count, stations)

    observed = observed.reshape((slots,) + observed.shape[2:])
    duals_raw = duals.reshape(entries * dirs, 1, block)
    prior = prior_coeffs.reshape(entries * dirs, 4, block)
    masks = baseline_masks(block)
    rows = field_rows(
        masks,
        gains.reshape(entries * dirs, 1, block),
        delays.reshape(dumps * dirs, block),
        pair_table.reshape(1, slots),
        flag_rows.reshape(1, slots),
    )
    if stn_count == 2:
        fields = (rows, other_stations(rows))
    else:
        fields = (lax.all_gather(rows, "stn", axis=2, tiled=True),)
    duals_own, start, coh, counts = prepare(
        geometry, pair_table, flag_rows, duals_raw, prior, brightness
    )
    if stn_count != 2:
        counts = jnp.zeros_like(counts)
    data = functools.partial(data_part, geometry, pair_table, flag_rows, observed, coh, masks)
    share, current, delay_all, counts = data(fields + (start, counts))
    shares = both_stations(share, stn_count)

    step = before = None
    for iteration in range(ITERS):
        last = iteration + 1 == ITERS
        gradient, *rest = gradient_part(geometry, counts, delay_all, coh, current, step)
        if step is not None:
            current, alpha, *rest = rest
            before = (alpha, linear)
        direction, *rest = curvature_part(
            geometry,
            counts,
            delay_all,
            coh,
            rest,
            gradient,
            shares,
            before,
            (duals_own, current) if last else None,
        )
        if not last:
            linear, sums = rest
            sums = lax.all_to_all(sums, ("chan", "stn"), 0, 0, tiled=True)
            (share,) = data((direction, delay_all))
            shares = both_stations(share, stn_count)
            step = (sums, direction)

    quarters = rest[:1] + [swap(rest[o], chan_count, o) for o in (1, 2, 3)]
    value, bit = weigh(geometry, *quarters), 4
    other = swap(value, chan_count, bit)
    while 2 * bit < chan_count:
        value, bit = value + other, 2 * bit
        other = swap(value, chan_count, bit)
    quarter, alpha = combine(geometry, value, other)
    gains_new, shifted = last_step(geometry, alpha, current, direction, duals_own)
    quarters = [quarter] + [swap(quarter, chan_count, o) for o in (1, 2, 3)]
    coeffs, duals_new = consensus(geometry, *quarters, shifted)
    return (
        gains_new.reshape(gains.shape),
        coeffs.reshape(entries, dirs, 4, block),
        duals_new.reshape(gains.shape),
    )


def solution(mesh):
    return jax.shard_map(
        shards,
        mesh=mesh,
        in_specs=(
            P("stn", ("band", "chan"), None, None, None, None),
            P("stn"),
            P("stn"),
            P(None, None, ("band", "chan"), "stn"),
            P(None, None, ("band", "chan"), "stn"),
            P("band", None, None, "stn"),
            P(None, None, "stn"),
            P("band", None),
        ),
        out_specs=(
            P(None, None, ("band", "chan"), "stn"),
            P("band", None, None, "stn"),
            P(None, None, ("band", "chan"), "stn"),
        ),
        check_vma=False,
    )
```

```python
import functools
import math

import jax
import jax.numpy as jnp
import numpy as np
from jax import lax
from jax.experimental import pallas as pl
from jax.experimental.pallas import tpu as pltpu
from jax.sharding import PartitionSpec as P

ITERS = 3
EPSILON = 1e-06
SPECTRAL_INDEX = 0.7
DIRS = 8
CHUNK = 128
VMEM_BYTES = 24 * 1024 * 1024
COPY_BYTES = 48 * 1024 * 1024
AHEAD = 2
F32 = jnp.float32
BF16 = jnp.bfloat16

COSTLY = pl.CostEstimate(flops=20000000000, bytes_accessed=20000000, transcendentals=0)

NT = (((1,), (1,)), ((), ()))
NN = (((1,), (0,)), ((), ()))
TN = (((0,), (0,)), ((), ()))


def dot(lhs, rhs, dims):
    return lax.dot_general(lhs, rhs, dims, preferred_element_type=F32)


def pair_lists(station_blocks):
    return [(p, q) for p in range(station_blocks) for q in range(p, station_blocks)]


def bernstein_np(total_channels):
    position = (np.arange(total_channels, dtype=np.float64) + 0.5) / total_channels
    others = 1.0 - position
    return np.stack(
        [others**3, 3.0 * position * others**2, 3.0 * position**2 * others, position**3], axis=1
    )


def split(x):
    high = x.astype(BF16)
    return high, (x - high.astype(F32)).astype(BF16)


def pack(x):
    high, low = split(x)
    return jnp.concatenate([high, low], axis=0)


def trig(delay, freq):
    turns = delay * freq
    turns = turns - jnp.floor(turns + 0.5)
    x = turns * math.pi
    x2 = x * x
    sin_half = x * (
        1.0
        + x2
        * (
            -1.0 / 6
            + x2
            * (
                1.0 / 120
                + x2
                * (
                    -1.0 / 5040
                    + x2 * (1.0 / 362880 + x2 * (-1.0 / 39916800 + x2 * (1.0 / 6227020800)))
                )
            )
        )
    )
    cos_half = 1.0 + x2 * (
        -0.5
        + x2
        * (
            1.0 / 24
            + x2
            * (
                -1.0 / 720
                + x2
                * (
                    1.0 / 40320
                    + x2 * (-1.0 / 3628800 + x2 * (1.0 / 479001600 + x2 * (-1.0 / 87178291200)))
                )
            )
        )
    )
    return 1.0 - 2.0 * sin_half * sin_half, 2.0 * sin_half * cos_half


def rotate(field, cosine, sine):
    re = [field[8 * m : 8 * m + 8] for m in range(4)]
    im = [field[32 + 8 * m : 40 + 8 * m] for m in range(4)]
    return (
        [cosine * re[m] - sine * im[m] for m in range(4)],
        [cosine * im[m] + sine * re[m] for m in range(4)],
    )


def coherency_rows(coh, width):
    reps = width // coh.shape[1]
    rows = [jnp.concatenate([coh[8 * e : 8 * e + 8]] * reps, axis=1) for e in range(8)]
    return rows[:4], rows[4:]


def left_rows(rot, bright):
    (a_re, a_im), (c_re, c_im) = rot, bright
    out = []
    for i in range(2):
        re_rows, im_rows = [], []
        for l in range(2):
            re = im = None
            for k in range(2):
                ar, ai, cr, ci = a_re[2 * i + k], a_im[2 * i + k], c_re[2 * k + l], c_im[2 * k + l]
                tr, ti = ar * cr - ai * ci, ar * ci + ai * cr
                re, im = (tr, ti) if re is None else (re + tr, im + ti)
            re_rows.append(re)
            im_rows.append(im)
        out.append(jnp.concatenate(re_rows + im_rows, axis=0))
    return out


def right_rows(rot):
    a_re, a_im = rot
    real = [
        jnp.concatenate([a_re[2 * j], a_re[2 * j + 1], a_im[2 * j], a_im[2 * j + 1]], axis=0)
        for j in range(2)
    ]
    imag = [
        jnp.concatenate([-a_im[2 * j], -a_im[2 * j + 1], a_re[2 * j], a_re[2 * j + 1]], axis=0)
        for j in range(2)
    ]
    return real + imag


def field_gradient(h_left, h_right, bright, cosine, sine):
    c_re, c_im = bright
    g_re, g_im = [], []
    for i in range(2):
        for k in range(2):
            j = i
            re = h_right[j][8 * k : 8 * k + 8] + h_right[2 + j][16 + 8 * k : 24 + 8 * k]
            im = h_right[j][16 + 8 * k : 24 + 8 * k] - h_right[2 + j][8 * k : 8 * k + 8]
            for l in range(2):
                lr = h_left[i][8 * l : 8 * l + 8]
                li = h_left[i][16 + 8 * l : 24 + 8 * l]
                cr, ci = c_re[2 * k + l], c_im[2 * k + l]
                re = re + lr * cr + li * ci
                im = im + li * cr - lr * ci
            g_re.append(cosine * re + sine * im)
            g_im.append(cosine * im - sine * re)
    return jnp.concatenate(g_re + g_im, axis=0)


def coherency_tile(brightness, freq):
    spectral = jnp.exp(-SPECTRAL_INDEX * jnp.log(jnp.full((8, 128), freq, F32)))
    tiles = []
    for e in range(8):
        column = jnp.transpose(jnp.broadcast_to(brightness[e : e + 1, :], (8, 8)))[:, :1]
        tiles.append(column * spectral)
    return jnp.concatenate(tiles, axis=0)


def position_of(chan_count, offset=0):
    place = lax.axis_index("chan")
    if offset:
        place = place ^ offset
    return place.astype(F32) * (1.0 / chan_count)


def frequency_of(chan_count):
    return 1.0 + position_of(chan_count)


def basis_of(chan_count, offset=0):
    x = position_of(chan_count, offset) + 0.5 / chan_count
    y = 1.0 - x
    return [y * y * y, 3.0 * x * y * y, 3.0 * x * x * y, x * x * x]


def solve_of(chan_count, offset):
    basis = bernstein_np(chan_count)
    inverse = np.linalg.inv(basis.T @ basis)
    row = basis_of(chan_count, offset)
    return [sum(row[m] * float(inverse[m, k]) for m in range(4)) for k in range(4)]


def vmem_specs(count):
    return [pl.BlockSpec(memory_space=pltpu.VMEM)] * count


def smem_specs(count):
    return [pl.BlockSpec(memory_space=pltpu.SMEM)] * count


def params(limit=None):
    return pltpu.CompilerParams(vmem_limit_bytes=limit or VMEM_BYTES)


def shape(*dims, dtype=F32):
    return jax.ShapeDtypeStruct(dims, dtype)


def own_lanes(block):
    return pl.ds(pl.multiple_of(lax.axis_index("stn") * block, CHUNK), block)


def pair_blocks(pairs, pair):
    first, second = jnp.int32(0), jnp.int32(0)
    for k, (p, q) in enumerate(pairs):
        first = first + jnp.where(pair == k, p, 0)
        second = second + jnp.where(pair == k, q, 0)
    return first, second


def masks_kernel(masks):
    block = masks.shape[1]
    row = lax.broadcasted_iota(jnp.int32, (block, block), 0)
    col = lax.broadcasted_iota(jnp.int32, (block, block), 1)
    masks[0] = (row < col).astype(F32).astype(BF16)
    masks[1] = jnp.ones((block, block), BF16)


def baseline_masks(block):
    return pl.pallas_call(
        masks_kernel,
        name="baseline_masks",
        out_shape=shape(2, block, block, dtype=BF16),
        out_specs=vmem_specs(1)[0],
        compiler_params=params(),
        cost_estimate=COSTLY,
    )()


def rows_kernel(masks, gains, delays, ids, flags, rows):
    fields, stations = gains.shape[0] + delays.shape[0], gains.shape[2]
    rows[: gains.shape[0]] = gains[...]
    rows[gains.shape[0] : fields] = delays[...].reshape(delays.shape[0], 1, stations)
    rows[fields:] = jnp.full((2, 1, stations), -1.0, F32)
    slots = ids.shape[1]
    rows[fields, :, :slots] = ids[...].astype(F32)
    rows[fields + 1, :, :slots] = flags[...].astype(F32)


def field_rows(masks, gains, delays, ids, flags):
    return pl.pallas_call(
        rows_kernel,
        name="field_rows",
        out_shape=shape(gains.shape[0] + delays.shape[0] + 2, 1, gains.shape[2]),
        in_specs=vmem_specs(5),
        out_specs=vmem_specs(1)[0],
        compiler_params=params(),
        cost_estimate=COSTLY,
    )(masks, gains, delays, ids, flags)


def prepare_kernel(block, pairs, slots, penalty, chan_count, *refs):
    table, flags, duals, prior, bright, *refs = refs
    duals_out, start_out, coh_out, counts_out = refs
    lane = lax.broadcasted_iota(jnp.int32, (8, 128), 1)
    counts = jnp.zeros((8, 128), F32)
    for slot in range(slots):
        held_here = (lane == table[slot]) & (lane < len(pairs))
        counts = counts + jnp.where(held_here, flags[slot].astype(F32), 0.0)
    counts_out[...] = counts
    coh_out[...] = coherency_tile(bright[...], frequency_of(chan_count))
    duals_own = duals[:, 0, :]
    duals_out[...] = duals_own
    target = -duals_own
    for k, scale in enumerate(basis_of(chan_count)):
        target = target + scale * prior[:, k, :]
    start_out[...] = -penalty * target


def prepare(geometry, table, flags, duals, prior, brightness):
    block, pairs, dumps, penalty, chan_count, stations = geometry
    return pl.pallas_call(
        functools.partial(
            prepare_kernel, block, pairs, table.shape[0], penalty, chan_count
        ),
        name="prepare",
        out_shape=(
            shape(64, block),
            shape(64, block),
            shape(64, 128),
            shape(8, 128),
        ),
        in_specs=smem_specs(2) + vmem_specs(3),
        out_specs=tuple(vmem_specs(4)),
        compiler_params=params(),
        cost_estimate=pl.CostEstimate(flops=1000000, bytes_accessed=2000000, transcendentals=0),
    )(table, flags, duals, prior, brightness)


def data_kernel(block, pairs, dumps, slots, penalty, chan_count, first_call, joined, *refs):
    table, flags, observed, coh_ref, keep, *refs = refs
    if first_call:
        if joined:
            rows_all, *refs = refs
        else:
            rows_mine, rows_other, *refs = refs
        start, counts_mine, out_ref, field_ref, delay_ref, counts_ref, lead, *refs = refs
    else:
        lead, field_ref, delay_ref, out_ref, *refs = refs
    if first_call:
        order, xp, yp, hl, ha = refs
    else:
        held, sems, order, xp, yp, hl, ha = refs
    stations = field_ref.shape[1]
    pair_count = len(pairs)
    at_own = own_lanes(block)

    live_count = jnp.int32(0)
    for slot in range(slots):
        order[live_count] = jnp.int32(slot)
        live_count = live_count + jnp.where(table[slot] < pair_count, 1, 0)
    items = live_count * dumps

    def copy_of(item):
        slot, t = order[item // dumps], item % dumps
        return pltpu.make_async_copy(observed.at[slot, t], held.at[item], sems.at[item])

    if not first_call:
        for item in range(1, min(1 + AHEAD, slots * dumps)):

            @pl.when(item < items)
            def _():
                copy_of(jnp.int32(item)).start()

    freq_value = frequency_of(chan_count)
    if first_call:
        if joined:
            rows_other = rows_all
            field_ref[...] = rows_all[:64, 0, :]
            delay_ref[...] = rows_all[64 : 64 + 8 * dumps, 0, :]
        else:
            at_other = pl.ds(pl.multiple_of((1 - lax.axis_index("stn")) * block, CHUNK), block)
            for at, rows in ((at_own, rows_mine), (at_other, rows_other)):
                field_ref[:, at] = rows[:64, 0, :]
                delay_ref[:, at] = rows[64 : 64 + 8 * dumps, 0, :]
    bright = coherency_rows(coh_ref[...], stations)
    for t in range(dumps):
        cosine, sine = trig(delay_ref[8 * t : 8 * t + 8, :], freq_value)
        rot = rotate(field_ref[...], cosine, sine)
        for i, rows in enumerate(left_rows(rot, bright)):
            xp[t, i] = pack(rows)
        for rj, rows in enumerate(right_rows(rot)):
            yp[t, rj] = pack(rows)
    hl[...] = jnp.zeros_like(hl)
    ha[...] = jnp.zeros_like(ha)

    lane = lax.broadcasted_iota(jnp.int32, (1, block), 1)

    def visit(item, tiles):
        slot, t = order[item // dumps], item % dumps
        first, second = pair_blocks(pairs, table[slot])
        kept = keep[jnp.where(first < second, 1, 0)]
        live = (lane >= flags[slot]).astype(F32)
        live16 = live.astype(BF16)
        at_p = pl.ds(pl.multiple_of(first * block, CHUNK), block)
        at_q = pl.ds(pl.multiple_of(second * block, CHUNK), block)
        acc_left = [None, None]
        acc_right = [None] * 4
        xs = [xp[t, i, :, at_p] * live16 for i in range(2)]
        ys = [yp[t, rj, :, at_q] for rj in range(4)]
        for r in range(2):
            for i in range(2):
                for j in range(2):
                    tile = tiles[4 * r + 2 * i + j] * kept
                    rj = 2 * r + j
                    left = dot(ys[rj], tile, NT)
                    right = dot(xs[i], tile, NN)
                    acc_left[i] = left if acc_left[i] is None else acc_left[i] + left
                    acc_right[rj] = right if acc_right[rj] is None else acc_right[rj] + right
        for i in range(2):
            hl[t, i, :, at_p] += (acc_left[i][:32] + acc_left[i][32:]) * live
        for rj in range(4):
            ha[t, rj, :, at_q] += acc_right[rj][:32] + acc_right[rj][32:]

    def visit_held(item, unused):
        copy_of(item).wait()

        @pl.when(item + AHEAD < items)
        def _():
            copy_of(item + AHEAD).start()

        visit(item, held.at[item])
        return unused

    def visit_there(item, unused):
        visit(item, observed.at[order[item // dumps], item % dumps])
        return unused

    if first_call:
        lax.fori_loop(0, items, visit_there, jnp.int32(0))

        @pl.when(items > 0)
        def _():
            lead[...] = observed[order[0], 0]
    else:

        @pl.when(items > 0)
        def _():
            visit(jnp.int32(0), lead)

        lax.fori_loop(1, items, visit_held, jnp.int32(0))

    total = None
    for t in range(dumps):
        cosine, sine = trig(delay_ref[8 * t : 8 * t + 8, :], freq_value)
        piece = field_gradient(
            [hl[t, i] for i in range(2)], [ha[t, rj] for rj in range(4)], bright, cosine, sine
        )
        total = piece if total is None else total + piece
    out_ref[...] = -total
    prior = penalty * field_ref[:, at_own]
    if first_call:
        prior = prior + start[...]
        counts = counts_mine[...]
        ids_other, flags_other = rows_other[64 + 8 * dumps], rows_other[65 + 8 * dumps]
        pair_lane = lax.broadcasted_iota(jnp.int32, (8, 128), 1)
        for k in range(pair_count):
            theirs = jnp.where(ids_other == float(k), flags_other, 0.0)
            total_flags = jnp.sum(theirs, axis=1, keepdims=True)
            counts = counts + jnp.where(pair_lane == k, total_flags, 0.0)
        counts_ref[...] = counts
    out_ref[:, at_own] += prior


def data_part(geometry, table, flags, observed, coh, masks, fields):
    block, pairs, dumps, penalty, chan_count, stations = geometry
    slots = observed.shape[0]
    first_call = len(fields[0].shape) == 3 and fields[0].dtype == F32
    joined = len(fields) == 3
    body = functools.partial(
        data_kernel, block, pairs, dumps, slots, penalty, chan_count, first_call, joined
    )
    shapes = [shape(64, stations)]
    if first_call:
        shapes += [shape(64, stations), shape(8 * dumps, stations), shape(8, 128)]
        shapes.append(shape(*observed.shape[2:], dtype=BF16))
        place, copies = vmem_specs(1), []
    else:
        place = [pl.BlockSpec(memory_space=pl.ANY)]
        copies = [
            pltpu.VMEM((slots * dumps,) + observed.shape[2:], BF16),
            pltpu.SemaphoreType.DMA((slots * dumps,)),
        ]
    return pl.pallas_call(
        body,
        name="data_part",
        out_shape=tuple(shapes),
        in_specs=smem_specs(2) + place + vmem_specs(2 + len(fields)),
        out_specs=tuple(vmem_specs(len(shapes))),
        scratch_shapes=copies
        + [
            pltpu.SMEM((slots,), jnp.int32),
            pltpu.VMEM((dumps, 2, 64, stations), BF16),
            pltpu.VMEM((dumps, 4, 64, stations), BF16),
            pltpu.VMEM((dumps, 2, 32, stations), F32),
            pltpu.VMEM((dumps, 4, 32, stations), F32),
        ],
        compiler_params=params() if first_call else params(COPY_BYTES),
        cost_estimate=pl.CostEstimate(
            flops=6000000000, bytes_accessed=8000000, transcendentals=0
        ),
    )(table, flags, observed, coh, masks, *fields)


def fold_gram(high_low, other, rows):
    wide = dot(high_low, other[:rows], NT)
    return wide[:rows] + wide[rows:] + dot(high_low[:rows], other[rows:], NT)


def apply_gram(gram, packed, rows):
    size = gram.shape[0]
    both = pack(gram)
    wide = dot(both, packed[:rows], NN)
    return wide[:size] + wide[size:] + dot(both[:size], packed[rows:], NN)


def lanes(parts, start, size):
    return jnp.concatenate([part[:, start : start + size] for part in parts], axis=1)


def twice(mask):
    return jnp.concatenate([mask, mask], axis=1)


class Chunks:
    def __init__(self, block, stations, pairs, counts):
        self.block = block
        self.size = min(CHUNK, block)
        self.per_block = block // self.size
        self.count = stations // self.size
        self.blocks = stations // block
        lane = lax.broadcasted_iota(jnp.int32, (1, block), 1).astype(F32)
        self.masks = {
            pair: (lane >= counts[:, k : k + 1]).astype(F32) for k, pair in enumerate(pairs)
        }
        row = lax.broadcasted_iota(jnp.int32, (2 * self.size, 4 * self.size), 0) % self.size
        col = lax.broadcasted_iota(jnp.int32, (2 * self.size, 4 * self.size), 1) % self.size
        self.upper = row < col

    def mask(self, pair, chunk):
        start = (chunk % self.per_block) * self.size
        return twice(self.masks[pair][:, start : start + self.size])

    def own_pair(self, chunk):
        return (chunk // self.per_block, chunk // self.per_block)

    def rect_terms(self, chunk):
        own = chunk // self.per_block
        terms = []
        inside = list(range(chunk + 1, (own + 1) * self.per_block))
        if inside:
            terms.append(((own, own), inside))
        for q in range(own + 1, self.blocks):
            terms.append(((own, q), list(range(q * self.per_block, (q + 1) * self.per_block))))
        return terms


def sum_of(parts):
    total = parts[0]
    for part in parts[1:]:
        total = total + part
    return total


def halves(rows, axis, odd):
    size = rows.shape[axis] // 2
    low = lax.slice_in_dim(rows, 0, size, axis=axis)
    high = lax.slice_in_dim(rows, size, 2 * size, axis=axis)
    return jnp.where(odd, high, low), jnp.where(odd, low, high)


def store_quarters(fields, sums, outs):
    place = lax.axis_index("chan")
    odd_lanes, odd_rows = place % 2 == 1, (place // 2) % 2 == 1
    for n, field in enumerate(fields):
        for o, part in enumerate(halves(field, 1, odd_lanes)):
            for p, quarter in enumerate(halves(part, 0, odd_rows)):
                outs[o + 2 * p][32 * n : 32 * n + 32, :] = quarter
    for out in outs:
        out[32 * len(fields) :, :] = sums


def step_length(grad_sq, curvature, penalty):
    return grad_sq / (curvature + penalty * grad_sq + EPSILON)


def gradient_kernel(block, pairs, dumps, penalty, chan_count, update, *refs):
    counts_ref, delay_ref, coh_ref, current_ref, *refs = refs
    if update:
        sums_ref, direction_ref, *refs = refs
    gradient_out, *refs = refs
    if update:
        current_out, alpha_out, *refs = refs
    xp, yp, hl, ha = refs
    stations = current_ref.shape[1]
    chunks = Chunks(block, stations, pairs, counts_ref[0:1, :])
    size = chunks.size

    current = current_ref[...]
    if update:
        sums = jnp.sum(sums_ref[...], axis=0, keepdims=True)
        alpha = step_length(sums[:, 0:1], sums[:, 1:2], penalty)
        alpha_out[...] = jnp.broadcast_to(alpha, (8, 128))
        current = current - alpha * direction_ref[...]
        current_out[...] = current
    freq_value = frequency_of(chan_count)
    bright = coherency_rows(coh_ref[...], stations)
    gradient = None
    for t in range(dumps):
        cosine, sine = trig(delay_ref[8 * t : 8 * t + 8, :], freq_value)
        rot = rotate(current, cosine, sine)
        xs = [pack(v) for v in left_rows(rot, bright)]
        ys = [pack(v) for v in right_rows(rot)]
        for i in range(2):
            xp[t, i] = xs[i]
        for rj in range(4):
            yp[t, rj] = ys[rj]
        gram_y = [
            fold_gram(lanes(ys, c * size, size), lanes(ys, c * size, size), 32)
            for c in range(chunks.count)
        ]
        sums_x = [None] * chunks.count
        for c in range(chunks.count):
            xc = lanes(xs, c * size, size)
            yc = lanes(ys, c * size, size)
            xw = xc * chunks.mask(chunks.own_pair(c), c).astype(BF16)
            yn = jnp.concatenate([yc[:32], yc[:32], yc[32:], yc[32:]], axis=0)
            model = dot(jnp.concatenate([xw, xw], axis=0), yn, TN)
            model = jnp.where(chunks.upper, model, 0.0)
            high, low = split(model)
            left = dot(yc, high, NT) + dot(yc, low, NT)
            right = dot(xw, high, NN) + dot(xw, low, NN)
            left = left[:32] + left[32:]
            right = right[:32] + right[32:]
            for pair, others in chunks.rect_terms(c):
                mask = chunks.mask(pair, c)
                left = left + apply_gram(sum_of([gram_y[o] for o in others]), xc, 32) * mask
                gram_x = fold_gram(xc * mask.astype(BF16), xc, 32)
                for o in others:
                    sums_x[o] = gram_x if sums_x[o] is None else sums_x[o] + gram_x
            if sums_x[c] is not None:
                right = right + apply_gram(sums_x[c], yc, 32)
            for i in range(2):
                hl[i, :, c * size : (c + 1) * size] = left[:, i * size : (i + 1) * size]
            for rj in range(4):
                ha[rj, :, c * size : (c + 1) * size] = right[:, rj * size : (rj + 1) * size]
        piece = field_gradient(
            [hl[i] for i in range(2)], [ha[rj] for rj in range(4)], bright, cosine, sine
        )
        gradient = piece if gradient is None else gradient + piece
    gradient_out[...] = gradient


def gradient_part(geometry, counts, delays, coh, current, step):
    block, pairs, dumps, penalty, chan_count, stations = geometry
    update = step is not None
    field = shape(64, stations)
    outs = [field]
    inputs = [counts, delays, coh, current]
    if update:
        inputs += step
        outs += [field, shape(8, 128)]
    outs += [shape(dumps, rows, 64, stations, dtype=BF16) for rows in (2, 4)]
    return pl.pallas_call(
        functools.partial(gradient_kernel, block, pairs, dumps, penalty, chan_count, update),
        name="gradient_part",
        out_shape=tuple(outs),
        in_specs=vmem_specs(len(inputs)),
        out_specs=tuple(vmem_specs(len(outs))),
        scratch_shapes=[pltpu.VMEM((2, 32, stations), F32), pltpu.VMEM((4, 32, stations), F32)],
        compiler_params=params(),
        cost_estimate=pl.CostEstimate(
            flops=4000000000, bytes_accessed=2000000, transcendentals=0
        ),
    )(*inputs)


def curvature_kernel(block, pairs, dumps, penalty, chan_count, update, last, *refs):
    counts_ref, delay_ref, coh_ref, xp, yp, gradient_ref, mine_ref, theirs_ref, *refs = refs
    if update:
        alpha_ref, linear_ref, *refs = refs
    if last:
        duals_ref, current_ref, *refs = refs
    direction_out, *refs = refs
    if not last:
        linear_out, sums_out = refs
    stations = mine_ref.shape[1]
    chunks = Chunks(block, stations, pairs, counts_ref[0:1, :])
    size = chunks.size

    linear = mine_ref[...] + theirs_ref[...]
    if update:
        linear = linear_ref[...] - alpha_ref[0:1, 0:1] * linear
    direction = linear + gradient_ref[...]
    direction_out[...] = direction
    if not last:
        linear_out[...] = linear

    freq_value = frequency_of(chan_count)
    bright = coherency_rows(coh_ref[...], stations)
    squares = jnp.zeros((8, 4 * size), F32)
    grams = jnp.zeros((64, 64), F32)
    if last:
        visited, repeats, copies = range(dumps), 1, 1
    else:
        stn_count = stations // block
        shared = stn_count % dumps == 0
        visited = [lax.axis_index("stn") % dumps] if shared else range(dumps)
        repeats, copies = (stn_count // dumps if shared else stn_count), stn_count
    for t in visited:
        delay = delay_ref[pl.ds(pl.multiple_of(8 * t, 8), 8), :]
        cosine, sine = trig(delay, freq_value)
        step = rotate(direction, cosine, sine)
        xs = [xp[t, i] for i in range(2)]
        ys = [yp[t, rj] for rj in range(4)]
        dxs = [pack(v) for v in left_rows(step, bright)]
        dys = [pack(v) for v in right_rows(step)]

        def stacked(first, second, c):
            one = lanes(first, c * size, size)
            two = lanes(second, c * size, size)
            return jnp.concatenate([one[:32], two[:32], one[32:], two[32:]], axis=0)

        gram_y = [None] * chunks.count
        for c in range(chunks.count):
            xc = stacked(dxs, xs, c)
            yc = stacked(ys, dys, c)
            xw = xc * chunks.mask(chunks.own_pair(c), c).astype(BF16)
            tangent = dot(
                jnp.concatenate([xw, xw], axis=0),
                jnp.concatenate([yc[:64], yc[:64], yc[64:], yc[64:]], axis=0),
                TN,
            )
            tangent = jnp.where(chunks.upper, tangent, 0.0)
            square = tangent * tangent
            squares = squares + jnp.sum(square.reshape(2 * size // 8, 8, 4 * size), axis=0)
            if c > 0:
                gram_y[c] = fold_gram(yc, yc, 64)
        for c in range(chunks.count):
            for pair, others in chunks.rect_terms(c):
                xc = stacked(dxs, xs, c)
                gram_x = fold_gram(xc * chunks.mask(pair, c).astype(BF16), xc, 64)
                grams = grams + sum_of([gram_y[o] for o in others]) * gram_x
    curvature = jnp.sum(squares, keepdims=True) + jnp.sum(grams, keepdims=True)
    grad_sq = jnp.sum(direction * direction, keepdims=True)
    grad_sq = grad_sq * (1.0 / copies)
    curvature = curvature * (1.0 / repeats)
    rows = 8 if last else chan_count * copies
    lane = lax.broadcasted_iota(jnp.int32, (rows, block // 2 if last else 128), 1)
    sums = jnp.where(lane == 0, grad_sq, jnp.where(lane == 1, curvature, 0.0))
    if last:
        base = current_ref[:, own_lanes(block)] + duals_ref[...]
        store_quarters((base, direction_out[:, own_lanes(block)]), sums, refs)
    else:
        sums_out[...] = sums


def curvature_part(geometry, counts, delays, coh, factors, gradient, shares, before, last):
    block, pairs, dumps, penalty, chan_count, stations = geometry
    update = before is not None
    field = shape(64, stations)
    if last is not None:
        outs = [field] + [shape(72, block // 2)] * 4
    else:
        outs = [field, field, shape(chan_count * (stations // block), 128)]
    inputs = [counts, delays, coh, *factors, gradient, *shares]
    if update:
        inputs += before
    if last is not None:
        inputs += last
    return pl.pallas_call(
        functools.partial(
            curvature_kernel, block, pairs, dumps, penalty, chan_count, update, last is not None
        ),
        name="curvature_part",
        out_shape=tuple(outs),
        in_specs=vmem_specs(len(inputs)),
        out_specs=tuple(vmem_specs(len(outs))),
        compiler_params=params(),
        cost_estimate=pl.CostEstimate(
            flops=2000000000, bytes_accessed=2000000, transcendentals=0
        ),
    )(*inputs)


def weigh_kernel(chan_count, *refs):
    *parts, out = refs
    scales = [solve_of(chan_count, offset) for offset in range(4)]
    for n in range(2):
        for k in range(4):
            at = 128 * n + 32 * k
            terms = [scales[o][k] * parts[o][32 * n : 32 * n + 32, :] for o in range(4)]
            out[at : at + 32, :] = sum_in_pairs(terms)
    out[256:, :] = sum_in_pairs([part[64:, :] for part in parts])


def sum_in_pairs(terms):
    return (terms[0] + terms[1]) + (terms[2] + terms[3])


def weigh(geometry, *parts):
    chan_count = geometry[4]
    return pl.pallas_call(
        functools.partial(weigh_kernel, chan_count),
        name="weigh",
        out_shape=shape(264, parts[0].shape[1]),
        in_specs=vmem_specs(4),
        out_specs=vmem_specs(1)[0],
        compiler_params=params(),
    )(*parts)


def combine_kernel(penalty, one, two, coeffs_out, alpha_out):
    total = one[...] + two[...]
    alpha = step_length(total[256:257, 0:1], total[256:257, 1:2], penalty)
    coeffs_out[...] = total[:128] - alpha * total[128:256]
    alpha_out[...] = jnp.broadcast_to(alpha, (8, 128))


def combine(geometry, one, two):
    penalty = geometry[3]
    return pl.pallas_call(
        functools.partial(combine_kernel, penalty),
        name="combine",
        out_shape=(shape(128, one.shape[1]), shape(8, 128)),
        in_specs=vmem_specs(2),
        out_specs=tuple(vmem_specs(2)),
        compiler_params=params(),
    )(one, two)


def last_step_kernel(block, alpha, current, direction, duals, gains_out, shifted_out):
    at_own = own_lanes(block)
    gains_new = current[:, at_own] - alpha[0:1, 0:1] * direction[:, at_own]
    gains_out[:, 0, :] = gains_new
    shifted_out[...] = gains_new + duals[...]


def last_step(geometry, *inputs):
    block = geometry[0]
    return pl.pallas_call(
        functools.partial(last_step_kernel, block),
        name="last_step",
        out_shape=(shape(64, 1, block), shape(64, block)),
        in_specs=vmem_specs(len(inputs)),
        out_specs=tuple(vmem_specs(2)),
        compiler_params=params(),
    )(*inputs)


def consensus_kernel(chan_count, own, core, row, both, shifted, coeffs_out, duals_out):
    place = lax.axis_index("chan")
    odd_core, odd_row = place % 2 == 1, (place // 2) % 2 == 1

    def joined(one, two, odd, axis):
        return jnp.concatenate([jnp.where(odd, two, one), jnp.where(odd, one, two)], axis=axis)

    fitted = None
    for k, scale in enumerate(basis_of(chan_count)):
        at = slice(32 * k, 32 * k + 32)
        coeffs = joined(
            joined(own[at, :], core[at, :], odd_core, 1),
            joined(row[at, :], both[at, :], odd_core, 1),
            odd_row,
            0,
        )
        coeffs_out[:, k, :] = coeffs
        fitted = scale * coeffs if fitted is None else fitted + scale * coeffs
    duals_out[:, 0, :] = shifted[...] - fitted


def consensus(geometry, *inputs):
    block, pairs, dumps, penalty, chan_count, stations = geometry
    return pl.pallas_call(
        functools.partial(consensus_kernel, chan_count),
        name="consensus",
        out_shape=(shape(64, 4, block), shape(64, 1, block)),
        in_specs=vmem_specs(len(inputs)),
        out_specs=tuple(vmem_specs(2)),
        compiler_params=params(),
    )(*inputs)


def swap(value, count, offset):
    return lax.ppermute(value, "chan", [(i, i ^ offset) for i in range(count)])


def other_stations(value):
    return lax.ppermute(value, "stn", [(0, 1), (1, 0)])


def both_stations(value, count):
    if count == 2:
        return value, other_stations(value)
    return jnp.zeros_like(value), lax.psum(value, "stn")


def shards(observed, pair_table, flag_rows, gains, duals, prior_coeffs, delays, brightness):
    stn_count = lax.axis_size("stn")
    chan_count = lax.axis_size("chan")
    entries, dirs, chan_local, block = gains.shape
    slots, dumps = observed.shape[0], observed.shape[2]
    stations = block * stn_count
    pairs = pair_lists(stn_count)
    penalty = stations * dumps / 16.0
    geometry = (block, pairs, dumps, penalty, chan_count, stations)

    observed = observed.reshape((slots,) + observed.shape[2:])
    duals_raw = duals.reshape(entries * dirs, 1, block)
    prior = prior_coeffs.reshape(entries * dirs, 4, block)
    masks = baseline_masks(block)
    rows = field_rows(
        masks,
        gains.reshape(entries * dirs, 1, block),
        delays.reshape(dumps * dirs, block),
        pair_table.reshape(1, slots),
        flag_rows.reshape(1, slots),
    )
    if stn_count == 2:
        fields = (rows, other_stations(rows))
    else:
        fields = (lax.all_gather(rows, "stn", axis=2, tiled=True),)
    duals_own, start, coh, counts = prepare(
        geometry, pair_table, flag_rows, duals_raw, prior, brightness
    )
    if stn_count != 2:
        counts = jnp.zeros_like(counts)
    data = functools.partial(data_part, geometry, pair_table, flag_rows, observed, coh, masks)
    share, current, delay_all, counts, lead = data(fields + (start, counts))
    shares = both_stations(share, stn_count)

    step = before = None
    for iteration in range(ITERS):
        last = iteration + 1 == ITERS
        gradient, *rest = gradient_part(geometry, counts, delay_all, coh, current, step)
        if step is not None:
            current, alpha, *rest = rest
            before = (alpha, linear)
        direction, *rest = curvature_part(
            geometry,
            counts,
            delay_all,
            coh,
            rest,
            gradient,
            shares,
            before,
            (duals_own, current) if last else None,
        )
        if not last:
            linear, sums = rest
            sums = lax.all_to_all(sums, ("chan", "stn"), 0, 0, tiled=True)
            (share,) = data((lead, direction, delay_all))
            shares = both_stations(share, stn_count)
            step = (sums, direction)

    quarters = rest[:1] + [swap(rest[o], chan_count, o) for o in (1, 2, 3)]
    value, bit = weigh(geometry, *quarters), 4
    other = swap(value, chan_count, bit)
    while 2 * bit < chan_count:
        value, bit = value + other, 2 * bit
        other = swap(value, chan_count, bit)
    quarter, alpha = combine(geometry, value, other)
    gains_new, shifted = last_step(geometry, alpha, current, direction, duals_own)
    quarters = [quarter] + [swap(quarter, chan_count, o) for o in (1, 2, 3)]
    coeffs, duals_new = consensus(geometry, *quarters, shifted)
    return (
        gains_new.reshape(gains.shape),
        coeffs.reshape(entries, dirs, 4, block),
        duals_new.reshape(gains.shape),
    )


def solution(mesh):
    return jax.shard_map(
        shards,
        mesh=mesh,
        in_specs=(
            P("stn", ("band", "chan"), None, None, None, None),
            P("stn"),
            P("stn"),
            P(None, None, ("band", "chan"), "stn"),
            P(None, None, ("band", "chan"), "stn"),
            P("band", None, None, "stn"),
            P(None, None, "stn"),
            P("band", None),
        ),
        out_specs=(
            P(None, None, ("band", "chan"), "stn"),
            P("band", None, None, "stn"),
            P(None, None, ("band", "chan"), "stn"),
        ),
        check_vma=False,
    )
```

```python
import functools
import math

import jax
import jax.numpy as jnp
import numpy as np
from jax import lax
from jax.experimental import pallas as pl
from jax.experimental.pallas import tpu as pltpu
from jax.sharding import PartitionSpec as P

ITERS = 3
EPSILON = 1e-06
SPECTRAL_INDEX = 0.7
DIRS = 8
CHUNK = 128
VMEM_BYTES = 24 * 1024 * 1024
COPY_BYTES = 48 * 1024 * 1024
AHEAD = 2
F32 = jnp.float32
BF16 = jnp.bfloat16

COSTLY = pl.CostEstimate(flops=20000000000, bytes_accessed=20000000, transcendentals=0)

NT = (((1,), (1,)), ((), ()))
NN = (((1,), (0,)), ((), ()))
TN = (((0,), (0,)), ((), ()))


def dot(lhs, rhs, dims):
    return lax.dot_general(lhs, rhs, dims, preferred_element_type=F32)


def pair_lists(station_blocks):
    return [(p, q) for p in range(station_blocks) for q in range(p, station_blocks)]


def bernstein_np(total_channels):
    position = (np.arange(total_channels, dtype=np.float64) + 0.5) / total_channels
    others = 1.0 - position
    return np.stack(
        [others**3, 3.0 * position * others**2, 3.0 * position**2 * others, position**3], axis=1
    )


def split(x):
    high = x.astype(BF16)
    return high, (x - high.astype(F32)).astype(BF16)


def pack(x):
    high, low = split(x)
    return jnp.concatenate([high, low], axis=0)


def trig(delay, freq):
    turns = delay * freq
    turns = turns - jnp.floor(turns + 0.5)
    x = turns * math.pi
    x2 = x * x
    sin_half = x * (
        1.0
        + x2
        * (
            -1.0 / 6
            + x2
            * (
                1.0 / 120
                + x2
                * (
                    -1.0 / 5040
                    + x2 * (1.0 / 362880 + x2 * (-1.0 / 39916800 + x2 * (1.0 / 6227020800)))
                )
            )
        )
    )
    cos_half = 1.0 + x2 * (
        -0.5
        + x2
        * (
            1.0 / 24
            + x2
            * (
                -1.0 / 720
                + x2
                * (
                    1.0 / 40320
                    + x2 * (-1.0 / 3628800 + x2 * (1.0 / 479001600 + x2 * (-1.0 / 87178291200)))
                )
            )
        )
    )
    return 1.0 - 2.0 * sin_half * sin_half, 2.0 * sin_half * cos_half


def rotate(field, cosine, sine):
    re = [field[8 * m : 8 * m + 8] for m in range(4)]
    im = [field[32 + 8 * m : 40 + 8 * m] for m in range(4)]
    return (
        [cosine * re[m] - sine * im[m] for m in range(4)],
        [cosine * im[m] + sine * re[m] for m in range(4)],
    )


def coherency_rows(coh, width):
    reps = width // coh.shape[1]
    rows = [jnp.concatenate([coh[8 * e : 8 * e + 8]] * reps, axis=1) for e in range(8)]
    return rows[:4], rows[4:]


def left_rows(rot, bright):
    (a_re, a_im), (c_re, c_im) = rot, bright
    out = []
    for i in range(2):
        re_rows, im_rows = [], []
        for l in range(2):
            re = im = None
            for k in range(2):
                ar, ai, cr, ci = a_re[2 * i + k], a_im[2 * i + k], c_re[2 * k + l], c_im[2 * k + l]
                tr, ti = ar * cr - ai * ci, ar * ci + ai * cr
                re, im = (tr, ti) if re is None else (re + tr, im + ti)
            re_rows.append(re)
            im_rows.append(im)
        out.append(jnp.concatenate(re_rows + im_rows, axis=0))
    return out


def right_rows(rot):
    a_re, a_im = rot
    real = [
        jnp.concatenate([a_re[2 * j], a_re[2 * j + 1], a_im[2 * j], a_im[2 * j + 1]], axis=0)
        for j in range(2)
    ]
    imag = [
        jnp.concatenate([-a_im[2 * j], -a_im[2 * j + 1], a_re[2 * j], a_re[2 * j + 1]], axis=0)
        for j in range(2)
    ]
    return real + imag


def field_gradient(h_left, h_right, bright, cosine, sine):
    c_re, c_im = bright
    g_re, g_im = [], []
    for i in range(2):
        for k in range(2):
            j = i
            re = h_right[j][8 * k : 8 * k + 8] + h_right[2 + j][16 + 8 * k : 24 + 8 * k]
            im = h_right[j][16 + 8 * k : 24 + 8 * k] - h_right[2 + j][8 * k : 8 * k + 8]
            for l in range(2):
                lr = h_left[i][8 * l : 8 * l + 8]
                li = h_left[i][16 + 8 * l : 24 + 8 * l]
                cr, ci = c_re[2 * k + l], c_im[2 * k + l]
                re = re + lr * cr + li * ci
                im = im + li * cr - lr * ci
            g_re.append(cosine * re + sine * im)
            g_im.append(cosine * im - sine * re)
    return jnp.concatenate(g_re + g_im, axis=0)


def coherency_tile(brightness, freq):
    spectral = jnp.exp(-SPECTRAL_INDEX * jnp.log(jnp.full((8, 128), freq, F32)))
    tiles = []
    for e in range(8):
        column = jnp.transpose(jnp.broadcast_to(brightness[e : e + 1, :], (8, 8)))[:, :1]
        tiles.append(column * spectral)
    return jnp.concatenate(tiles, axis=0)


def position_of(chan_count, offset=0):
    place = lax.axis_index("chan")
    if offset:
        place = place ^ offset
    return place.astype(F32) * (1.0 / chan_count)


def frequency_of(chan_count):
    return 1.0 + position_of(chan_count)


def basis_of(chan_count, offset=0):
    x = position_of(chan_count, offset) + 0.5 / chan_count
    y = 1.0 - x
    return [y * y * y, 3.0 * x * y * y, 3.0 * x * x * y, x * x * x]


def solve_of(chan_count, offset):
    basis = bernstein_np(chan_count)
    inverse = np.linalg.inv(basis.T @ basis)
    row = basis_of(chan_count, offset)
    return [sum(row[m] * float(inverse[m, k]) for m in range(4)) for k in range(4)]


def vmem_specs(count):
    return [pl.BlockSpec(memory_space=pltpu.VMEM)] * count


def smem_specs(count):
    return [pl.BlockSpec(memory_space=pltpu.SMEM)] * count


def params(limit=None):
    return pltpu.CompilerParams(vmem_limit_bytes=limit or VMEM_BYTES)


def shape(*dims, dtype=F32):
    return jax.ShapeDtypeStruct(dims, dtype)


def own_lanes(block):
    return pl.ds(pl.multiple_of(lax.axis_index("stn") * block, CHUNK), block)


def pair_blocks(pairs, pair):
    first, second = jnp.int32(0), jnp.int32(0)
    for k, (p, q) in enumerate(pairs):
        first = first + jnp.where(pair == k, p, 0)
        second = second + jnp.where(pair == k, q, 0)
    return first, second


def masks_kernel(masks):
    block = masks.shape[1]
    row = lax.broadcasted_iota(jnp.int32, (block, block), 0)
    col = lax.broadcasted_iota(jnp.int32, (block, block), 1)
    masks[0] = (row < col).astype(F32).astype(BF16)
    masks[1] = jnp.ones((block, block), BF16)


def baseline_masks(block):
    return pl.pallas_call(
        masks_kernel,
        name="baseline_masks",
        out_shape=shape(2, block, block, dtype=BF16),
        out_specs=vmem_specs(1)[0],
        compiler_params=params(),
        cost_estimate=COSTLY,
    )()


def rows_kernel(masks, gains, delays, ids, flags, rows):
    fields, stations = gains.shape[0] + delays.shape[0], gains.shape[2]
    rows[: gains.shape[0]] = gains[...]
    rows[gains.shape[0] : fields] = delays[...].reshape(delays.shape[0], 1, stations)
    rows[fields:] = jnp.full((2, 1, stations), -1.0, F32)
    slots = ids.shape[1]
    rows[fields, :, :slots] = ids[...].astype(F32)
    rows[fields + 1, :, :slots] = flags[...].astype(F32)


def field_rows(masks, gains, delays, ids, flags):
    return pl.pallas_call(
        rows_kernel,
        name="field_rows",
        out_shape=shape(gains.shape[0] + delays.shape[0] + 2, 1, gains.shape[2]),
        in_specs=vmem_specs(5),
        out_specs=vmem_specs(1)[0],
        compiler_params=params(),
        cost_estimate=COSTLY,
    )(masks, gains, delays, ids, flags)


def prepare_kernel(block, pairs, slots, penalty, chan_count, *refs):
    table, flags, duals, prior, bright, *refs = refs
    duals_out, start_out, coh_out, counts_out = refs
    lane = lax.broadcasted_iota(jnp.int32, (8, 128), 1)
    counts = jnp.zeros((8, 128), F32)
    for slot in range(slots):
        held_here = (lane == table[slot]) & (lane < len(pairs))
        counts = counts + jnp.where(held_here, flags[slot].astype(F32), 0.0)
    counts_out[...] = counts
    coh_out[...] = coherency_tile(bright[...], frequency_of(chan_count))
    duals_own = duals[:, 0, :]
    duals_out[...] = duals_own
    target = -duals_own
    for k, scale in enumerate(basis_of(chan_count)):
        target = target + scale * prior[:, k, :]
    start_out[...] = -penalty * target


def prepare(geometry, table, flags, duals, prior, brightness):
    block, pairs, dumps, penalty, chan_count, stations = geometry
    return pl.pallas_call(
        functools.partial(
            prepare_kernel, block, pairs, table.shape[0], penalty, chan_count
        ),
        name="prepare",
        out_shape=(
            shape(64, block),
            shape(64, block),
            shape(64, 128),
            shape(8, 128),
        ),
        in_specs=smem_specs(2) + vmem_specs(3),
        out_specs=tuple(vmem_specs(4)),
        compiler_params=params(),
        cost_estimate=pl.CostEstimate(flops=1000000, bytes_accessed=2000000, transcendentals=0),
    )(table, flags, duals, prior, brightness)


def data_kernel(block, pairs, dumps, slots, penalty, chan_count, first_call, joined, *refs):
    table, flags, observed, coh_ref, keep, *refs = refs
    if first_call:
        if joined:
            rows_all, *refs = refs
        else:
            rows_mine, rows_other, *refs = refs
        start, counts_mine, out_ref, field_ref, delay_ref, counts_ref, lead, *refs = refs
    else:
        lead, field_ref, delay_ref, out_ref, *refs = refs
    if first_call:
        order, xp, yp, hl, ha = refs
    else:
        held, sems, order, xp, yp, hl, ha = refs
    stations = field_ref.shape[1]
    pair_count = len(pairs)
    at_own = own_lanes(block)

    live_count = jnp.int32(0)
    for slot in range(slots):
        order[live_count] = jnp.int32(slot)
        live_count = live_count + jnp.where(table[slot] < pair_count, 1, 0)
    items = live_count * dumps

    def copy_of(item):
        slot, t = order[item // dumps], item % dumps
        return pltpu.make_async_copy(observed.at[slot, t], held.at[item], sems.at[item])

    if not first_call:
        for item in range(1, min(1 + AHEAD, slots * dumps)):

            @pl.when(item < items)
            def _():
                copy_of(jnp.int32(item)).start()

    freq_value = frequency_of(chan_count)
    if first_call:
        if joined:
            rows_other = rows_all
            field_ref[...] = rows_all[:64, 0, :]
            delay_ref[...] = rows_all[64 : 64 + 8 * dumps, 0, :]
        else:
            at_other = pl.ds(pl.multiple_of((1 - lax.axis_index("stn")) * block, CHUNK), block)
            for at, rows in ((at_own, rows_mine), (at_other, rows_other)):
                field_ref[:, at] = rows[:64, 0, :]
                delay_ref[:, at] = rows[64 : 64 + 8 * dumps, 0, :]
    bright = coherency_rows(coh_ref[...], stations)
    for t in range(dumps):
        cosine, sine = trig(delay_ref[8 * t : 8 * t + 8, :], freq_value)
        rot = rotate(field_ref[...], cosine, sine)
        for i, rows in enumerate(left_rows(rot, bright)):
            xp[t, i] = pack(rows)
        for rj, rows in enumerate(right_rows(rot)):
            yp[t, rj] = pack(rows)
    hl[...] = jnp.zeros_like(hl)
    ha[...] = jnp.zeros_like(ha)

    lane = lax.broadcasted_iota(jnp.int32, (1, block), 1)

    def visit(item, tiles):
        slot, t = order[item // dumps], item % dumps
        first, second = pair_blocks(pairs, table[slot])
        kept = keep[jnp.where(first < second, 1, 0)]
        live = (lane >= flags[slot]).astype(F32)
        live16 = live.astype(BF16)
        at_p = pl.ds(pl.multiple_of(first * block, CHUNK), block)
        at_q = pl.ds(pl.multiple_of(second * block, CHUNK), block)
        acc_left = [None, None]
        acc_right = [None] * 4
        xs = [xp[t, i, :, at_p] * live16 for i in range(2)]
        ys = [yp[t, rj, :, at_q] for rj in range(4)]
        for r in range(2):
            for i in range(2):
                for j in range(2):
                    tile = tiles[4 * r + 2 * i + j] * kept
                    rj = 2 * r + j
                    left = dot(ys[rj], tile, NT)
                    right = dot(xs[i], tile, NN)
                    acc_left[i] = left if acc_left[i] is None else acc_left[i] + left
                    acc_right[rj] = right if acc_right[rj] is None else acc_right[rj] + right
        for i in range(2):
            hl[t, i, :, at_p] += (acc_left[i][:32] + acc_left[i][32:]) * live
        for rj in range(4):
            ha[t, rj, :, at_q] += acc_right[rj][:32] + acc_right[rj][32:]

    def visit_held(item, unused):
        copy_of(item).wait()

        @pl.when(item + AHEAD < items)
        def _():
            copy_of(item + AHEAD).start()

        visit(item, held.at[item])
        return unused

    def visit_there(item, unused):
        visit(item, observed.at[order[item // dumps], item % dumps])
        return unused

    if first_call:
        lax.fori_loop(0, items, visit_there, jnp.int32(0))

        @pl.when(items > 0)
        def _():
            lead[...] = observed[order[0], 0]
    else:

        @pl.when(items > 0)
        def _():
            visit(jnp.int32(0), lead)

        lax.fori_loop(1, items, visit_held, jnp.int32(0))

    total = None
    for t in range(dumps):
        cosine, sine = trig(delay_ref[8 * t : 8 * t + 8, :], freq_value)
        piece = field_gradient(
            [hl[t, i] for i in range(2)], [ha[t, rj] for rj in range(4)], bright, cosine, sine
        )
        total = piece if total is None else total + piece
    out_ref[...] = -total
    prior = penalty * field_ref[:, at_own]
    if first_call:
        prior = prior + start[...]
        counts = counts_mine[...]
        ids_other, flags_other = rows_other[64 + 8 * dumps], rows_other[65 + 8 * dumps]
        pair_lane = lax.broadcasted_iota(jnp.int32, (8, 128), 1)
        for k in range(pair_count):
            theirs = jnp.where(ids_other == float(k), flags_other, 0.0)
            total_flags = jnp.sum(theirs, axis=1, keepdims=True)
            counts = counts + jnp.where(pair_lane == k, total_flags, 0.0)
        counts_ref[...] = counts
    out_ref[:, at_own] += prior


def data_part(geometry, table, flags, observed, coh, masks, fields):
    block, pairs, dumps, penalty, chan_count, stations = geometry
    slots = observed.shape[0]
    first_call = len(fields[0].shape) == 3 and fields[0].dtype == F32
    joined = len(fields) == 3
    body = functools.partial(
        data_kernel, block, pairs, dumps, slots, penalty, chan_count, first_call, joined
    )
    shapes = [shape(64, stations)]
    if first_call:
        shapes += [shape(64, stations), shape(8 * dumps, stations), shape(8, 128)]
        shapes.append(shape(*observed.shape[2:], dtype=BF16))
        place, copies = vmem_specs(1), []
    else:
        place = [pl.BlockSpec(memory_space=pl.ANY)]
        copies = [
            pltpu.VMEM((slots * dumps,) + observed.shape[2:], BF16),
            pltpu.SemaphoreType.DMA((slots * dumps,)),
        ]
    return pl.pallas_call(
        body,
        name="data_part",
        out_shape=tuple(shapes),
        in_specs=smem_specs(2) + place + vmem_specs(2 + len(fields)),
        out_specs=tuple(vmem_specs(len(shapes))),
        scratch_shapes=copies
        + [
            pltpu.SMEM((slots,), jnp.int32),
            pltpu.VMEM((dumps, 2, 64, stations), BF16),
            pltpu.VMEM((dumps, 4, 64, stations), BF16),
            pltpu.VMEM((dumps, 2, 32, stations), F32),
            pltpu.VMEM((dumps, 4, 32, stations), F32),
        ],
        compiler_params=params() if first_call else params(COPY_BYTES),
        cost_estimate=pl.CostEstimate(
            flops=6000000000, bytes_accessed=8000000, transcendentals=0
        ),
    )(table, flags, observed, coh, masks, *fields)


def fold_gram(high_low, other, rows):
    wide = dot(high_low, other[:rows], NT)
    return wide[:rows] + wide[rows:] + dot(high_low[:rows], other[rows:], NT)


def apply_gram(gram, packed, rows):
    size = gram.shape[0]
    both = pack(gram)
    wide = dot(both, packed[:rows], NN)
    return wide[:size] + wide[size:] + dot(both[:size], packed[rows:], NN)


def lanes(parts, start, size):
    return jnp.concatenate([part[:, start : start + size] for part in parts], axis=1)


def twice(mask):
    return jnp.concatenate([mask, mask], axis=1)


class Chunks:
    def __init__(self, block, stations, pairs, counts):
        self.block = block
        self.size = min(CHUNK, block)
        self.per_block = block // self.size
        self.count = stations // self.size
        self.blocks = stations // block
        lane = lax.broadcasted_iota(jnp.int32, (1, block), 1).astype(F32)
        self.masks = {
            pair: (lane >= counts[:, k : k + 1]).astype(F32) for k, pair in enumerate(pairs)
        }
        row = lax.broadcasted_iota(jnp.int32, (2 * self.size, 4 * self.size), 0) % self.size
        col = lax.broadcasted_iota(jnp.int32, (2 * self.size, 4 * self.size), 1) % self.size
        self.upper = row < col

    def mask(self, pair, chunk):
        start = (chunk % self.per_block) * self.size
        return twice(self.masks[pair][:, start : start + self.size])

    def own_pair(self, chunk):
        return (chunk // self.per_block, chunk // self.per_block)

    def rect_terms(self, chunk):
        own = chunk // self.per_block
        terms = []
        inside = list(range(chunk + 1, (own + 1) * self.per_block))
        if inside:
            terms.append(((own, own), inside))
        for q in range(own + 1, self.blocks):
            terms.append(((own, q), list(range(q * self.per_block, (q + 1) * self.per_block))))
        return terms


def sum_of(parts):
    total = parts[0]
    for part in parts[1:]:
        total = total + part
    return total


def halves(rows, axis, odd):
    size = rows.shape[axis] // 2
    low = lax.slice_in_dim(rows, 0, size, axis=axis)
    high = lax.slice_in_dim(rows, size, 2 * size, axis=axis)
    return jnp.where(odd, high, low), jnp.where(odd, low, high)


def store_eighths(fields, sums, outs):
    place = lax.axis_index("chan")
    odd_lanes, odd_low, odd_high = place % 2 == 1, (place // 2) % 2 == 1, (place // 4) % 2 == 1
    for n, field in enumerate(fields):
        for out, part in zip(outs, halves(field, 1, odd_lanes)):
            for high, half in enumerate(halves(part, 0, odd_high)):
                for low, rows in enumerate(halves(half, 0, odd_low)):
                    at = 32 * (2 * high + low) + 16 * n
                    out[at : at + 16, :] = rows
    for out in outs:
        out[128:, :] = sums


def step_length(grad_sq, curvature, penalty):
    return grad_sq / (curvature + penalty * grad_sq + EPSILON)


def gradient_kernel(block, pairs, dumps, penalty, chan_count, update, *refs):
    counts_ref, delay_ref, coh_ref, current_ref, *refs = refs
    if update:
        sums_ref, direction_ref, *refs = refs
    gradient_out, *refs = refs
    if update:
        current_out, alpha_out, *refs = refs
    xp, yp, hl, ha = refs
    stations = current_ref.shape[1]
    chunks = Chunks(block, stations, pairs, counts_ref[0:1, :])
    size = chunks.size

    current = current_ref[...]
    if update:
        sums = jnp.sum(sums_ref[...], axis=0, keepdims=True)
        alpha = step_length(sums[:, 0:1], sums[:, 1:2], penalty)
        alpha_out[...] = jnp.broadcast_to(alpha, (8, 128))
        current = current - alpha * direction_ref[...]
        current_out[...] = current
    freq_value = frequency_of(chan_count)
    bright = coherency_rows(coh_ref[...], stations)
    gradient = None
    for t in range(dumps):
        cosine, sine = trig(delay_ref[8 * t : 8 * t + 8, :], freq_value)
        rot = rotate(current, cosine, sine)
        xs = [pack(v) for v in left_rows(rot, bright)]
        ys = [pack(v) for v in right_rows(rot)]
        for i in range(2):
            xp[t, i] = xs[i]
        for rj in range(4):
            yp[t, rj] = ys[rj]
        gram_y = [
            fold_gram(lanes(ys, c * size, size), lanes(ys, c * size, size), 32)
            for c in range(chunks.count)
        ]
        sums_x = [None] * chunks.count
        for c in range(chunks.count):
            xc = lanes(xs, c * size, size)
            yc = lanes(ys, c * size, size)
            xw = xc * chunks.mask(chunks.own_pair(c), c).astype(BF16)
            yn = jnp.concatenate([yc[:32], yc[:32], yc[32:], yc[32:]], axis=0)
            model = dot(jnp.concatenate([xw, xw], axis=0), yn, TN)
            model = jnp.where(chunks.upper, model, 0.0)
            high, low = split(model)
            left = dot(yc, high, NT) + dot(yc, low, NT)
            right = dot(xw, high, NN) + dot(xw, low, NN)
            left = left[:32] + left[32:]
            right = right[:32] + right[32:]
            for pair, others in chunks.rect_terms(c):
                mask = chunks.mask(pair, c)
                left = left + apply_gram(sum_of([gram_y[o] for o in others]), xc, 32) * mask
                gram_x = fold_gram(xc * mask.astype(BF16), xc, 32)
                for o in others:
                    sums_x[o] = gram_x if sums_x[o] is None else sums_x[o] + gram_x
            if sums_x[c] is not None:
                right = right + apply_gram(sums_x[c], yc, 32)
            for i in range(2):
                hl[i, :, c * size : (c + 1) * size] = left[:, i * size : (i + 1) * size]
            for rj in range(4):
                ha[rj, :, c * size : (c + 1) * size] = right[:, rj * size : (rj + 1) * size]
        piece = field_gradient(
            [hl[i] for i in range(2)], [ha[rj] for rj in range(4)], bright, cosine, sine
        )
        gradient = piece if gradient is None else gradient + piece
    gradient_out[...] = gradient


def gradient_part(geometry, counts, delays, coh, current, step):
    block, pairs, dumps, penalty, chan_count, stations = geometry
    update = step is not None
    field = shape(64, stations)
    outs = [field]
    inputs = [counts, delays, coh, current]
    if update:
        inputs += step
        outs += [field, shape(8, 128)]
    outs += [shape(dumps, rows, 64, stations, dtype=BF16) for rows in (2, 4)]
    return pl.pallas_call(
        functools.partial(gradient_kernel, block, pairs, dumps, penalty, chan_count, update),
        name="gradient_part",
        out_shape=tuple(outs),
        in_specs=vmem_specs(len(inputs)),
        out_specs=tuple(vmem_specs(len(outs))),
        scratch_shapes=[pltpu.VMEM((2, 32, stations), F32), pltpu.VMEM((4, 32, stations), F32)],
        compiler_params=params(),
        cost_estimate=pl.CostEstimate(
            flops=4000000000, bytes_accessed=2000000, transcendentals=0
        ),
    )(*inputs)


def curvature_kernel(block, pairs, dumps, penalty, chan_count, update, last, *refs):
    counts_ref, delay_ref, coh_ref, xp, yp, gradient_ref, mine_ref, theirs_ref, *refs = refs
    if update:
        alpha_ref, linear_ref, *refs = refs
    if last:
        duals_ref, current_ref, *refs = refs
    direction_out, *refs = refs
    if not last:
        linear_out, sums_out = refs
    stations = mine_ref.shape[1]
    chunks = Chunks(block, stations, pairs, counts_ref[0:1, :])
    size = chunks.size

    linear = mine_ref[...] + theirs_ref[...]
    if update:
        linear = linear_ref[...] - alpha_ref[0:1, 0:1] * linear
    direction = linear + gradient_ref[...]
    direction_out[...] = direction
    if not last:
        linear_out[...] = linear

    freq_value = frequency_of(chan_count)
    bright = coherency_rows(coh_ref[...], stations)
    squares = jnp.zeros((8, 4 * size), F32)
    grams = jnp.zeros((64, 64), F32)
    if last:
        visited, repeats, copies = range(dumps), 1, 1
    else:
        stn_count = stations // block
        shared = stn_count % dumps == 0
        visited = [lax.axis_index("stn") % dumps] if shared else range(dumps)
        repeats, copies = (stn_count // dumps if shared else stn_count), stn_count
    for t in visited:
        delay = delay_ref[pl.ds(pl.multiple_of(8 * t, 8), 8), :]
        cosine, sine = trig(delay, freq_value)
        step = rotate(direction, cosine, sine)
        xs = [xp[t, i] for i in range(2)]
        ys = [yp[t, rj] for rj in range(4)]
        dxs = [pack(v) for v in left_rows(step, bright)]
        dys = [pack(v) for v in right_rows(step)]

        def stacked(first, second, c):
            one = lanes(first, c * size, size)
            two = lanes(second, c * size, size)
            return jnp.concatenate([one[:32], two[:32], one[32:], two[32:]], axis=0)

        gram_y = [None] * chunks.count
        for c in range(chunks.count):
            xc = stacked(dxs, xs, c)
            yc = stacked(ys, dys, c)
            xw = xc * chunks.mask(chunks.own_pair(c), c).astype(BF16)
            tangent = dot(
                jnp.concatenate([xw, xw], axis=0),
                jnp.concatenate([yc[:64], yc[:64], yc[64:], yc[64:]], axis=0),
                TN,
            )
            tangent = jnp.where(chunks.upper, tangent, 0.0)
            square = tangent * tangent
            squares = squares + jnp.sum(square.reshape(2 * size // 8, 8, 4 * size), axis=0)
            if c > 0:
                gram_y[c] = fold_gram(yc, yc, 64)
        for c in range(chunks.count):
            for pair, others in chunks.rect_terms(c):
                xc = stacked(dxs, xs, c)
                gram_x = fold_gram(xc * chunks.mask(pair, c).astype(BF16), xc, 64)
                grams = grams + sum_of([gram_y[o] for o in others]) * gram_x
    curvature = jnp.sum(squares, keepdims=True) + jnp.sum(grams, keepdims=True)
    grad_sq = jnp.sum(direction * direction, keepdims=True)
    grad_sq = grad_sq * (1.0 / copies)
    curvature = curvature * (1.0 / repeats)
    rows = 8 if last else chan_count * copies
    lane = lax.broadcasted_iota(jnp.int32, (rows, block // 2 if last else 128), 1)
    sums = jnp.where(lane == 0, grad_sq, jnp.where(lane == 1, curvature, 0.0))
    if last:
        base = current_ref[:, own_lanes(block)] + duals_ref[...]
        store_eighths((base, direction_out[:, own_lanes(block)]), sums, refs)
    else:
        sums_out[...] = sums


def curvature_part(geometry, counts, delays, coh, factors, gradient, shares, before, last):
    block, pairs, dumps, penalty, chan_count, stations = geometry
    update = before is not None
    field = shape(64, stations)
    if last is not None:
        outs = [field] + [shape(136, block // 2)] * 2
    else:
        outs = [field, field, shape(chan_count * (stations // block), 128)]
    inputs = [counts, delays, coh, *factors, gradient, *shares]
    if update:
        inputs += before
    if last is not None:
        inputs += last
    return pl.pallas_call(
        functools.partial(
            curvature_kernel, block, pairs, dumps, penalty, chan_count, update, last is not None
        ),
        name="curvature_part",
        out_shape=tuple(outs),
        in_specs=vmem_specs(len(inputs)),
        out_specs=tuple(vmem_specs(len(outs))),
        compiler_params=params(),
        cost_estimate=pl.CostEstimate(
            flops=2000000000, bytes_accessed=2000000, transcendentals=0
        ),
    )(*inputs)


def regroup_kernel(mine, theirs, *outs):
    for o, out in enumerate(outs):
        out[:32, :] = mine[32 * o : 32 * o + 32, :]
        out[32:64, :] = theirs[32 * o : 32 * o + 32, :]
        out[64:, :] = mine[128:, :] + theirs[128:, :]


def regroup(mine, theirs):
    return pl.pallas_call(
        regroup_kernel,
        name="regroup",
        out_shape=(shape(72, mine.shape[1]),) * 4,
        in_specs=vmem_specs(2),
        out_specs=tuple(vmem_specs(4)),
        compiler_params=params(),
    )(mine, theirs)


def sum_in_pairs(terms):
    return (terms[0] + terms[1]) + (terms[2] + terms[3])


def weigh_kernel(chan_count, *refs):
    *parts, out = refs
    scales = [solve_of(chan_count, offset) for offset in range(8)]
    for n in range(2):
        for k in range(4):
            terms = []
            for o, part in enumerate(parts):
                one = part[16 * n : 16 * n + 16, :]
                two = part[32 + 16 * n : 48 + 16 * n, :]
                terms.append(scales[2 * o][k] * one + scales[2 * o + 1][k] * two)
            at = 64 * n + 16 * k
            out[at : at + 16, :] = sum_in_pairs(terms)
    out[128:, :] = sum_in_pairs([part[64:, :] for part in parts])


def weigh(geometry, parts):
    chan_count = geometry[4]
    return pl.pallas_call(
        functools.partial(weigh_kernel, chan_count),
        name="weigh",
        out_shape=shape(136, parts[0].shape[1]),
        in_specs=vmem_specs(4),
        out_specs=vmem_specs(1)[0],
        compiler_params=params(),
    )(*parts)


def combine_kernel(penalty, one, two, coeffs_out, alpha_out):
    total = one[...] + two[...]
    alpha = step_length(total[128:129, 0:1], total[128:129, 1:2], penalty)
    coeffs_out[...] = total[:64] - alpha * total[64:128]
    alpha_out[...] = jnp.broadcast_to(alpha, (8, 128))


def combine(geometry, one, two):
    penalty = geometry[3]
    return pl.pallas_call(
        functools.partial(combine_kernel, penalty),
        name="combine",
        out_shape=(shape(64, one.shape[1]), shape(8, 128)),
        in_specs=vmem_specs(2),
        out_specs=tuple(vmem_specs(2)),
        compiler_params=params(),
    )(one, two)


def last_step_kernel(block, alpha, current, direction, duals, gains_out, shifted_out):
    at_own = own_lanes(block)
    gains_new = current[:, at_own] - alpha[0:1, 0:1] * direction[:, at_own]
    gains_out[:, 0, :] = gains_new
    shifted_out[:, 0, :] = gains_new + duals[...]


def last_step(geometry, *inputs):
    block = geometry[0]
    return pl.pallas_call(
        functools.partial(last_step_kernel, block),
        name="last_step",
        out_shape=(shape(64, 1, block), shape(64, 1, block)),
        in_specs=vmem_specs(len(inputs)),
        out_specs=tuple(vmem_specs(2)),
        compiler_params=params(),
    )(*inputs)


def consensus_kernel(chan_count, mine, theirs, shifted, coeffs_out, duals_out):
    place = lax.axis_index("chan")
    odd = place % 2 == 1
    for o in range(4):
        rows = pl.ds((((place // 2) % 4) ^ o) * 16, 16)
        fitted = None
        for k, scale in enumerate(basis_of(chan_count)):
            at = slice(64 * o + 16 * k, 64 * o + 16 * k + 16)
            one, two = mine[at, :], theirs[at, :]
            coeffs = jnp.concatenate([jnp.where(odd, two, one), jnp.where(odd, one, two)], axis=1)
            coeffs_out[rows, k, :] = coeffs
            fitted = scale * coeffs if fitted is None else fitted + scale * coeffs
        duals_out[rows, 0, :] = shifted[rows, 0, :] - fitted


def consensus(geometry, *inputs):
    block, pairs, dumps, penalty, chan_count, stations = geometry
    return pl.pallas_call(
        functools.partial(consensus_kernel, chan_count),
        name="consensus",
        out_shape=(shape(64, 4, block), shape(64, 1, block)),
        in_specs=vmem_specs(len(inputs)),
        out_specs=tuple(vmem_specs(2)),
        compiler_params=params(),
    )(*inputs)


def swap(value, count, offset):
    return lax.ppermute(value, "chan", [(i, i ^ offset) for i in range(count)])


def other_stations(value):
    return lax.ppermute(value, "stn", [(0, 1), (1, 0)])


def both_stations(value, count):
    if count == 2:
        return value, other_stations(value)
    return jnp.zeros_like(value), lax.psum(value, "stn")


def shards(observed, pair_table, flag_rows, gains, duals, prior_coeffs, delays, brightness):
    stn_count = lax.axis_size("stn")
    chan_count = lax.axis_size("chan")
    entries, dirs, chan_local, block = gains.shape
    slots, dumps = observed.shape[0], observed.shape[2]
    stations = block * stn_count
    pairs = pair_lists(stn_count)
    penalty = stations * dumps / 16.0
    geometry = (block, pairs, dumps, penalty, chan_count, stations)

    observed = observed.reshape((slots,) + observed.shape[2:])
    duals_raw = duals.reshape(entries * dirs, 1, block)
    prior = prior_coeffs.reshape(entries * dirs, 4, block)
    masks = baseline_masks(block)
    rows = field_rows(
        masks,
        gains.reshape(entries * dirs, 1, block),
        delays.reshape(dumps * dirs, block),
        pair_table.reshape(1, slots),
        flag_rows.reshape(1, slots),
    )
    if stn_count == 2:
        fields = (rows, other_stations(rows))
    else:
        fields = (lax.all_gather(rows, "stn", axis=2, tiled=True),)
    duals_own, start, coh, counts = prepare(
        geometry, pair_table, flag_rows, duals_raw, prior, brightness
    )
    if stn_count != 2:
        counts = jnp.zeros_like(counts)
    data = functools.partial(data_part, geometry, pair_table, flag_rows, observed, coh, masks)
    share, current, delay_all, counts, lead = data(fields + (start, counts))
    shares = both_stations(share, stn_count)

    step = before = None
    for iteration in range(ITERS):
        last = iteration + 1 == ITERS
        gradient, *rest = gradient_part(geometry, counts, delay_all, coh, current, step)
        if step is not None:
            current, alpha, *rest = rest
            before = (alpha, linear)
        direction, *rest = curvature_part(
            geometry,
            counts,
            delay_all,
            coh,
            rest,
            gradient,
            shares,
            before,
            (duals_own, current) if last else None,
        )
        if not last:
            linear, sums = rest
            sums = lax.all_to_all(sums, ("chan", "stn"), 0, 0, tiled=True)
            (share,) = data((lead, direction, delay_all))
            shares = both_stations(share, stn_count)
            step = (sums, direction)

    keep, send = rest
    own, *others = regroup(keep, swap(send, chan_count, 1))
    parts = [own] + [swap(part, chan_count, 2 + 2 * o) for o, part in enumerate(others)]
    value, bit = weigh(geometry, parts), 8
    other = swap(value, chan_count, bit)
    while 2 * bit < chan_count:
        value, bit = value + other, 2 * bit
        other = swap(value, chan_count, bit)
    rows, alpha = combine(geometry, value, other)
    gains_new, shifted = last_step(geometry, alpha, current, direction, duals_own)
    mine = jnp.concatenate([rows] + [swap(rows, chan_count, o) for o in (2, 4, 6)])
    coeffs, duals_new = consensus(geometry, mine, swap(mine, chan_count, 1), shifted)
    return (
        gains_new.reshape(gains.shape),
        coeffs.reshape(entries, dirs, 4, block),
        duals_new.reshape(gains.shape),
    )


def solution(mesh):
    return jax.shard_map(
        shards,
        mesh=mesh,
        in_specs=(
            P("stn", ("band", "chan"), None, None, None, None),
            P("stn"),
            P("stn"),
            P(None, None, ("band", "chan"), "stn"),
            P(None, None, ("band", "chan"), "stn"),
            P("band", None, None, "stn"),
            P(None, None, "stn"),
            P("band", None),
        ),
        out_specs=(
            P(None, None, ("band", "chan"), "stn"),
            P("band", None, None, "stn"),
            P(None, None, ("band", "chan"), "stn"),
        ),
        check_vma=False,
    )
```

```python
import functools
import math

import jax
import jax.numpy as jnp
import numpy as np
from jax import lax
from jax.experimental import pallas as pl
from jax.experimental.pallas import tpu as pltpu
from jax.sharding import PartitionSpec as P

ITERS = 3
EPSILON = 1e-06
SPECTRAL_INDEX = 0.7
DIRS = 8
CHUNK = 128
VMEM_BYTES = 24 * 1024 * 1024
COPY_BYTES = 48 * 1024 * 1024
AHEAD = 2
F32 = jnp.float32
BF16 = jnp.bfloat16

COSTLY = pl.CostEstimate(flops=20000000000, bytes_accessed=20000000, transcendentals=0)

NT = (((1,), (1,)), ((), ()))
NN = (((1,), (0,)), ((), ()))
TN = (((0,), (0,)), ((), ()))


def dot(lhs, rhs, dims):
    return lax.dot_general(lhs, rhs, dims, preferred_element_type=F32)


def pair_lists(station_blocks):
    return [(p, q) for p in range(station_blocks) for q in range(p, station_blocks)]


def bernstein_np(total_channels):
    position = (np.arange(total_channels, dtype=np.float64) + 0.5) / total_channels
    others = 1.0 - position
    return np.stack(
        [others**3, 3.0 * position * others**2, 3.0 * position**2 * others, position**3], axis=1
    )


def split(x):
    high = x.astype(BF16)
    return high, (x - high.astype(F32)).astype(BF16)


def pack(x):
    high, low = split(x)
    return jnp.concatenate([high, low], axis=0)


def trig(delay, freq):
    turns = delay * freq
    turns = turns - jnp.floor(turns + 0.5)
    x = turns * math.pi
    x2 = x * x
    sin_half = x * (
        1.0
        + x2
        * (
            -1.0 / 6
            + x2
            * (
                1.0 / 120
                + x2
                * (
                    -1.0 / 5040
                    + x2 * (1.0 / 362880 + x2 * (-1.0 / 39916800 + x2 * (1.0 / 6227020800)))
                )
            )
        )
    )
    cos_half = 1.0 + x2 * (
        -0.5
        + x2
        * (
            1.0 / 24
            + x2
            * (
                -1.0 / 720
                + x2
                * (
                    1.0 / 40320
                    + x2 * (-1.0 / 3628800 + x2 * (1.0 / 479001600 + x2 * (-1.0 / 87178291200)))
                )
            )
        )
    )
    return 1.0 - 2.0 * sin_half * sin_half, 2.0 * sin_half * cos_half


def rotate(field, cosine, sine):
    re = [field[8 * m : 8 * m + 8] for m in range(4)]
    im = [field[32 + 8 * m : 40 + 8 * m] for m in range(4)]
    return (
        [cosine * re[m] - sine * im[m] for m in range(4)],
        [cosine * im[m] + sine * re[m] for m in range(4)],
    )


def coherency_rows(coh, width):
    reps = width // coh.shape[1]
    rows = [jnp.concatenate([coh[8 * e : 8 * e + 8]] * reps, axis=1) for e in range(8)]
    return rows[:4], rows[4:]


def left_rows(rot, bright):
    (a_re, a_im), (c_re, c_im) = rot, bright
    out = []
    for i in range(2):
        re_rows, im_rows = [], []
        for l in range(2):
            re = im = None
            for k in range(2):
                ar, ai, cr, ci = a_re[2 * i + k], a_im[2 * i + k], c_re[2 * k + l], c_im[2 * k + l]
                tr, ti = ar * cr - ai * ci, ar * ci + ai * cr
                re, im = (tr, ti) if re is None else (re + tr, im + ti)
            re_rows.append(re)
            im_rows.append(im)
        out.append(jnp.concatenate(re_rows + im_rows, axis=0))
    return out


def right_rows(rot):
    a_re, a_im = rot
    real = [
        jnp.concatenate([a_re[2 * j], a_re[2 * j + 1], a_im[2 * j], a_im[2 * j + 1]], axis=0)
        for j in range(2)
    ]
    imag = [
        jnp.concatenate([-a_im[2 * j], -a_im[2 * j + 1], a_re[2 * j], a_re[2 * j + 1]], axis=0)
        for j in range(2)
    ]
    return real + imag


def field_gradient(h_left, h_right, bright, cosine, sine):
    c_re, c_im = bright
    g_re, g_im = [], []
    for i in range(2):
        for k in range(2):
            j = i
            re = h_right[j][8 * k : 8 * k + 8] + h_right[2 + j][16 + 8 * k : 24 + 8 * k]
            im = h_right[j][16 + 8 * k : 24 + 8 * k] - h_right[2 + j][8 * k : 8 * k + 8]
            for l in range(2):
                lr = h_left[i][8 * l : 8 * l + 8]
                li = h_left[i][16 + 8 * l : 24 + 8 * l]
                cr, ci = c_re[2 * k + l], c_im[2 * k + l]
                re = re + lr * cr + li * ci
                im = im + li * cr - lr * ci
            g_re.append(cosine * re + sine * im)
            g_im.append(cosine * im - sine * re)
    return jnp.concatenate(g_re + g_im, axis=0)


def coherency_tile(brightness, freq):
    spectral = jnp.exp(-SPECTRAL_INDEX * jnp.log(jnp.full((8, 128), freq, F32)))
    tiles = []
    for e in range(8):
        column = jnp.transpose(jnp.broadcast_to(brightness[e : e + 1, :], (8, 8)))[:, :1]
        tiles.append(column * spectral)
    return jnp.concatenate(tiles, axis=0)


def position_of(chan_count, offset=0):
    place = lax.axis_index("chan")
    if offset:
        place = place ^ offset
    return place.astype(F32) * (1.0 / chan_count)


def frequency_of(chan_count):
    return 1.0 + position_of(chan_count)


def basis_of(chan_count, offset=0):
    x = position_of(chan_count, offset) + 0.5 / chan_count
    y = 1.0 - x
    return [y * y * y, 3.0 * x * y * y, 3.0 * x * x * y, x * x * x]


def solve_of(chan_count, offset):
    basis = bernstein_np(chan_count)
    inverse = np.linalg.inv(basis.T @ basis)
    row = basis_of(chan_count, offset)
    return [sum(row[m] * float(inverse[m, k]) for m in range(4)) for k in range(4)]


def vmem_specs(count):
    return [pl.BlockSpec(memory_space=pltpu.VMEM)] * count


def smem_specs(count):
    return [pl.BlockSpec(memory_space=pltpu.SMEM)] * count


def params(limit=None):
    return pltpu.CompilerParams(vmem_limit_bytes=limit or VMEM_BYTES)


def shape(*dims, dtype=F32):
    return jax.ShapeDtypeStruct(dims, dtype)


def own_lanes(block):
    return pl.ds(pl.multiple_of(lax.axis_index("stn") * block, CHUNK), block)


def pair_blocks(pairs, pair):
    first, second = jnp.int32(0), jnp.int32(0)
    for k, (p, q) in enumerate(pairs):
        first = first + jnp.where(pair == k, p, 0)
        second = second + jnp.where(pair == k, q, 0)
    return first, second


def masks_kernel(masks):
    block = masks.shape[1]
    row = lax.broadcasted_iota(jnp.int32, (block, block), 0)
    col = lax.broadcasted_iota(jnp.int32, (block, block), 1)
    masks[0] = (row < col).astype(F32).astype(BF16)
    masks[1] = jnp.ones((block, block), BF16)


def baseline_masks(block):
    return pl.pallas_call(
        masks_kernel,
        name="baseline_masks",
        out_shape=shape(2, block, block, dtype=BF16),
        out_specs=vmem_specs(1)[0],
        compiler_params=params(),
        cost_estimate=COSTLY,
    )()


def rows_kernel(masks, gains, delays, ids, flags, rows):
    fields, stations = gains.shape[0] + delays.shape[0], gains.shape[2]
    rows[: gains.shape[0]] = gains[...]
    rows[gains.shape[0] : fields] = delays[...].reshape(delays.shape[0], 1, stations)
    rows[fields:] = jnp.full((2, 1, stations), -1.0, F32)
    slots = ids.shape[1]
    rows[fields, :, :slots] = ids[...].astype(F32)
    rows[fields + 1, :, :slots] = flags[...].astype(F32)


def field_rows(masks, gains, delays, ids, flags):
    return pl.pallas_call(
        rows_kernel,
        name="field_rows",
        out_shape=shape(gains.shape[0] + delays.shape[0] + 2, 1, gains.shape[2]),
        in_specs=vmem_specs(5),
        out_specs=vmem_specs(1)[0],
        compiler_params=params(),
        cost_estimate=COSTLY,
    )(masks, gains, delays, ids, flags)


def prepare_kernel(block, pairs, slots, penalty, chan_count, *refs):
    table, flags, duals, prior, bright, *refs = refs
    duals_out, start_out, coh_out, counts_out = refs
    lane = lax.broadcasted_iota(jnp.int32, (8, 128), 1)
    counts = jnp.zeros((8, 128), F32)
    for slot in range(slots):
        held_here = (lane == table[slot]) & (lane < len(pairs))
        counts = counts + jnp.where(held_here, flags[slot].astype(F32), 0.0)
    counts_out[...] = counts
    coh_out[...] = coherency_tile(bright[...], frequency_of(chan_count))
    duals_own = duals[:, 0, :]
    duals_out[...] = duals_own
    target = -duals_own
    for k, scale in enumerate(basis_of(chan_count)):
        target = target + scale * prior[:, k, :]
    start_out[...] = -penalty * target


def prepare(geometry, table, flags, duals, prior, brightness):
    block, pairs, dumps, penalty, chan_count, stations = geometry
    return pl.pallas_call(
        functools.partial(
            prepare_kernel, block, pairs, table.shape[0], penalty, chan_count
        ),
        name="prepare",
        out_shape=(
            shape(64, block),
            shape(64, block),
            shape(64, 128),
            shape(8, 128),
        ),
        in_specs=smem_specs(2) + vmem_specs(3),
        out_specs=tuple(vmem_specs(4)),
        compiler_params=params(),
        cost_estimate=pl.CostEstimate(flops=1000000, bytes_accessed=2000000, transcendentals=0),
    )(table, flags, duals, prior, brightness)


def data_kernel(block, pairs, dumps, slots, penalty, chan_count, first_call, joined, *refs):
    table, flags, observed, coh_ref, keep, *refs = refs
    if first_call:
        if joined:
            rows_all, *refs = refs
        else:
            rows_mine, rows_other, *refs = refs
        start, counts_mine, out_ref, field_ref, delay_ref, counts_ref, lead, *refs = refs
    else:
        lead, field_ref, delay_ref, out_ref, *refs = refs
    if first_call:
        order, xp, yp, hl, ha = refs
    else:
        held, sems, order, xp, yp, hl, ha = refs
    stations = field_ref.shape[1]
    pair_count = len(pairs)
    at_own = own_lanes(block)

    live_count = jnp.int32(0)
    for slot in range(slots):
        order[live_count] = jnp.int32(slot)
        live_count = live_count + jnp.where(table[slot] < pair_count, 1, 0)
    items = live_count * dumps

    def copy_of(item):
        slot, t = order[item // dumps], item % dumps
        return pltpu.make_async_copy(observed.at[slot, t], held.at[item], sems.at[item])

    freq_value = frequency_of(chan_count)
    if first_call:
        if joined:
            rows_other = rows_all
            field_ref[...] = rows_all[:64, 0, :]
            delay_ref[...] = rows_all[64 : 64 + 8 * dumps, 0, :]
        else:
            at_other = pl.ds(pl.multiple_of((1 - lax.axis_index("stn")) * block, CHUNK), block)
            for at, rows in ((at_own, rows_mine), (at_other, rows_other)):
                field_ref[:, at] = rows[:64, 0, :]
                delay_ref[:, at] = rows[64 : 64 + 8 * dumps, 0, :]
    bright = coherency_rows(coh_ref[...], stations)
    for t in range(dumps):
        cosine, sine = trig(delay_ref[8 * t : 8 * t + 8, :], freq_value)
        rot = rotate(field_ref[...], cosine, sine)
        for i, rows in enumerate(left_rows(rot, bright)):
            xp[t, i] = pack(rows)
        for rj, rows in enumerate(right_rows(rot)):
            yp[t, rj] = pack(rows)
    if not first_call:
        for item in range(1, min(1 + AHEAD, slots * dumps)):

            @pl.when(item < items)
            def _():
                copy_of(jnp.int32(item)).start()

    hl[...] = jnp.zeros_like(hl)
    ha[...] = jnp.zeros_like(ha)

    lane = lax.broadcasted_iota(jnp.int32, (1, block), 1)

    def visit(item, tiles):
        slot, t = order[item // dumps], item % dumps
        first, second = pair_blocks(pairs, table[slot])
        kept = keep[jnp.where(first < second, 1, 0)]
        live = (lane >= flags[slot]).astype(F32)
        live16 = live.astype(BF16)
        at_p = pl.ds(pl.multiple_of(first * block, CHUNK), block)
        at_q = pl.ds(pl.multiple_of(second * block, CHUNK), block)
        acc_left = [None, None]
        acc_right = [None] * 4
        xs = [xp[t, i, :, at_p] * live16 for i in range(2)]
        ys = [yp[t, rj, :, at_q] for rj in range(4)]
        for r in range(2):
            for i in range(2):
                for j in range(2):
                    tile = tiles[4 * r + 2 * i + j] * kept
                    rj = 2 * r + j
                    left = dot(ys[rj], tile, NT)
                    right = dot(xs[i], tile, NN)
                    acc_left[i] = left if acc_left[i] is None else acc_left[i] + left
                    acc_right[rj] = right if acc_right[rj] is None else acc_right[rj] + right
        for i in range(2):
            hl[t, i, :, at_p] += (acc_left[i][:32] + acc_left[i][32:]) * live
        for rj in range(4):
            ha[t, rj, :, at_q] += acc_right[rj][:32] + acc_right[rj][32:]

    def visit_held(item, unused):
        copy_of(item).wait()

        @pl.when(item + AHEAD < items)
        def _():
            copy_of(item + AHEAD).start()

        visit(item, held.at[item])
        return unused

    def visit_there(item, unused):
        visit(item, observed.at[order[item // dumps], item % dumps])
        return unused

    if first_call:
        lax.fori_loop(0, items, visit_there, jnp.int32(0))

        @pl.when(items > 0)
        def _():
            lead[...] = observed[order[0], 0]
    else:

        @pl.when(items > 0)
        def _():
            visit(jnp.int32(0), lead)

        lax.fori_loop(1, items, visit_held, jnp.int32(0))

    total = None
    for t in range(dumps):
        cosine, sine = trig(delay_ref[8 * t : 8 * t + 8, :], freq_value)
        piece = field_gradient(
            [hl[t, i] for i in range(2)], [ha[t, rj] for rj in range(4)], bright, cosine, sine
        )
        total = piece if total is None else total + piece
    out_ref[...] = -total
    prior = penalty * field_ref[:, at_own]
    if first_call:
        prior = prior + start[...]
        counts = counts_mine[...]
        ids_other, flags_other = rows_other[64 + 8 * dumps], rows_other[65 + 8 * dumps]
        pair_lane = lax.broadcasted_iota(jnp.int32, (8, 128), 1)
        for k in range(pair_count):
            theirs = jnp.where(ids_other == float(k), flags_other, 0.0)
            total_flags = jnp.sum(theirs, axis=1, keepdims=True)
            counts = counts + jnp.where(pair_lane == k, total_flags, 0.0)
        counts_ref[...] = counts
    out_ref[:, at_own] += prior


def data_part(geometry, table, flags, observed, coh, masks, fields):
    block, pairs, dumps, penalty, chan_count, stations = geometry
    slots = observed.shape[0]
    first_call = len(fields[0].shape) == 3 and fields[0].dtype == F32
    joined = len(fields) == 3
    body = functools.partial(
        data_kernel, block, pairs, dumps, slots, penalty, chan_count, first_call, joined
    )
    shapes = [shape(64, stations)]
    if first_call:
        shapes += [shape(64, stations), shape(8 * dumps, stations), shape(8, 128)]
        shapes.append(shape(*observed.shape[2:], dtype=BF16))
        place, copies = vmem_specs(1), []
    else:
        place = [pl.BlockSpec(memory_space=pl.ANY)]
        copies = [
            pltpu.VMEM((slots * dumps,) + observed.shape[2:], BF16),
            pltpu.SemaphoreType.DMA((slots * dumps,)),
        ]
    return pl.pallas_call(
        body,
        name="data_part",
        out_shape=tuple(shapes),
        in_specs=smem_specs(2) + place + vmem_specs(2 + len(fields)),
        out_specs=tuple(vmem_specs(len(shapes))),
        scratch_shapes=copies
        + [
            pltpu.SMEM((slots,), jnp.int32),
            pltpu.VMEM((dumps, 2, 64, stations), BF16),
            pltpu.VMEM((dumps, 4, 64, stations), BF16),
            pltpu.VMEM((dumps, 2, 32, stations), F32),
            pltpu.VMEM((dumps, 4, 32, stations), F32),
        ],
        compiler_params=params() if first_call else params(COPY_BYTES),
        cost_estimate=pl.CostEstimate(
            flops=6000000000, bytes_accessed=8000000, transcendentals=0
        ),
    )(table, flags, observed, coh, masks, *fields)


def fold_gram(high_low, other, rows):
    wide = dot(high_low, other[:rows], NT)
    return wide[:rows] + wide[rows:] + dot(high_low[:rows], other[rows:], NT)


def apply_gram(gram, packed, rows):
    size = gram.shape[0]
    both = pack(gram)
    factors = jnp.concatenate([both[:size], both[size:], both[:size]], axis=1)
    return dot(factors, jnp.concatenate([packed[:rows], packed], axis=0), NN)


def lanes(parts, start, size):
    return jnp.concatenate([part[:, start : start + size] for part in parts], axis=1)


def twice(mask):
    return jnp.concatenate([mask, mask], axis=1)


class Chunks:
    def __init__(self, block, stations, pairs, counts):
        self.block = block
        self.size = min(CHUNK, block)
        self.per_block = block // self.size
        self.count = stations // self.size
        self.blocks = stations // block
        lane = lax.broadcasted_iota(jnp.int32, (1, block), 1).astype(F32)
        self.masks = {
            pair: (lane >= counts[:, k : k + 1]).astype(F32) for k, pair in enumerate(pairs)
        }
        row = lax.broadcasted_iota(jnp.int32, (self.size, self.size), 0)
        col = lax.broadcasted_iota(jnp.int32, (self.size, self.size), 1)
        self.upper = row < col

    def kept(self, values):
        n = self.size
        return jnp.concatenate(
            [
                jnp.concatenate(
                    [
                        jnp.where(self.upper, values[i : i + n, j : j + n], 0.0)
                        for j in range(0, 4 * n, n)
                    ],
                    axis=1,
                )
                for i in range(0, 2 * n, n)
            ],
            axis=0,
        )

    def mask(self, pair, chunk):
        start = (chunk % self.per_block) * self.size
        return twice(self.masks[pair][:, start : start + self.size])

    def own_pair(self, chunk):
        return (chunk // self.per_block, chunk // self.per_block)

    def rect_terms(self, chunk):
        own = chunk // self.per_block
        terms = []
        inside = list(range(chunk + 1, (own + 1) * self.per_block))
        if inside:
            terms.append(((own, own), inside))
        for q in range(own + 1, self.blocks):
            terms.append(((own, q), list(range(q * self.per_block, (q + 1) * self.per_block))))
        return terms


def sum_of(parts):
    total = parts[0]
    for part in parts[1:]:
        total = total + part
    return total


def halves(rows, axis, odd):
    size = rows.shape[axis] // 2
    low = lax.slice_in_dim(rows, 0, size, axis=axis)
    high = lax.slice_in_dim(rows, size, 2 * size, axis=axis)
    return jnp.where(odd, high, low), jnp.where(odd, low, high)


def store_eighths(fields, sums, outs):
    place = lax.axis_index("chan")
    odd_lanes, odd_low, odd_high = place % 2 == 1, (place // 2) % 2 == 1, (place // 4) % 2 == 1
    for n, field in enumerate(fields):
        for out, part in zip(outs, halves(field, 1, odd_lanes)):
            for high, half in enumerate(halves(part, 0, odd_high)):
                for low, rows in enumerate(halves(half, 0, odd_low)):
                    at = 32 * (2 * high + low) + 16 * n
                    out[at : at + 16, :] = rows
    for out in outs:
        out[128:, :] = sums


def step_length(grad_sq, curvature, penalty):
    return grad_sq / (curvature + penalty * grad_sq + EPSILON)


def gradient_kernel(block, pairs, dumps, penalty, chan_count, update, *refs):
    counts_ref, delay_ref, coh_ref, current_ref, *refs = refs
    if update:
        sums_ref, direction_ref, *refs = refs
    gradient_out, *refs = refs
    if update:
        current_out, alpha_out, *refs = refs
    xp, yp, hl, ha = refs
    stations = current_ref.shape[1]
    chunks = Chunks(block, stations, pairs, counts_ref[0:1, :])
    size = chunks.size

    current = current_ref[...]
    if update:
        sums = jnp.sum(sums_ref[...], axis=0, keepdims=True)
        alpha = step_length(sums[:, 0:1], sums[:, 1:2], penalty)
        alpha_out[...] = jnp.broadcast_to(alpha, (8, 128))
        current = current - alpha * direction_ref[...]
        current_out[...] = current
    freq_value = frequency_of(chan_count)
    bright = coherency_rows(coh_ref[...], stations)
    gradient = None
    for t in range(dumps):
        cosine, sine = trig(delay_ref[8 * t : 8 * t + 8, :], freq_value)
        rot = rotate(current, cosine, sine)
        xs = [pack(v) for v in left_rows(rot, bright)]
        ys = [pack(v) for v in right_rows(rot)]
        for i in range(2):
            xp[t, i] = xs[i]
        for rj in range(4):
            yp[t, rj] = ys[rj]
        gram_y = [
            fold_gram(lanes(ys, c * size, size), lanes(ys, c * size, size), 32)
            for c in range(chunks.count)
        ]
        sums_x = [None] * chunks.count
        for c in range(chunks.count):
            xc = lanes(xs, c * size, size)
            yc = lanes(ys, c * size, size)
            xw = xc * chunks.mask(chunks.own_pair(c), c).astype(BF16)
            yn = jnp.concatenate([yc[:32], yc[:32], yc[32:], yc[32:]], axis=0)
            model = dot(jnp.concatenate([xw, xw], axis=0), yn, TN)
            model = chunks.kept(model)
            high, low = split(model)
            left = dot(yc, high, NT) + dot(yc, low, NT)
            right = dot(
                jnp.concatenate([xw, xw], axis=1), jnp.concatenate([high, low], axis=0), NN
            )
            left = left[:32] + left[32:]
            right = right[:32] + right[32:]
            for pair, others in chunks.rect_terms(c):
                mask = chunks.mask(pair, c)
                left = left + apply_gram(sum_of([gram_y[o] for o in others]), xc, 32) * mask
                gram_x = fold_gram(xc * mask.astype(BF16), xc, 32)
                for o in others:
                    sums_x[o] = gram_x if sums_x[o] is None else sums_x[o] + gram_x
            if sums_x[c] is not None:
                right = right + apply_gram(sums_x[c], yc, 32)
            for i in range(2):
                hl[i, :, c * size : (c + 1) * size] = left[:, i * size : (i + 1) * size]
            for rj in range(4):
                ha[rj, :, c * size : (c + 1) * size] = right[:, rj * size : (rj + 1) * size]
        piece = field_gradient(
            [hl[i] for i in range(2)], [ha[rj] for rj in range(4)], bright, cosine, sine
        )
        gradient = piece if gradient is None else gradient + piece
    gradient_out[...] = gradient


def gradient_part(geometry, counts, delays, coh, current, step):
    block, pairs, dumps, penalty, chan_count, stations = geometry
    update = step is not None
    field = shape(64, stations)
    outs = [field]
    inputs = [counts, delays, coh, current]
    if update:
        inputs += step
        outs += [field, shape(8, 128)]
    outs += [shape(dumps, rows, 64, stations, dtype=BF16) for rows in (2, 4)]
    return pl.pallas_call(
        functools.partial(gradient_kernel, block, pairs, dumps, penalty, chan_count, update),
        name="gradient_part",
        out_shape=tuple(outs),
        in_specs=vmem_specs(len(inputs)),
        out_specs=tuple(vmem_specs(len(outs))),
        scratch_shapes=[pltpu.VMEM((2, 32, stations), F32), pltpu.VMEM((4, 32, stations), F32)],
        compiler_params=params(),
        cost_estimate=pl.CostEstimate(
            flops=4000000000, bytes_accessed=2000000, transcendentals=0
        ),
    )(*inputs)


def curvature_kernel(block, pairs, dumps, penalty, chan_count, update, last, *refs):
    counts_ref, delay_ref, coh_ref, xp, yp, gradient_ref, mine_ref, theirs_ref, *refs = refs
    if update:
        alpha_ref, linear_ref, *refs = refs
    if last:
        duals_ref, current_ref, *refs = refs
    direction_out, *refs = refs
    if not last:
        linear_out, sums_out = refs
    stations = mine_ref.shape[1]
    chunks = Chunks(block, stations, pairs, counts_ref[0:1, :])
    size = chunks.size

    linear = mine_ref[...] + theirs_ref[...]
    if update:
        linear = linear_ref[...] - alpha_ref[0:1, 0:1] * linear
    direction = linear + gradient_ref[...]
    direction_out[...] = direction
    if not last:
        linear_out[...] = linear

    freq_value = frequency_of(chan_count)
    bright = coherency_rows(coh_ref[...], stations)
    squares = jnp.zeros((8, 4 * size), F32)
    grams = jnp.zeros((64, 64), F32)
    if last:
        visited, repeats, copies = range(dumps), 1, 1
    else:
        stn_count = stations // block
        shared = stn_count % dumps == 0
        visited = [lax.axis_index("stn") % dumps] if shared else range(dumps)
        repeats, copies = (stn_count // dumps if shared else stn_count), stn_count
    for t in visited:
        delay = delay_ref[pl.ds(pl.multiple_of(8 * t, 8), 8), :]
        cosine, sine = trig(delay, freq_value)
        step = rotate(direction, cosine, sine)
        xs = [xp[t, i] for i in range(2)]
        ys = [yp[t, rj] for rj in range(4)]
        dxs = [pack(v) for v in left_rows(step, bright)]
        dys = [pack(v) for v in right_rows(step)]

        def stacked(first, second, c):
            one = lanes(first, c * size, size)
            two = lanes(second, c * size, size)
            return jnp.concatenate([one[:32], two[:32], one[32:], two[32:]], axis=0)

        gram_y = [None] * chunks.count
        for c in range(chunks.count):
            xc = stacked(dxs, xs, c)
            yc = stacked(ys, dys, c)
            xw = xc * chunks.mask(chunks.own_pair(c), c).astype(BF16)
            tangent = dot(
                jnp.concatenate([xw, xw], axis=0),
                jnp.concatenate([yc[:64], yc[:64], yc[64:], yc[64:]], axis=0),
                TN,
            )
            tangent = chunks.kept(tangent)
            square = tangent * tangent
            squares = squares + jnp.sum(square.reshape(2 * size // 8, 8, 4 * size), axis=0)
            if c > 0:
                gram_y[c] = fold_gram(yc, yc, 64)
        for c in range(chunks.count):
            for pair, others in chunks.rect_terms(c):
                xc = stacked(dxs, xs, c)
                gram_x = fold_gram(xc * chunks.mask(pair, c).astype(BF16), xc, 64)
                grams = grams + sum_of([gram_y[o] for o in others]) * gram_x
    curvature = jnp.sum(squares, keepdims=True) + jnp.sum(grams, keepdims=True)
    grad_sq = jnp.sum(direction * direction, keepdims=True)
    grad_sq = grad_sq * (1.0 / copies)
    curvature = curvature * (1.0 / repeats)
    rows = 8 if last else chan_count * copies
    lane = lax.broadcasted_iota(jnp.int32, (rows, block // 2 if last else 128), 1)
    sums = jnp.where(lane == 0, grad_sq, jnp.where(lane == 1, curvature, 0.0))
    if last:
        base = current_ref[:, own_lanes(block)] + duals_ref[...]
        store_eighths((base, direction_out[:, own_lanes(block)]), sums, refs)
    else:
        sums_out[...] = sums


def curvature_part(geometry, counts, delays, coh, factors, gradient, shares, before, last):
    block, pairs, dumps, penalty, chan_count, stations = geometry
    update = before is not None
    field = shape(64, stations)
    if last is not None:
        outs = [field] + [shape(136, block // 2)] * 2
    else:
        outs = [field, field, shape(chan_count * (stations // block), 128)]
    inputs = [counts, delays, coh, *factors, gradient, *shares]
    if update:
        inputs += before
    if last is not None:
        inputs += last
    return pl.pallas_call(
        functools.partial(
            curvature_kernel, block, pairs, dumps, penalty, chan_count, update, last is not None
        ),
        name="curvature_part",
        out_shape=tuple(outs),
        in_specs=vmem_specs(len(inputs)),
        out_specs=tuple(vmem_specs(len(outs))),
        compiler_params=params(),
        cost_estimate=pl.CostEstimate(
            flops=2000000000, bytes_accessed=2000000, transcendentals=0
        ),
    )(*inputs)


def regroup_kernel(mine, theirs, *outs):
    for o, out in enumerate(outs):
        out[:32, :] = mine[32 * o : 32 * o + 32, :]
        out[32:64, :] = theirs[32 * o : 32 * o + 32, :]
        out[64:, :] = mine[128:, :] + theirs[128:, :]


def regroup(mine, theirs):
    return pl.pallas_call(
        regroup_kernel,
        name="regroup",
        out_shape=(shape(72, mine.shape[1]),) * 4,
        in_specs=vmem_specs(2),
        out_specs=tuple(vmem_specs(4)),
        compiler_params=params(),
    )(mine, theirs)


def sum_in_pairs(terms):
    return (terms[0] + terms[1]) + (terms[2] + terms[3])


def weigh_kernel(chan_count, *refs):
    *parts, out = refs
    scales = [solve_of(chan_count, offset) for offset in range(8)]
    for n in range(2):
        for k in range(4):
            terms = []
            for o, part in enumerate(parts):
                one = part[16 * n : 16 * n + 16, :]
                two = part[32 + 16 * n : 48 + 16 * n, :]
                terms.append(scales[2 * o][k] * one + scales[2 * o + 1][k] * two)
            at = 64 * n + 16 * k
            out[at : at + 16, :] = sum_in_pairs(terms)
    out[128:, :] = sum_in_pairs([part[64:, :] for part in parts])


def weigh(geometry, parts):
    chan_count = geometry[4]
    return pl.pallas_call(
        functools.partial(weigh_kernel, chan_count),
        name="weigh",
        out_shape=shape(136, parts[0].shape[1]),
        in_specs=vmem_specs(4),
        out_specs=vmem_specs(1)[0],
        compiler_params=params(),
    )(*parts)


def combine_kernel(penalty, one, two, coeffs_out, alpha_out):
    total = one[...] + two[...]
    alpha = step_length(total[128:129, 0:1], total[128:129, 1:2], penalty)
    coeffs_out[...] = total[:64] - alpha * total[64:128]
    alpha_out[...] = jnp.broadcast_to(alpha, (8, 128))


def combine(geometry, one, two):
    penalty = geometry[3]
    return pl.pallas_call(
        functools.partial(combine_kernel, penalty),
        name="combine",
        out_shape=(shape(64, one.shape[1]), shape(8, 128)),
        in_specs=vmem_specs(2),
        out_specs=tuple(vmem_specs(2)),
        compiler_params=params(),
    )(one, two)


def last_step_kernel(block, alpha, current, direction, duals, gains_out, shifted_out):
    at_own = own_lanes(block)
    gains_new = current[:, at_own] - alpha[0:1, 0:1] * direction[:, at_own]
    gains_out[:, 0, :] = gains_new
    shifted_out[:, 0, :] = gains_new + duals[...]


def last_step(geometry, *inputs):
    block = geometry[0]
    return pl.pallas_call(
        functools.partial(last_step_kernel, block),
        name="last_step",
        out_shape=(shape(64, 1, block), shape(64, 1, block)),
        in_specs=vmem_specs(len(inputs)),
        out_specs=tuple(vmem_specs(2)),
        compiler_params=params(),
    )(*inputs)


def consensus_kernel(chan_count, mine, theirs, shifted, coeffs_out, duals_out):
    place = lax.axis_index("chan")
    odd = place % 2 == 1
    for o in range(4):
        rows = pl.ds((((place // 2) % 4) ^ o) * 16, 16)
        fitted = None
        for k, scale in enumerate(basis_of(chan_count)):
            at = slice(64 * o + 16 * k, 64 * o + 16 * k + 16)
            one, two = mine[at, :], theirs[at, :]
            coeffs = jnp.concatenate([jnp.where(odd, two, one), jnp.where(odd, one, two)], axis=1)
            coeffs_out[rows, k, :] = coeffs
            fitted = scale * coeffs if fitted is None else fitted + scale * coeffs
        duals_out[rows, 0, :] = shifted[rows, 0, :] - fitted


def consensus(geometry, *inputs):
    block, pairs, dumps, penalty, chan_count, stations = geometry
    return pl.pallas_call(
        functools.partial(consensus_kernel, chan_count),
        name="consensus",
        out_shape=(shape(64, 4, block), shape(64, 1, block)),
        in_specs=vmem_specs(len(inputs)),
        out_specs=tuple(vmem_specs(2)),
        compiler_params=params(),
    )(*inputs)


def swap(value, count, offset):
    return lax.ppermute(value, "chan", [(i, i ^ offset) for i in range(count)])


def other_stations(value):
    return lax.ppermute(value, "stn", [(0, 1), (1, 0)])


def both_stations(value, count):
    if count == 2:
        return value, other_stations(value)
    return jnp.zeros_like(value), lax.psum(value, "stn")


def shards(observed, pair_table, flag_rows, gains, duals, prior_coeffs, delays, brightness):
    stn_count = lax.axis_size("stn")
    chan_count = lax.axis_size("chan")
    entries, dirs, chan_local, block = gains.shape
    slots, dumps = observed.shape[0], observed.shape[2]
    stations = block * stn_count
    pairs = pair_lists(stn_count)
    penalty = stations * dumps / 16.0
    geometry = (block, pairs, dumps, penalty, chan_count, stations)

    observed = observed.reshape((slots,) + observed.shape[2:])
    duals_raw = duals.reshape(entries * dirs, 1, block)
    prior = prior_coeffs.reshape(entries * dirs, 4, block)
    masks = baseline_masks(block)
    rows = field_rows(
        masks,
        gains.reshape(entries * dirs, 1, block),
        delays.reshape(dumps * dirs, block),
        pair_table.reshape(1, slots),
        flag_rows.reshape(1, slots),
    )
    if stn_count == 2:
        fields = (rows, other_stations(rows))
    else:
        fields = (lax.all_gather(rows, "stn", axis=2, tiled=True),)
    duals_own, start, coh, counts = prepare(
        geometry, pair_table, flag_rows, duals_raw, prior, brightness
    )
    if stn_count != 2:
        counts = jnp.zeros_like(counts)
    data = functools.partial(data_part, geometry, pair_table, flag_rows, observed, coh, masks)
    share, current, delay_all, counts, lead = data(fields + (start, counts))
    shares = both_stations(share, stn_count)

    step = before = None
    for iteration in range(ITERS):
        last = iteration + 1 == ITERS
        gradient, *rest = gradient_part(geometry, counts, delay_all, coh, current, step)
        if step is not None:
            current, alpha, *rest = rest
            before = (alpha, linear)
        direction, *rest = curvature_part(
            geometry,
            counts,
            delay_all,
            coh,
            rest,
            gradient,
            shares,
            before,
            (duals_own, current) if last else None,
        )
        if not last:
            linear, sums = rest
            sums = lax.all_to_all(sums, ("chan", "stn"), 0, 0, tiled=True)
            (share,) = data((lead, direction, delay_all))
            shares = both_stations(share, stn_count)
            step = (sums, direction)

    keep, send = rest
    own, *others = regroup(keep, swap(send, chan_count, 1))
    parts = [own] + [swap(part, chan_count, 2 + 2 * o) for o, part in enumerate(others)]
    value, bit = weigh(geometry, parts), 8
    other = swap(value, chan_count, bit)
    while 2 * bit < chan_count:
        value, bit = value + other, 2 * bit
        other = swap(value, chan_count, bit)
    rows, alpha = combine(geometry, value, other)
    gains_new, shifted = last_step(geometry, alpha, current, direction, duals_own)
    mine = jnp.concatenate([rows] + [swap(rows, chan_count, o) for o in (2, 4, 6)])
    coeffs, duals_new = consensus(geometry, mine, swap(mine, chan_count, 1), shifted)
    return (
        gains_new.reshape(gains.shape),
        coeffs.reshape(entries, dirs, 4, block),
        duals_new.reshape(gains.shape),
    )


def solution(mesh):
    return jax.shard_map(
        shards,
        mesh=mesh,
        in_specs=(
            P("stn", ("band", "chan"), None, None, None, None),
            P("stn"),
            P("stn"),
            P(None, None, ("band", "chan"), "stn"),
            P(None, None, ("band", "chan"), "stn"),
            P("band", None, None, "stn"),
            P(None, None, "stn"),
            P("band", None),
        ),
        out_specs=(
            P(None, None, ("band", "chan"), "stn"),
            P("band", None, None, "stn"),
            P(None, None, ("band", "chan"), "stn"),
        ),
        check_vma=False,
    )
```

```python
import functools
import math

import jax
import jax.numpy as jnp
import numpy as np
from jax import lax
from jax.experimental import pallas as pl
from jax.experimental.pallas import tpu as pltpu
from jax.sharding import PartitionSpec as P

ITERS = 3
EPSILON = 1e-06
SPECTRAL_INDEX = 0.7
DIRS = 8
CHUNK = 128
VMEM_BYTES = 24 * 1024 * 1024
COPY_BYTES = 48 * 1024 * 1024
AHEAD = 2
F32 = jnp.float32
BF16 = jnp.bfloat16

COSTLY = pl.CostEstimate(flops=20000000000, bytes_accessed=20000000, transcendentals=0)

NT = (((1,), (1,)), ((), ()))
NN = (((1,), (0,)), ((), ()))
TN = (((0,), (0,)), ((), ()))


def dot(lhs, rhs, dims):
    return lax.dot_general(lhs, rhs, dims, preferred_element_type=F32)


def pair_lists(station_blocks):
    return [(p, q) for p in range(station_blocks) for q in range(p, station_blocks)]


def bernstein_np(total_channels):
    position = (np.arange(total_channels, dtype=np.float64) + 0.5) / total_channels
    others = 1.0 - position
    return np.stack(
        [others**3, 3.0 * position * others**2, 3.0 * position**2 * others, position**3], axis=1
    )


def split(x):
    high = x.astype(BF16)
    return high, (x - high.astype(F32)).astype(BF16)


def pack(x):
    high, low = split(x)
    return jnp.concatenate([high, low], axis=0)


def trig(delay, freq):
    turns = delay * freq
    turns = turns - jnp.floor(turns + 0.5)
    x = turns * math.pi
    x2 = x * x
    sin_half = x * (
        1.0
        + x2
        * (
            -1.0 / 6
            + x2
            * (
                1.0 / 120
                + x2
                * (
                    -1.0 / 5040
                    + x2 * (1.0 / 362880 + x2 * (-1.0 / 39916800 + x2 * (1.0 / 6227020800)))
                )
            )
        )
    )
    cos_half = 1.0 + x2 * (
        -0.5
        + x2
        * (
            1.0 / 24
            + x2
            * (
                -1.0 / 720
                + x2
                * (
                    1.0 / 40320
                    + x2 * (-1.0 / 3628800 + x2 * (1.0 / 479001600 + x2 * (-1.0 / 87178291200)))
                )
            )
        )
    )
    return 1.0 - 2.0 * sin_half * sin_half, 2.0 * sin_half * cos_half


def turned(turns_ref, t):
    dumps = turns_ref.shape[0] // 16

    def rows(n):
        return turns_ref[pl.ds(n if isinstance(n, int) else pl.multiple_of(n, 8), 8), :]

    return rows(8 * t), rows(8 * (t + dumps))


def rotate(field, cosine, sine):
    re = [field[8 * m : 8 * m + 8] for m in range(4)]
    im = [field[32 + 8 * m : 40 + 8 * m] for m in range(4)]
    return (
        [cosine * re[m] - sine * im[m] for m in range(4)],
        [cosine * im[m] + sine * re[m] for m in range(4)],
    )


def coherency_rows(coh, width):
    reps = width // coh.shape[1]
    rows = [jnp.concatenate([coh[8 * e : 8 * e + 8]] * reps, axis=1) for e in range(8)]
    return rows[:4], rows[4:]


def left_rows(rot, bright):
    (a_re, a_im), (c_re, c_im) = rot, bright
    out = []
    for i in range(2):
        re_rows, im_rows = [], []
        for l in range(2):
            re = im = None
            for k in range(2):
                ar, ai, cr, ci = a_re[2 * i + k], a_im[2 * i + k], c_re[2 * k + l], c_im[2 * k + l]
                tr, ti = ar * cr - ai * ci, ar * ci + ai * cr
                re, im = (tr, ti) if re is None else (re + tr, im + ti)
            re_rows.append(re)
            im_rows.append(im)
        out.append(jnp.concatenate(re_rows + im_rows, axis=0))
    return out


def right_rows(rot):
    a_re, a_im = rot
    real = [
        jnp.concatenate([a_re[2 * j], a_re[2 * j + 1], a_im[2 * j], a_im[2 * j + 1]], axis=0)
        for j in range(2)
    ]
    imag = [
        jnp.concatenate([-a_im[2 * j], -a_im[2 * j + 1], a_re[2 * j], a_re[2 * j + 1]], axis=0)
        for j in range(2)
    ]
    return real + imag


def field_gradient(h_left, h_right, bright, cosine, sine):
    c_re, c_im = bright
    g_re, g_im = [], []
    for i in range(2):
        for k in range(2):
            j = i
            re = h_right[j][8 * k : 8 * k + 8] + h_right[2 + j][16 + 8 * k : 24 + 8 * k]
            im = h_right[j][16 + 8 * k : 24 + 8 * k] - h_right[2 + j][8 * k : 8 * k + 8]
            for l in range(2):
                lr = h_left[i][8 * l : 8 * l + 8]
                li = h_left[i][16 + 8 * l : 24 + 8 * l]
                cr, ci = c_re[2 * k + l], c_im[2 * k + l]
                re = re + lr * cr + li * ci
                im = im + li * cr - lr * ci
            g_re.append(cosine * re + sine * im)
            g_im.append(cosine * im - sine * re)
    return jnp.concatenate(g_re + g_im, axis=0)


def coherency_tile(brightness, freq):
    spectral = jnp.exp(-SPECTRAL_INDEX * jnp.log(jnp.full((8, 128), freq, F32)))
    tiles = []
    for e in range(8):
        column = jnp.transpose(jnp.broadcast_to(brightness[e : e + 1, :], (8, 8)))[:, :1]
        tiles.append(column * spectral)
    return jnp.concatenate(tiles, axis=0)


def position_of(chan_count, offset=0):
    place = lax.axis_index("chan")
    if offset:
        place = place ^ offset
    return place.astype(F32) * (1.0 / chan_count)


def frequency_of(chan_count):
    return 1.0 + position_of(chan_count)


def basis_of(chan_count, offset=0):
    x = position_of(chan_count, offset) + 0.5 / chan_count
    y = 1.0 - x
    return [y * y * y, 3.0 * x * y * y, 3.0 * x * x * y, x * x * x]


def solve_of(chan_count, offset):
    basis = bernstein_np(chan_count)
    inverse = np.linalg.inv(basis.T @ basis)
    row = basis_of(chan_count, offset)
    return [sum(row[m] * float(inverse[m, k]) for m in range(4)) for k in range(4)]


def vmem_specs(count):
    return [pl.BlockSpec(memory_space=pltpu.VMEM)] * count


def smem_specs(count):
    return [pl.BlockSpec(memory_space=pltpu.SMEM)] * count


def params(limit=None):
    return pltpu.CompilerParams(vmem_limit_bytes=limit or VMEM_BYTES)


def shape(*dims, dtype=F32):
    return jax.ShapeDtypeStruct(dims, dtype)


def own_lanes(block):
    return pl.ds(pl.multiple_of(lax.axis_index("stn") * block, CHUNK), block)


def pair_blocks(pairs, pair):
    first, second = jnp.int32(0), jnp.int32(0)
    for k, (p, q) in enumerate(pairs):
        first = first + jnp.where(pair == k, p, 0)
        second = second + jnp.where(pair == k, q, 0)
    return first, second


def masks_kernel(masks):
    block = masks.shape[1]
    row = lax.broadcasted_iota(jnp.int32, (block, block), 0)
    col = lax.broadcasted_iota(jnp.int32, (block, block), 1)
    masks[0] = (row < col).astype(F32).astype(BF16)
    masks[1] = jnp.ones((block, block), BF16)


def baseline_masks(block):
    return pl.pallas_call(
        masks_kernel,
        name="baseline_masks",
        out_shape=shape(2, block, block, dtype=BF16),
        out_specs=vmem_specs(1)[0],
        compiler_params=params(),
        cost_estimate=COSTLY,
    )()


def rows_kernel(masks, gains, delays, ids, flags, rows):
    fields, stations = gains.shape[0] + delays.shape[0], gains.shape[2]
    rows[: gains.shape[0]] = gains[...]
    rows[gains.shape[0] : fields] = delays[...].reshape(delays.shape[0], 1, stations)
    rows[fields:] = jnp.full((2, 1, stations), -1.0, F32)
    slots = ids.shape[1]
    rows[fields, :, :slots] = ids[...].astype(F32)
    rows[fields + 1, :, :slots] = flags[...].astype(F32)


def field_rows(masks, gains, delays, ids, flags):
    return pl.pallas_call(
        rows_kernel,
        name="field_rows",
        out_shape=shape(gains.shape[0] + delays.shape[0] + 2, 1, gains.shape[2]),
        in_specs=vmem_specs(5),
        out_specs=vmem_specs(1)[0],
        compiler_params=params(),
        cost_estimate=COSTLY,
    )(masks, gains, delays, ids, flags)


def prepare_kernel(block, pairs, slots, penalty, chan_count, *refs):
    table, flags, duals, prior, bright, *refs = refs
    duals_out, start_out, coh_out, counts_out = refs
    lane = lax.broadcasted_iota(jnp.int32, (8, 128), 1)
    counts = jnp.zeros((8, 128), F32)
    for slot in range(slots):
        held_here = (lane == table[slot]) & (lane < len(pairs))
        counts = counts + jnp.where(held_here, flags[slot].astype(F32), 0.0)
    counts_out[...] = counts
    coh_out[...] = coherency_tile(bright[...], frequency_of(chan_count))
    duals_own = duals[:, 0, :]
    duals_out[...] = duals_own
    target = -duals_own
    for k, scale in enumerate(basis_of(chan_count)):
        target = target + scale * prior[:, k, :]
    start_out[...] = -penalty * target


def prepare(geometry, table, flags, duals, prior, brightness):
    block, pairs, dumps, penalty, chan_count, stations = geometry
    return pl.pallas_call(
        functools.partial(
            prepare_kernel, block, pairs, table.shape[0], penalty, chan_count
        ),
        name="prepare",
        out_shape=(
            shape(64, block),
            shape(64, block),
            shape(64, 128),
            shape(8, 128),
        ),
        in_specs=smem_specs(2) + vmem_specs(3),
        out_specs=tuple(vmem_specs(4)),
        compiler_params=params(),
        cost_estimate=pl.CostEstimate(flops=1000000, bytes_accessed=2000000, transcendentals=0),
    )(table, flags, duals, prior, brightness)


def data_kernel(block, pairs, dumps, slots, penalty, chan_count, first_call, joined, *refs):
    table, flags, observed, coh_ref, keep, *refs = refs
    if first_call:
        if joined:
            rows_all, *refs = refs
        else:
            rows_mine, rows_other, *refs = refs
        start, counts_mine, out_ref, field_ref, delay_ref, counts_ref, lead, *refs = refs
    else:
        lead, field_ref, delay_ref, out_ref, *refs = refs
    if first_call:
        order, xp, yp, hl, ha = refs
    else:
        held, sems, order, xp, yp, hl, ha = refs
    stations = field_ref.shape[1]
    pair_count = len(pairs)
    at_own = own_lanes(block)

    live_count = jnp.int32(0)
    for slot in range(slots):
        order[live_count] = jnp.int32(slot)
        live_count = live_count + jnp.where(table[slot] < pair_count, 1, 0)
    items = live_count * dumps

    def copy_of(item):
        slot, t = order[item // dumps], item % dumps
        return pltpu.make_async_copy(observed.at[slot, t], held.at[item], sems.at[item])

    if first_call:
        if joined:
            rows_other = rows_all
            field_ref[...] = rows_all[:64, 0, :]
            delay_ref[: 8 * dumps, :] = rows_all[64 : 64 + 8 * dumps, 0, :]
        else:
            at_other = pl.ds(pl.multiple_of((1 - lax.axis_index("stn")) * block, CHUNK), block)
            for at, rows in ((at_own, rows_mine), (at_other, rows_other)):
                field_ref[:, at] = rows[:64, 0, :]
                delay_ref[: 8 * dumps, at] = rows[64 : 64 + 8 * dumps, 0, :]
    if first_call:
        cosine, sine = trig(delay_ref[: 8 * dumps, :], frequency_of(chan_count))
        delay_ref[: 8 * dumps, :] = cosine
        delay_ref[8 * dumps :, :] = sine
    bright = coherency_rows(coh_ref[...], stations)
    for t in range(dumps):
        cosine, sine = turned(delay_ref, t)
        rot = rotate(field_ref[...], cosine, sine)
        for i, rows in enumerate(left_rows(rot, bright)):
            xp[t, i] = pack(rows)
        for rj, rows in enumerate(right_rows(rot)):
            yp[t, rj] = pack(rows)
    if not first_call:
        for item in range(1, min(1 + AHEAD, slots * dumps)):

            @pl.when(item < items)
            def _():
                copy_of(jnp.int32(item)).start()

    hl[...] = jnp.zeros_like(hl)
    ha[...] = jnp.zeros_like(ha)

    lane = lax.broadcasted_iota(jnp.int32, (1, block), 1)

    def visit(item, tiles):
        slot, t = order[item // dumps], item % dumps
        first, second = pair_blocks(pairs, table[slot])
        kept = keep[jnp.where(first < second, 1, 0)]
        live = (lane >= flags[slot]).astype(F32)
        live16 = live.astype(BF16)
        at_p = pl.ds(pl.multiple_of(first * block, CHUNK), block)
        at_q = pl.ds(pl.multiple_of(second * block, CHUNK), block)
        acc_left = [None, None]
        acc_right = [None] * 4
        xs = [xp[t, i, :, at_p] * live16 for i in range(2)]
        ys = [yp[t, rj, :, at_q] for rj in range(4)]
        for r in range(2):
            for i in range(2):
                for j in range(2):
                    tile = tiles[4 * r + 2 * i + j] * kept
                    rj = 2 * r + j
                    left = dot(ys[rj], tile, NT)
                    right = dot(xs[i], tile, NN)
                    acc_left[i] = left if acc_left[i] is None else acc_left[i] + left
                    acc_right[rj] = right if acc_right[rj] is None else acc_right[rj] + right
        for i in range(2):
            hl[t, i, :, at_p] += (acc_left[i][:32] + acc_left[i][32:]) * live
        for rj in range(4):
            ha[t, rj, :, at_q] += acc_right[rj][:32] + acc_right[rj][32:]

    def visit_held(item, unused):
        copy_of(item).wait()

        @pl.when(item + AHEAD < items)
        def _():
            copy_of(item + AHEAD).start()

        visit(item, held.at[item])
        return unused

    def visit_there(item, unused):
        visit(item, observed.at[order[item // dumps], item % dumps])
        return unused

    if first_call:
        lax.fori_loop(0, items, visit_there, jnp.int32(0))

        @pl.when(items > 0)
        def _():
            lead[...] = observed[order[0], 0]
    else:

        @pl.when(items > 0)
        def _():
            visit(jnp.int32(0), lead)

        lax.fori_loop(1, items, visit_held, jnp.int32(0))

    total = None
    for t in range(dumps):
        cosine, sine = turned(delay_ref, t)
        piece = field_gradient(
            [hl[t, i] for i in range(2)], [ha[t, rj] for rj in range(4)], bright, cosine, sine
        )
        total = piece if total is None else total + piece
    out_ref[...] = -total
    prior = penalty * field_ref[:, at_own]
    if first_call:
        prior = prior + start[...]
        counts = counts_mine[...]
        ids_other, flags_other = rows_other[64 + 8 * dumps], rows_other[65 + 8 * dumps]
        pair_lane = lax.broadcasted_iota(jnp.int32, (8, 128), 1)
        for k in range(pair_count):
            theirs = jnp.where(ids_other == float(k), flags_other, 0.0)
            total_flags = jnp.sum(theirs, axis=1, keepdims=True)
            counts = counts + jnp.where(pair_lane == k, total_flags, 0.0)
        counts_ref[...] = counts
    out_ref[:, at_own] += prior


def data_part(geometry, table, flags, observed, coh, masks, fields):
    block, pairs, dumps, penalty, chan_count, stations = geometry
    slots = observed.shape[0]
    first_call = len(fields[0].shape) == 3 and fields[0].dtype == F32
    joined = len(fields) == 3
    body = functools.partial(
        data_kernel, block, pairs, dumps, slots, penalty, chan_count, first_call, joined
    )
    shapes = [shape(64, stations)]
    if first_call:
        shapes += [shape(64, stations), shape(16 * dumps, stations), shape(8, 128)]
        shapes.append(shape(*observed.shape[2:], dtype=BF16))
        place, copies = vmem_specs(1), []
    else:
        place = [pl.BlockSpec(memory_space=pl.ANY)]
        copies = [
            pltpu.VMEM((slots * dumps,) + observed.shape[2:], BF16),
            pltpu.SemaphoreType.DMA((slots * dumps,)),
        ]
    return pl.pallas_call(
        body,
        name="data_part",
        out_shape=tuple(shapes),
        in_specs=smem_specs(2) + place + vmem_specs(2 + len(fields)),
        out_specs=tuple(vmem_specs(len(shapes))),
        scratch_shapes=copies
        + [
            pltpu.SMEM((slots,), jnp.int32),
            pltpu.VMEM((dumps, 2, 64, stations), BF16),
            pltpu.VMEM((dumps, 4, 64, stations), BF16),
            pltpu.VMEM((dumps, 2, 32, stations), F32),
            pltpu.VMEM((dumps, 4, 32, stations), F32),
        ],
        compiler_params=params() if first_call else params(COPY_BYTES),
        cost_estimate=pl.CostEstimate(
            flops=6000000000, bytes_accessed=8000000, transcendentals=0
        ),
    )(table, flags, observed, coh, masks, *fields)


def fold_gram(high_low, other, rows):
    wide = dot(high_low, other[:rows], NT)
    return wide[:rows] + wide[rows:] + dot(high_low[:rows], other[rows:], NT)


def apply_gram(gram, packed, rows):
    size = gram.shape[0]
    both = pack(gram)
    factors = jnp.concatenate([both[:size], both[size:], both[:size]], axis=1)
    return dot(factors, jnp.concatenate([packed[:rows], packed], axis=0), NN)


def lanes(parts, start, size):
    return jnp.concatenate([part[:, start : start + size] for part in parts], axis=1)


def twice(mask):
    return jnp.concatenate([mask, mask], axis=1)


class Chunks:
    def __init__(self, block, stations, pairs, counts):
        self.block = block
        self.size = min(CHUNK, block)
        self.per_block = block // self.size
        self.count = stations // self.size
        self.blocks = stations // block
        lane = lax.broadcasted_iota(jnp.int32, (1, block), 1).astype(F32)
        self.masks = {
            pair: (lane >= counts[:, k : k + 1]).astype(F32) for k, pair in enumerate(pairs)
        }
        row = lax.broadcasted_iota(jnp.int32, (self.size, self.size), 0)
        col = lax.broadcasted_iota(jnp.int32, (self.size, self.size), 1)
        self.upper = row < col

    def kept(self, values):
        n = self.size
        return jnp.concatenate(
            [
                jnp.concatenate(
                    [
                        jnp.where(self.upper, values[i : i + n, j : j + n], 0.0)
                        for j in range(0, 4 * n, n)
                    ],
                    axis=1,
                )
                for i in range(0, 2 * n, n)
            ],
            axis=0,
        )

    def mask(self, pair, chunk):
        start = (chunk % self.per_block) * self.size
        return twice(self.masks[pair][:, start : start + self.size])

    def own_pair(self, chunk):
        return (chunk // self.per_block, chunk // self.per_block)

    def rect_terms(self, chunk):
        own = chunk // self.per_block
        terms = []
        inside = list(range(chunk + 1, (own + 1) * self.per_block))
        if inside:
            terms.append(((own, own), inside))
        for q in range(own + 1, self.blocks):
            terms.append(((own, q), list(range(q * self.per_block, (q + 1) * self.per_block))))
        return terms


def sum_of(parts):
    total = parts[0]
    for part in parts[1:]:
        total = total + part
    return total


def halves(rows, axis, odd):
    size = rows.shape[axis] // 2
    low = lax.slice_in_dim(rows, 0, size, axis=axis)
    high = lax.slice_in_dim(rows, size, 2 * size, axis=axis)
    return jnp.where(odd, high, low), jnp.where(odd, low, high)


def store_eighths(fields, sums, outs):
    place = lax.axis_index("chan")
    odd_lanes, odd_low, odd_high = place % 2 == 1, (place // 2) % 2 == 1, (place // 4) % 2 == 1
    for n, field in enumerate(fields):
        for out, part in zip(outs, halves(field, 1, odd_lanes)):
            for high, half in enumerate(halves(part, 0, odd_high)):
                for low, rows in enumerate(halves(half, 0, odd_low)):
                    at = 32 * (2 * high + low) + 16 * n
                    out[at : at + 16, :] = rows
    for out in outs:
        out[128:, :] = sums


def step_length(grad_sq, curvature, penalty):
    return grad_sq / (curvature + penalty * grad_sq + EPSILON)


def gradient_kernel(block, pairs, dumps, penalty, chan_count, update, *refs):
    counts_ref, delay_ref, coh_ref, current_ref, *refs = refs
    if update:
        sums_ref, direction_ref, *refs = refs
    gradient_out, *refs = refs
    if update:
        current_out, alpha_out, *refs = refs
    xp, yp, hl, ha = refs
    stations = current_ref.shape[1]
    chunks = Chunks(block, stations, pairs, counts_ref[0:1, :])
    size = chunks.size

    current = current_ref[...]
    if update:
        sums = jnp.sum(sums_ref[...], axis=0, keepdims=True)
        alpha = step_length(sums[:, 0:1], sums[:, 1:2], penalty)
        alpha_out[...] = jnp.broadcast_to(alpha, (8, 128))
        current = current - alpha * direction_ref[...]
        current_out[...] = current
    bright = coherency_rows(coh_ref[...], stations)
    gradient = None
    for t in range(dumps):
        cosine, sine = turned(delay_ref, t)
        rot = rotate(current, cosine, sine)
        xs = [pack(v) for v in left_rows(rot, bright)]
        ys = [pack(v) for v in right_rows(rot)]
        for i in range(2):
            xp[t, i] = xs[i]
        for rj in range(4):
            yp[t, rj] = ys[rj]
        gram_y = [
            fold_gram(lanes(ys, c * size, size), lanes(ys, c * size, size), 32)
            for c in range(chunks.count)
        ]
        sums_x = [None] * chunks.count
        for c in range(chunks.count):
            xc = lanes(xs, c * size, size)
            yc = lanes(ys, c * size, size)
            xw = xc * chunks.mask(chunks.own_pair(c), c).astype(BF16)
            yn = jnp.concatenate([yc[:32], yc[:32], yc[32:], yc[32:]], axis=0)
            model = dot(jnp.concatenate([xw, xw], axis=0), yn, TN)
            model = chunks.kept(model)
            high, low = split(model)
            left = dot(yc, high, NT) + dot(yc, low, NT)
            right = dot(
                jnp.concatenate([xw, xw], axis=1), jnp.concatenate([high, low], axis=0), NN
            )
            left = left[:32] + left[32:]
            right = right[:32] + right[32:]
            for pair, others in chunks.rect_terms(c):
                mask = chunks.mask(pair, c)
                left = left + apply_gram(sum_of([gram_y[o] for o in others]), xc, 32) * mask
                gram_x = fold_gram(xc * mask.astype(BF16), xc, 32)
                for o in others:
                    sums_x[o] = gram_x if sums_x[o] is None else sums_x[o] + gram_x
            if sums_x[c] is not None:
                right = right + apply_gram(sums_x[c], yc, 32)
            for i in range(2):
                hl[i, :, c * size : (c + 1) * size] = left[:, i * size : (i + 1) * size]
            for rj in range(4):
                ha[rj, :, c * size : (c + 1) * size] = right[:, rj * size : (rj + 1) * size]
        piece = field_gradient(
            [hl[i] for i in range(2)], [ha[rj] for rj in range(4)], bright, cosine, sine
        )
        gradient = piece if gradient is None else gradient + piece
    gradient_out[...] = gradient


def gradient_part(geometry, counts, delays, coh, current, step):
    block, pairs, dumps, penalty, chan_count, stations = geometry
    update = step is not None
    field = shape(64, stations)
    outs = [field]
    inputs = [counts, delays, coh, current]
    if update:
        inputs += step
        outs += [field, shape(8, 128)]
    outs += [shape(dumps, rows, 64, stations, dtype=BF16) for rows in (2, 4)]
    return pl.pallas_call(
        functools.partial(gradient_kernel, block, pairs, dumps, penalty, chan_count, update),
        name="gradient_part",
        out_shape=tuple(outs),
        in_specs=vmem_specs(len(inputs)),
        out_specs=tuple(vmem_specs(len(outs))),
        scratch_shapes=[pltpu.VMEM((2, 32, stations), F32), pltpu.VMEM((4, 32, stations), F32)],
        compiler_params=params(),
        cost_estimate=pl.CostEstimate(
            flops=4000000000, bytes_accessed=2000000, transcendentals=0
        ),
    )(*inputs)


def curvature_kernel(block, pairs, dumps, penalty, chan_count, update, last, *refs):
    counts_ref, delay_ref, coh_ref, xp, yp, gradient_ref, mine_ref, theirs_ref, *refs = refs
    if update:
        alpha_ref, linear_ref, *refs = refs
    if last:
        duals_ref, current_ref, *refs = refs
    direction_out, *refs = refs
    if not last:
        linear_out, sums_out = refs
    stations = mine_ref.shape[1]
    chunks = Chunks(block, stations, pairs, counts_ref[0:1, :])
    size = chunks.size

    linear = mine_ref[...] + theirs_ref[...]
    if update:
        linear = linear_ref[...] - alpha_ref[0:1, 0:1] * linear
    direction = linear + gradient_ref[...]
    direction_out[...] = direction
    if not last:
        linear_out[...] = linear

    bright = coherency_rows(coh_ref[...], stations)
    squares = jnp.zeros((8, 4 * size), F32)
    grams = jnp.zeros((64, 64), F32)
    if last:
        visited, repeats, copies = range(dumps), 1, 1
    else:
        stn_count = stations // block
        shared = stn_count % dumps == 0
        visited = [lax.axis_index("stn") % dumps] if shared else range(dumps)
        repeats, copies = (stn_count // dumps if shared else stn_count), stn_count
    for t in visited:
        cosine, sine = turned(delay_ref, t)
        step = rotate(direction, cosine, sine)
        xs = [xp[t, i] for i in range(2)]
        ys = [yp[t, rj] for rj in range(4)]
        dxs = [pack(v) for v in left_rows(step, bright)]
        dys = [pack(v) for v in right_rows(step)]

        def stacked(first, second, c):
            one = lanes(first, c * size, size)
            two = lanes(second, c * size, size)
            return jnp.concatenate([one[:32], two[:32], one[32:], two[32:]], axis=0)

        gram_y = [None] * chunks.count
        for c in range(chunks.count):
            xc = stacked(dxs, xs, c)
            yc = stacked(ys, dys, c)
            xw = xc * chunks.mask(chunks.own_pair(c), c).astype(BF16)
            tangent = dot(
                jnp.concatenate([xw, xw], axis=0),
                jnp.concatenate([yc[:64], yc[:64], yc[64:], yc[64:]], axis=0),
                TN,
            )
            tangent = chunks.kept(tangent)
            square = tangent * tangent
            squares = squares + jnp.sum(square.reshape(2 * size // 8, 8, 4 * size), axis=0)
            if c > 0:
                gram_y[c] = fold_gram(yc, yc, 64)
        for c in range(chunks.count):
            for pair, others in chunks.rect_terms(c):
                xc = stacked(dxs, xs, c)
                gram_x = fold_gram(xc * chunks.mask(pair, c).astype(BF16), xc, 64)
                grams = grams + sum_of([gram_y[o] for o in others]) * gram_x
    curvature = jnp.sum(squares, keepdims=True) + jnp.sum(grams, keepdims=True)
    grad_sq = jnp.sum(direction * direction, keepdims=True)
    grad_sq = grad_sq * (1.0 / copies)
    curvature = curvature * (1.0 / repeats)
    rows = 8 if last else chan_count * copies
    lane = lax.broadcasted_iota(jnp.int32, (rows, block // 2 if last else 128), 1)
    sums = jnp.where(lane == 0, grad_sq, jnp.where(lane == 1, curvature, 0.0))
    if last:
        base = current_ref[:, own_lanes(block)] + duals_ref[...]
        store_eighths((base, direction_out[:, own_lanes(block)]), sums, refs)
    else:
        sums_out[...] = sums


def curvature_part(geometry, counts, delays, coh, factors, gradient, shares, before, last):
    block, pairs, dumps, penalty, chan_count, stations = geometry
    update = before is not None
    field = shape(64, stations)
    if last is not None:
        outs = [field] + [shape(136, block // 2)] * 2
    else:
        outs = [field, field, shape(chan_count * (stations // block), 128)]
    inputs = [counts, delays, coh, *factors, gradient, *shares]
    if update:
        inputs += before
    if last is not None:
        inputs += last
    return pl.pallas_call(
        functools.partial(
            curvature_kernel, block, pairs, dumps, penalty, chan_count, update, last is not None
        ),
        name="curvature_part",
        out_shape=tuple(outs),
        in_specs=vmem_specs(len(inputs)),
        out_specs=tuple(vmem_specs(len(outs))),
        compiler_params=params(),
        cost_estimate=pl.CostEstimate(
            flops=2000000000, bytes_accessed=2000000, transcendentals=0
        ),
    )(*inputs)


def regroup_kernel(mine, theirs, *outs):
    for o, out in enumerate(outs):
        out[:32, :] = mine[32 * o : 32 * o + 32, :]
        out[32:64, :] = theirs[32 * o : 32 * o + 32, :]
        out[64:, :] = mine[128:, :] + theirs[128:, :]


def regroup(mine, theirs):
    return pl.pallas_call(
        regroup_kernel,
        name="regroup",
        out_shape=(shape(72, mine.shape[1]),) * 4,
        in_specs=vmem_specs(2),
        out_specs=tuple(vmem_specs(4)),
        compiler_params=params(),
    )(mine, theirs)


def sum_in_pairs(terms):
    return (terms[0] + terms[1]) + (terms[2] + terms[3])


def weigh_kernel(chan_count, *refs):
    *parts, out = refs
    scales = [solve_of(chan_count, offset) for offset in range(8)]
    for n in range(2):
        for k in range(4):
            terms = []
            for o, part in enumerate(parts):
                one = part[16 * n : 16 * n + 16, :]
                two = part[32 + 16 * n : 48 + 16 * n, :]
                terms.append(scales[2 * o][k] * one + scales[2 * o + 1][k] * two)
            at = 64 * n + 16 * k
            out[at : at + 16, :] = sum_in_pairs(terms)
    out[128:, :] = sum_in_pairs([part[64:, :] for part in parts])


def weigh(geometry, parts):
    chan_count = geometry[4]
    return pl.pallas_call(
        functools.partial(weigh_kernel, chan_count),
        name="weigh",
        out_shape=shape(136, parts[0].shape[1]),
        in_specs=vmem_specs(4),
        out_specs=vmem_specs(1)[0],
        compiler_params=params(),
    )(*parts)


def combine_kernel(penalty, one, two, coeffs_out, alpha_out):
    total = one[...] + two[...]
    alpha = step_length(total[128:129, 0:1], total[128:129, 1:2], penalty)
    coeffs_out[...] = total[:64] - alpha * total[64:128]
    alpha_out[...] = jnp.broadcast_to(alpha, (8, 128))


def combine(geometry, one, two):
    penalty = geometry[3]
    return pl.pallas_call(
        functools.partial(combine_kernel, penalty),
        name="combine",
        out_shape=(shape(64, one.shape[1]), shape(8, 128)),
        in_specs=vmem_specs(2),
        out_specs=tuple(vmem_specs(2)),
        compiler_params=params(),
    )(one, two)


def last_step_kernel(block, alpha, current, direction, duals, gains_out, shifted_out):
    at_own = own_lanes(block)
    gains_new = current[:, at_own] - alpha[0:1, 0:1] * direction[:, at_own]
    gains_out[:, 0, :] = gains_new
    shifted_out[:, 0, :] = gains_new + duals[...]


def last_step(geometry, *inputs):
    block = geometry[0]
    return pl.pallas_call(
        functools.partial(last_step_kernel, block),
        name="last_step",
        out_shape=(shape(64, 1, block), shape(64, 1, block)),
        in_specs=vmem_specs(len(inputs)),
        out_specs=tuple(vmem_specs(2)),
        compiler_params=params(),
    )(*inputs)


def consensus_kernel(chan_count, mine, theirs, shifted, coeffs_out, duals_out):
    place = lax.axis_index("chan")
    odd = place % 2 == 1
    for o in range(4):
        rows = pl.ds((((place // 2) % 4) ^ o) * 16, 16)
        fitted = None
        for k, scale in enumerate(basis_of(chan_count)):
            at = slice(64 * o + 16 * k, 64 * o + 16 * k + 16)
            one, two = mine[at, :], theirs[at, :]
            coeffs = jnp.concatenate([jnp.where(odd, two, one), jnp.where(odd, one, two)], axis=1)
            coeffs_out[rows, k, :] = coeffs
            fitted = scale * coeffs if fitted is None else fitted + scale * coeffs
        duals_out[rows, 0, :] = shifted[rows, 0, :] - fitted


def consensus(geometry, *inputs):
    block, pairs, dumps, penalty, chan_count, stations = geometry
    return pl.pallas_call(
        functools.partial(consensus_kernel, chan_count),
        name="consensus",
        out_shape=(shape(64, 4, block), shape(64, 1, block)),
        in_specs=vmem_specs(len(inputs)),
        out_specs=tuple(vmem_specs(2)),
        compiler_params=params(),
    )(*inputs)


def swap(value, count, offset):
    return lax.ppermute(value, "chan", [(i, i ^ offset) for i in range(count)])


def other_stations(value):
    return lax.ppermute(value, "stn", [(0, 1), (1, 0)])


def both_stations(value, count):
    if count == 2:
        return value, other_stations(value)
    return jnp.zeros_like(value), lax.psum(value, "stn")


def shards(observed, pair_table, flag_rows, gains, duals, prior_coeffs, delays, brightness):
    stn_count = lax.axis_size("stn")
    chan_count = lax.axis_size("chan")
    entries, dirs, chan_local, block = gains.shape
    slots, dumps = observed.shape[0], observed.shape[2]
    stations = block * stn_count
    pairs = pair_lists(stn_count)
    penalty = stations * dumps / 16.0
    geometry = (block, pairs, dumps, penalty, chan_count, stations)

    observed = observed.reshape((slots,) + observed.shape[2:])
    duals_raw = duals.reshape(entries * dirs, 1, block)
    prior = prior_coeffs.reshape(entries * dirs, 4, block)
    masks = baseline_masks(block)
    rows = field_rows(
        masks,
        gains.reshape(entries * dirs, 1, block),
        delays.reshape(dumps * dirs, block),
        pair_table.reshape(1, slots),
        flag_rows.reshape(1, slots),
    )
    if stn_count == 2:
        fields = (rows, other_stations(rows))
    else:
        fields = (lax.all_gather(rows, "stn", axis=2, tiled=True),)
    duals_own, start, coh, counts = prepare(
        geometry, pair_table, flag_rows, duals_raw, prior, brightness
    )
    if stn_count != 2:
        counts = jnp.zeros_like(counts)
    data = functools.partial(data_part, geometry, pair_table, flag_rows, observed, coh, masks)
    share, current, delay_all, counts, lead = data(fields + (start, counts))
    shares = both_stations(share, stn_count)

    step = before = None
    for iteration in range(ITERS):
        last = iteration + 1 == ITERS
        gradient, *rest = gradient_part(geometry, counts, delay_all, coh, current, step)
        if step is not None:
            current, alpha, *rest = rest
            before = (alpha, linear)
        direction, *rest = curvature_part(
            geometry,
            counts,
            delay_all,
            coh,
            rest,
            gradient,
            shares,
            before,
            (duals_own, current) if last else None,
        )
        if not last:
            linear, sums = rest
            sums = lax.all_to_all(sums, ("chan", "stn"), 0, 0, tiled=True)
            (share,) = data((lead, direction, delay_all))
            shares = both_stations(share, stn_count)
            step = (sums, direction)

    keep, send = rest
    own, *others = regroup(keep, swap(send, chan_count, 1))
    parts = [own] + [swap(part, chan_count, 2 + 2 * o) for o, part in enumerate(others)]
    value, bit = weigh(geometry, parts), 8
    other = swap(value, chan_count, bit)
    while 2 * bit < chan_count:
        value, bit = value + other, 2 * bit
        other = swap(value, chan_count, bit)
    rows, alpha = combine(geometry, value, other)
    gains_new, shifted = last_step(geometry, alpha, current, direction, duals_own)
    mine = jnp.concatenate([rows] + [swap(rows, chan_count, o) for o in (2, 4, 6)])
    coeffs, duals_new = consensus(geometry, mine, swap(mine, chan_count, 1), shifted)
    return (
        gains_new.reshape(gains.shape),
        coeffs.reshape(entries, dirs, 4, block),
        duals_new.reshape(gains.shape),
    )


def solution(mesh):
    return jax.shard_map(
        shards,
        mesh=mesh,
        in_specs=(
            P("stn", ("band", "chan"), None, None, None, None),
            P("stn"),
            P("stn"),
            P(None, None, ("band", "chan"), "stn"),
            P(None, None, ("band", "chan"), "stn"),
            P("band", None, None, "stn"),
            P(None, None, "stn"),
            P("band", None),
        ),
        out_specs=(
            P(None, None, ("band", "chan"), "stn"),
            P("band", None, None, "stn"),
            P(None, None, ("band", "chan"), "stn"),
        ),
        check_vma=False,
    )
```
